128 devices in a mesh: img: 32 (over x, y, core), tile: 4 (over z).
Axes of the slice: x: 4, y: 4, z: 4, core: 2. Of those that a mesh axis runs over, the one named last changes fastest.
Arguments:
- features: bfloat16 [512, 64, 16, 768], P('img', None, 'tile'), may hold values from -6 to 6
- partner_ids: int32 [512], replicated, may hold values from 0 to 511, as said below
- depth_planes: float32 [64], replicated, may hold values from 0.5 to 4
- cam_height: float32 [512], P('img'), may hold values from 2 to 4
- ray_down: float32 [512, 16, 512], P('img', 'tile'), may hold values from 0.3 to 0.9
- depth_index: int32 [512, 16, 512], P('img', 'tile'), may hold values from 0 to 63
- cell_index: int32 [512, 16, 512], P('img', 'tile'), may hold values from 0 to 127
- block_list: int32 [32, 4, 4, 128], P('img', 'tile'), may hold values from 0 to 255, as said below
- block_slot: int32 [32, 4, 4, 128], P('img', 'tile'), may hold values from 0 to 511
- block_count: int32 [32, 4, 4], P('img', 'tile'), may hold values from 0 to 128, as said below
Outputs:
- mean_range_per_sample: float32 [512, 16, 512], P('img', 'tile')
- terrain_height_grid: float32 [2048, 128], P(('img', 'tile'))
The draws below stay inside these ranges and needn't reach their ends.
Inputs may be any that keep to these rules, and one draw needn't show every extreme that they name: `partner_ids`: image g lies on index g // 16 of img; the partners of the 16 images of one index of img include at most 1 images held by any one index of img, and exactly 1 from some. `block_list`: for each device and owner, entries below block_count are ids of that device's blocks; each block of a device is listed exactly once over its owners; entries at or past the count are 0. `block_count`: a device's counts sum to 256; every device has an owner with exactly 128.
All inputs are finite; a program needn't handle non-finite values.
Results may differ from the reference program's by a relative error of at most 0.0003.
Values may be sent and summed in bfloat16 or wider, within the bound.
No kernel may reach another device: no remote copies, remote signals or barrier semaphores. Data moves between devices by JAX's collectives and lax.ppermute only.
A program may use at most 192 MiB of HBM per device.

```python
import math
import jax
import jax.numpy as jnp
from jax import lax

C = 64
W = 512
IMG_DEV = 16
ROWS_DEV = 4
NDEPTH = 64
CELLS = 128
PATCH_DEV = 16
GROUPS = 32
OWNERS = 4
IMAGES = 512
ROWS = 16
WIDE = 768
NBLK = 4
BLK_DEV = 256
CAPB = 128
TERRAIN_TILES = 2048


def draw_partner_ids(key, part):

    def per_group(group):
        group_key = jax.random.fold_in(key, group)
        camera_views = jax.random.permutation(jax.random.fold_in(group_key, 1), GROUPS)
        source_of = camera_views[jnp.arange(IMG_DEV) % GROUPS]
        local_idx = jax.random.randint(jax.random.fold_in(group_key, 2), (IMG_DEV,), 0, IMG_DEV)
        return (source_of * IMG_DEV + local_idx).astype(jnp.int32)
    return jax.vmap(per_group)(jnp.arange(GROUPS)).reshape(IMAGES)


def block_tables(key):
    base_key = jax.random.fold_in(key, 77)

    def per_device(device):
        dev_key = jax.random.fold_in(base_key, device)
        busiest = jax.random.randint(jax.random.fold_in(dev_key, 1), (), 0, OWNERS)
        others = (busiest + 1 + jax.random.randint(jax.random.fold_in(dev_key, 2), (BLK_DEV,), 0, OWNERS - 1)) % OWNERS
        owners_of = jnp.where(jnp.arange(BLK_DEV) < CAPB, busiest, others)
        owners_of = jax.random.permutation(jax.random.fold_in(dev_key, 3), owners_of).astype(jnp.int32)
        sorted_ids = jnp.argsort(owners_of, stable=True).astype(jnp.int32)
        counts = jnp.sum((owners_of[None, :] == jnp.arange(OWNERS)[:, None]).astype(jnp.int32), axis=1)
        starts = jnp.cumsum(counts) - counts
        position = starts[:, None] + jnp.arange(CAPB)[None, :]
        usable = jnp.arange(CAPB)[None, :] < counts[:, None]
        lists = jnp.where(usable, sorted_ids[jnp.minimum(position, BLK_DEV - 1)], 0)
        return (lists.astype(jnp.int32), counts.astype(jnp.int32))
    lists, counts = jax.vmap(per_device)(jnp.arange(GROUPS * OWNERS))
    return (lists.reshape(GROUPS, OWNERS, OWNERS, CAPB), counts.reshape(GROUPS, OWNERS, OWNERS))


def draw_block_list(key, part):
    return block_tables(key)[0]


def draw_block_count(key, part):
    return block_tables(key)[1]


def place_ends(result, own_key, low, largest):
    longest = result.shape.index(max(result.shape))
    spots = []
    for shift in (0, 1):
        where = [jax.random.randint(jax.random.fold_in(own_key, axis), (), 0, length) for axis, length in enumerate(result.shape)]
        where[longest] = (where[longest] + shift) % result.shape[longest]
        spots.append(tuple(where))
    return result.at[spots[0]].set(low).at[spots[1]].set(largest)


def levels(rng, extent, pieces, smallest, high):
    def one(dim, parts):
        draws = jax.random.uniform(jax.random.fold_in(jax.random.fold_in(rng, 6), dim), (parts,), jnp.float32, smallest / len(pieces), high / len(pieces))
        return jnp.repeat(jnp.exp(draws), extent[dim] // parts).reshape((-1,) + (1,) * (len(extent) - dim - 1))

    factor_of = one(*pieces[0])
    for cut in pieces[1:]:
        factor_of = factor_of * one(*cut)
    return factor_of


def normal_values(stream_key, extent, width, reach, cuts=(), kind=jnp.bfloat16):
    loudness = levels(stream_key, extent, cuts, -0.22, 0.18) if cuts else 1.0
    values = jax.random.normal(stream_key, extent, jnp.float32) * width * loudness
    return jnp.minimum(jnp.maximum(values, -reach), reach).astype(kind)


def setup_inputs(seed: int = 0) -> dict:
    splits = jax.random.split(jax.random.key(seed), 11)
    return {
        "features": normal_values(splits[0], (IMAGES, C, ROWS, WIDE), 1.0, 6.0, ((0, 32), (2, 4))),
        "partner_ids": draw_partner_ids(jax.random.fold_in(splits[10], 71), 0),
        "depth_planes": jnp.clip(jnp.exp(jax.random.uniform(splits[2], (NDEPTH,), jnp.float32, math.log(0.5), math.log(4.0))), 0.5, 4.0),
        "cam_height": jnp.clip(2.0 + 2.0 * jax.random.uniform(splits[3], (IMAGES,), jnp.float32) ** levels(splits[3], (IMAGES,), ((0, 32),), -0.2, 0.2), 2.0, 4.0),
        "ray_down": jnp.clip(0.3 + 0.59999996 * jax.random.uniform(splits[4], (IMAGES, ROWS, W), jnp.float32) ** levels(splits[4], (IMAGES, ROWS, W), ((0, 32), (1, 4)), -0.2, 0.2), 0.3, 0.9),
        "depth_index": place_ends(jax.random.randint(splits[5], (IMAGES, ROWS, W), 0, NDEPTH), jax.random.fold_in(splits[5], 1), 0, NDEPTH - 1).astype(jnp.int32),
        "cell_index": place_ends(jax.random.randint(splits[6], (IMAGES, ROWS, W), 0, CELLS), jax.random.fold_in(splits[6], 1), 0, CELLS - 1).astype(jnp.int32),
        "block_list": draw_block_list(jax.random.fold_in(splits[10], 71), 0),
        "block_slot": place_ends(jax.random.randint(splits[8], (GROUPS, OWNERS, OWNERS, CAPB), 0, GROUPS * PATCH_DEV), jax.random.fold_in(splits[8], 1), 0, (GROUPS * PATCH_DEV) - 1).astype(jnp.int32),
        "block_count": draw_block_count(jax.random.fold_in(splits[10], 71), 0),
    }


def window(values, out_width):
    across = values[..., :, 0:out_width] + values[..., :, 1:out_width + 1] + values[..., :, 2:out_width + 2]
    return across[..., 0:-2, :] + across[..., 1:-1, :] + across[..., 2:, :]

def diagonals(stats, out_width):
    groups, count_of_rows, length = stats.shape
    span = out_width + NDEPTH
    trimmed = stats[:, :, :span]
    spread = jnp.broadcast_to(trimmed[:, :, None, :], (groups, count_of_rows, NDEPTH, span))
    flat = jnp.pad(spread.reshape(groups, count_of_rows, NDEPTH * span), ((0, 0), (0, 0), (0, NDEPTH)))
    skewed = flat.reshape(groups, count_of_rows, NDEPTH, span + 1)[:, :, :, :out_width]
    return jnp.transpose(skewed, (0, 2, 1, 3))

def sweep(own_ext, other_ext, planes, selected_image):
    channels, count_of_rows, full_width = own_ext.shape
    out_width = full_width - 256
    col_blocks = full_width // 128 - 1
    own_cols = own_ext[:, :, :col_blocks * 128].reshape(channels, count_of_rows, col_blocks, 128).astype(jnp.float32)
    other_split = other_ext.reshape(channels, count_of_rows, col_blocks + 1, 128)
    other_cols = jnp.concatenate([other_split[:, :, :-1], other_split[:, :, 1:]], axis=3).astype(jnp.float32)
    products = jnp.einsum('crkx,crky->rkxy', own_cols, other_cols, precision=lax.Precision.HIGHEST)
    flattened = jnp.pad(products.reshape(count_of_rows, col_blocks, 128 * 256), ((0, 0), (0, 0), (0, 128)))
    band_limited = flattened.reshape(count_of_rows, col_blocks, 128, 257)[:, :, :, :NDEPTH]
    band_limited = jnp.transpose(band_limited, (3, 0, 1, 2)).reshape(NDEPTH, count_of_rows, col_blocks * 128)
    cross_sum = window(band_limited, out_width)
    own_f = own_ext.astype(jnp.float32)
    other_f = other_ext.astype(jnp.float32)
    own_sum = window(lax.optimization_barrier(jnp.sum(own_f, 0)), out_width)
    own_squared_sum = window(lax.optimization_barrier(jnp.sum(own_f * own_f, 0)), out_width)
    other_stats = window(jnp.stack([lax.optimization_barrier(jnp.sum(other_f, 0)), lax.optimization_barrier(jnp.sum(other_f * other_f, 0))]), full_width - 2)
    shifted = diagonals(other_stats, out_width)
    other_sum = shifted[0]
    other_sq = shifted[1]
    entries = 9.0 * channels
    mean_own = own_sum / entries
    var_own = own_squared_sum / entries - mean_own * mean_own
    mean_other = other_sum / entries
    var_other = other_sq / entries - mean_other * mean_other
    correlation = (cross_sum / entries - mean_own * mean_other) / jnp.sqrt((var_own + 1e-05) * (var_other + 1e-05))
    weights_exp = jnp.exp(24.0 * correlation)
    likelihood = weights_exp / lax.optimization_barrier(jnp.sum(weights_exp, 0))
    depth_out = lax.optimization_barrier(jnp.sum(likelihood * planes[:, None, None], 0))
    matched = jnp.arange(NDEPTH, dtype=jnp.int32)[:, None, None] == selected_image[None]
    confidence = lax.optimization_barrier(jnp.sum(jnp.where(matched, likelihood, jnp.float32(0.0)), 0))
    plane_at = lax.optimization_barrier(jnp.sum(jnp.where(matched, planes[:, None, None], jnp.float32(0.0)), 0))
    return (depth_out, confidence, plane_at)

def to_blocks(values):
    shaped = values.reshape(GROUPS, IMG_DEV, OWNERS, ROWS_DEV, NBLK, 128)
    return jnp.transpose(shaped, (0, 2, 1, 3, 4, 5)).reshape(GROUPS * OWNERS * BLK_DEV, 128)

def reference(features, partner_ids, depth_planes, cam_height, ray_down, depth_index, cell_index, block_list, block_slot, block_count):

    def per_image(image):
        own_ext = jnp.pad(jnp.take(features, image, axis=0), ((0, 0), (1, 1), (0, 0)))
        other_ext = jnp.pad(jnp.take(features, jnp.take(partner_ids, image), axis=0), ((0, 0), (1, 1), (0, 0)))
        return sweep(own_ext, other_ext, depth_planes, jnp.take(depth_index, image, axis=0))
    mean_range_per_sample, confidence, plane_at = lax.map(per_image, jnp.arange(IMAGES, dtype=jnp.int32))
    point_elevation = cam_height[:, None, None] - ray_down * plane_at
    every_processor = GROUPS * OWNERS
    weighted = to_blocks(confidence * point_elevation).reshape(-1)
    plain = to_blocks(confidence).reshape(-1)
    cells = to_blocks(cell_index)
    segment = (jnp.arange(every_processor * BLK_DEV, dtype=jnp.int32)[:, None] * CELLS + cells).reshape(-1)
    block_num = jax.ops.segment_sum(weighted, segment, num_segments=every_processor * BLK_DEV * CELLS).reshape(every_processor * BLK_DEV, CELLS)
    block_den = jax.ops.segment_sum(plain, segment, num_segments=every_processor * BLK_DEV * CELLS).reshape(every_processor * BLK_DEV, CELLS)
    row_ids = block_list.reshape(every_processor, OWNERS, CAPB) + (jnp.arange(every_processor, dtype=jnp.int32) * BLK_DEV)[:, None, None]
    usable = jnp.arange(CAPB, dtype=jnp.int32)[None, None, :] < block_count.reshape(every_processor, OWNERS)[:, :, None]
    slot_ids = block_slot.reshape(every_processor, OWNERS, CAPB)
    owner_ids = jnp.arange(OWNERS, dtype=jnp.int32)[None, :, None]
    patch_ids = (slot_ids // PATCH_DEV * OWNERS + owner_ids) * PATCH_DEV + slot_ids % PATCH_DEV
    rows_num = jnp.where(usable[..., None], block_num[row_ids], jnp.float32(0.0)).reshape(-1, CELLS)
    rows_den = jnp.where(usable[..., None], block_den[row_ids], jnp.float32(0.0)).reshape(-1, CELLS)
    terrain_weighted_heights = jnp.zeros((TERRAIN_TILES, CELLS), jnp.float32).at[patch_ids.reshape(-1)].add(rows_num)
    terrain_weight_totals = jnp.zeros((TERRAIN_TILES, CELLS), jnp.float32).at[patch_ids.reshape(-1)].add(rows_den)
    terrain_height_grid = terrain_weighted_heights / (terrain_weight_totals + 1.0)
    return (mean_range_per_sample, terrain_height_grid)
```

```python
import math

import numpy as np
import jax
import jax.numpy as jnp
from jax import lax
from jax.experimental import pallas as pl
from jax.experimental.pallas import tpu as pltpu
from jax.sharding import PartitionSpec as P

NDEPTH = 64
CELLS = 128
PATCH_DEV = 16
STEPS = 4
WIN = 144
LOG2E = math.log2(math.e)
BF = jnp.bfloat16
F32 = jnp.float32
NT = (((1,), (1,)), ((), ()))


def dot(a, b):
    return jnp.dot(a, b, preferred_element_type=F32)


def dot_nt(a, b):
    return lax.dot_general(a, b, NT, preferred_element_type=F32)


def table_patterns():
    pat = np.zeros((128, 12, 128), np.float32)
    for half in range(2):
        lanes = slice(64 * half, 64 * half + 64)
        for y in range(4):
            for q in range(2):
                for s in range(3):
                    pat[half * 32 + s * 8 + q * 4 + y, y * 3 + q, lanes] = 1.0
            pat[half * 32 + 24 + y, y * 3 + 2, lanes] = 1.0
    return jnp.asarray(pat.reshape(128, 12 * 128), BF)


def row_masks():
    y = np.arange(16)[:, None]
    k = np.arange(256)[None, :] % 4
    return jnp.asarray((np.abs(k - y) <= 1) & (y < 4), BF)


def flips():
    m = np.zeros((128, 128), np.float32)
    for i in range(128):
        m[i, i // 64 * 64 + 63 - i % 64] = 1.0
    return jnp.asarray(m, BF)


def reversal():
    m = np.zeros((WIN, 256), np.float32)
    for i in range(WIN):
        m[i, WIN - 1 - i] = 1.0
    return jnp.asarray(m, BF)


def edge_constants():
    sel = np.zeros((128, 256), np.float32)
    for c in range(64):
        sel[c, 4 * c] = 1.0
        sel[64 + c, 4 * c + 3] = 1.0
    stat = np.zeros((16, 256), np.float32)
    for y in range(4):
        stat[y, y::4] = 1.0
        stat[12 + y, y::4] = 1.0
    return jnp.asarray(sel, BF), jnp.asarray(stat, BF)


def split2(a):
    high = a.astype(BF)
    return high, (a - high.astype(F32)).astype(BF)


def boxed_stats(stats, up, down):
    upf = up.astype(F32)
    downf = down.astype(F32)
    sums = [jnp.sum(upf, 0, keepdims=True)] + [stats[y : y + 1] for y in range(4)]
    sums.append(jnp.sum(downf, 0, keepdims=True))
    sqs = [jnp.sum(upf * upf, 0, keepdims=True)] + [stats[4 + y : 5 + y] for y in range(4)]
    sqs.append(jnp.sum(downf * downf, 0, keepdims=True))
    tall = jnp.concatenate(
        [v[y] + v[y + 1] + v[y + 2] for v in (sums, sqs) for y in range(4)], axis=0
    )
    boxed = (tall + pltpu.roll(tall, 255, 1) + pltpu.roll(tall, 254, 1)) * (1.0 / 576.0)
    mean = boxed[0:4]
    return mean, lax.rsqrt(boxed[4:8] - mean * mean + 1e-5)


def pick_kernel(blocks, idx_ref, strip_ref, out_ref):
    for j in range(blocks):
        out_ref[0, j] = strip_ref[0, :, :, 128 * j : 128 * j + 128]


def pick(idx, features, first, blocks):
    count = idx.shape[0]
    images, channels, rows, _ = features.shape

    def kernel(*refs):
        pick_kernel(blocks, *refs)

    out = pl.pallas_call(
        kernel,
        grid_spec=pltpu.PrefetchScalarGridSpec(
            num_scalar_prefetch=1,
            grid=(count,),
            in_specs=[
                pl.BlockSpec(
                    (1, channels, rows, 128 * blocks), lambda s, r: (r[s], 0, 0, first // blocks)
                )
            ],
            out_specs=pl.BlockSpec((1, blocks, channels, rows, 128), lambda s, r: (s, 0, 0, 0, 0)),
        ),
        out_shape=jax.ShapeDtypeStruct((count, blocks, channels, rows, 128), BF),
        cost_estimate=pl.CostEstimate(
            flops=0, bytes_accessed=count * blocks * 131072, transcendentals=0
        ),
        name="pick",
    )(idx, features)
    return out.reshape(count, blocks, channels * rows, 128)


def edge_kernel(slot_ref, block_ref, sel_ref, stat_ref, head_ref, tail_ref, stats_ref):
    for j in range(block_ref.shape[1]):
        block = block_ref[0, j]
        rows = dot(sel_ref[...], block).astype(BF)
        head_ref[0, j] = rows[0:64]
        tail_ref[0, j] = rows[64:128]
        value = block.astype(F32)
        high, low = split2(value * value)
        stats_ref[0, j] = (
            dot(stat_ref[0:8], block) + dot(stat_ref[8:16], high) + dot(stat_ref[8:16], low)
        )


def edges(slot, recv):
    images = slot.shape[0]
    blocks = recv.shape[1]
    sel, stat = edge_constants()
    return pl.pallas_call(
        edge_kernel,
        grid_spec=pltpu.PrefetchScalarGridSpec(
            num_scalar_prefetch=1,
            grid=(images,),
            in_specs=[
                pl.BlockSpec((1, blocks, 256, 128), lambda k, s: (s[k], 0, 0, 0)),
                pl.BlockSpec((128, 256), lambda k, s: (0, 0)),
                pl.BlockSpec((16, 256), lambda k, s: (0, 0)),
            ],
            out_specs=[
                pl.BlockSpec((1, blocks, 64, 128), lambda k, s: (k, 0, 0, 0)),
                pl.BlockSpec((1, blocks, 64, 128), lambda k, s: (k, 0, 0, 0)),
                pl.BlockSpec((1, blocks, 8, 128), lambda k, s: (k, 0, 0, 0)),
            ],
        ),
        out_shape=[
            jax.ShapeDtypeStruct((images, blocks, 64, 128), BF),
            jax.ShapeDtypeStruct((images, blocks, 64, 128), BF),
            jax.ShapeDtypeStruct((images, blocks, 8, 128), F32),
        ],
        cost_estimate=pl.CostEstimate(
            flops=images * blocks * 20_000_000, bytes_accessed=images * blocks * 100_000,
            transcendentals=0,
        ),
        name="edges",
    )(slot, recv, sel, stat)


def prepare_kernel(
    own_ref, up_ref, down_ref, stat_ref, index_ref, rev_ref, flip_ref, own_out, edge_out, table_out
):
    mean_inv = 24.0 * LOG2E
    for n in range(STEPS):
        block = jnp.concatenate([own_ref[0, n], own_ref[0, n + 1]], axis=1)
        up = jnp.concatenate([up_ref[0, n], up_ref[0, n + 1]], axis=1)
        down = jnp.concatenate([down_ref[0, n], down_ref[0, n + 1]], axis=1)
        own_out[0, n] = dot_nt(rev_ref[...], block).astype(BF)
        edge_out[0, n] = dot_nt(rev_ref[...], jnp.concatenate([up, down], axis=0)).astype(BF)
        stats = jnp.concatenate([stat_ref[0, n], stat_ref[0, n + 1]], axis=1)
        mean, inv = boxed_stats(stats, up, down)
        scaled = inv * mean_inv
        both = jnp.concatenate([scaled * (1.0 / 576.0), scaled * mean], axis=0)[:, :128]
        high = both.astype(BF).astype(F32)
        mid = (both - high).astype(BF).astype(F32)
        index = index_ref[0, :, 128 * n : 128 * n + 128].astype(F32)
        rows = jnp.concatenate(
            [high, mid, both - high - mid, index, jnp.zeros((4, 128), F32)], axis=0
        ).astype(BF)
        blank = jnp.zeros((64, 64), F32)
        left = dot_nt(flip_ref[0:64, :], rows)
        right = dot_nt(flip_ref[64:128, :], rows)
        table_out[0, n] = jnp.concatenate([left, right, blank], axis=1).astype(BF)


def prepare(own, up, down, stats, depth_index):
    images, blocks = own.shape[0], own.shape[1]
    return pl.pallas_call(
        prepare_kernel,
        grid=(images,),
        in_specs=[
            pl.BlockSpec((1, blocks, 256, 128), lambda k: (k, 0, 0, 0)),
            pl.BlockSpec((1, blocks, 64, 128), lambda k: (k, 0, 0, 0)),
            pl.BlockSpec((1, blocks, 64, 128), lambda k: (k, 0, 0, 0)),
            pl.BlockSpec((1, blocks, 8, 128), lambda k: (k, 0, 0, 0)),
            pl.BlockSpec((1, 4, 512), lambda k: (k, 0, 0)),
            pl.BlockSpec((WIN, 256), lambda k: (0, 0)),
            pl.BlockSpec((128, 128), lambda k: (0, 0)),
        ],
        out_specs=[
            pl.BlockSpec((1, STEPS, WIN, 256), lambda k: (k, 0, 0, 0)),
            pl.BlockSpec((1, STEPS, WIN, 128), lambda k: (k, 0, 0, 0)),
            pl.BlockSpec((1, STEPS, 64, 128), lambda k: (k, 0, 0, 0)),
        ],
        out_shape=[
            jax.ShapeDtypeStruct((images, STEPS, WIN, 256), BF),
            jax.ShapeDtypeStruct((images, STEPS, WIN, 128), BF),
            jax.ShapeDtypeStruct((images, STEPS, 64, 128), BF),
        ],
        cost_estimate=pl.CostEstimate(
            flops=images * STEPS * 40_000_000, bytes_accessed=images * 1_000_000, transcendentals=0
        ),
        name="prepare",
    )(own, up, down, stats, depth_index, reversal(), flips())


def sweep_kernel(
    slot_ref, own_ref, oh_ref, o0_ref, o1_ref, u0_ref, u1_ref, d0_ref, d1_ref, s0_ref, s1_ref,
    sl_ref, pat_ref, mask_ref, w2_ref, flip_ref, elev_ref, cell_ref, mean_ref, rows_ref, skew,
):
    rhs = jnp.concatenate([o0_ref[0, 0], o1_ref[0, 0]], axis=1)
    up = jnp.concatenate([u0_ref[0, 0], u1_ref[0, 0]], axis=1)
    down = jnp.concatenate([d0_ref[0, 0], d1_ref[0, 0]], axis=1)
    own = own_ref[0, 0]
    own_edge = oh_ref[0, 0]
    stats = jnp.concatenate([s0_ref[0, 0], s1_ref[0, 0]], axis=1)

    mean_b, inv_b = boxed_stats(stats, up, down)

    column = 63 - lax.broadcasted_iota(jnp.int32, (64, 128), 0)
    lane = lax.broadcasted_iota(jnp.int32, (64, 128), 1)
    wrapped = lane < column
    first = lane < column + 64
    column8 = 7 - lax.broadcasted_iota(jnp.int32, (8, 128), 0)
    lane8 = lax.broadcasted_iota(jnp.int32, (8, 128), 1)
    hyp = (lane % 64).astype(F32)

    table = dot(sl_ref[0, 0], pat_ref[...])

    soft = []
    chosen = []
    for y in range(4):
        p = dot(own * mask_ref[y : y + 1, :], rhs)
        if y == 0:
            p = p + dot(own_edge[:, 0:64], up)
        if y == 3:
            p = p + dot(own_edge[:, 64:128], down)
        z = jnp.where(wrapped, p[16:80, 128:], jnp.where(first, p[80:144, :128], p[16:80, :128]))
        z8 = jnp.where(
            lane8 < column8,
            p[72:80, 128:],
            jnp.where(lane8 < column8 + 64, p[8:16, 128:], p[72:80, :128]),
        )
        skew[y, 0:8, :] = pltpu.roll(z8, 57, 1, stride=1, stride_axis=0)
        skew[y, 8:72, :] = pltpu.roll(z, 65, 1, stride=1, stride_axis=0)
        cross = skew[y, 8:72, :] + skew[y, 7:71, :] + skew[y, 6:70, :]
        mb = pltpu.roll(
            jnp.where(wrapped, mean_b[y : y + 1, 128:], mean_b[y : y + 1, :128]),
            65, 1, stride=1, stride_axis=0,
        )
        rb = pltpu.roll(
            jnp.where(wrapped, inv_b[y : y + 1, 128:], inv_b[y : y + 1, :128]),
            65, 1, stride=1, stride_axis=0,
        )
        a1 = table[:, (3 * y) * 128 : (3 * y + 1) * 128]
        a2 = table[:, (3 * y + 1) * 128 : (3 * y + 2) * 128]
        at = table[:, (3 * y + 2) * 128 : (3 * y + 3) * 128]
        weight = jnp.exp2((cross * a1 - a2 * mb) * rb)
        picked = jnp.where(at == hyp, weight, 0.0)
        for value, out in ((weight, soft), (picked, chosen)):
            high = value.astype(BF)
            low = (value - high.astype(F32)).astype(BF)
            out.append(jnp.concatenate([high, low], axis=1))
    soft = jnp.concatenate(soft, axis=0)
    chosen = jnp.concatenate(chosen, axis=0)
    w2 = w2_ref[...]
    r = lax.dot_general(w2, soft, NT, preferred_element_type=F32)
    rc = lax.dot_general(w2, chosen, NT, preferred_element_type=F32)
    inv = 1.0 / r[0:2]
    depth = (r[2:4] + r[4:6] + r[6:8]) * inv
    conf = rc[0:2] * inv
    both = jnp.concatenate([depth, conf], axis=0)
    high = both.astype(BF).astype(F32)
    mid = (both - high).astype(BF).astype(F32)
    pieces = jnp.concatenate([high, mid, both - high - mid, jnp.zeros((4, 256), F32)], axis=0)
    pieces = jnp.concatenate([pieces[:, :128], pieces[:, 128:]], axis=0).astype(BF)
    flipped = dot(pieces, flip_ref[...])
    both = jnp.concatenate([flipped[0:16], flipped[16:32]], axis=1)
    both = both[0:4] + both[4:8] + both[8:12]
    lane1 = lax.broadcasted_iota(jnp.int32, (1, 128), 1)
    left = lane1 < 64
    cell_iota = lax.broadcasted_iota(jnp.int32, (128, 128), 0)
    for y in range(4):
        part = both[:, 128 * (y // 2) : 128 * (y // 2) + 128]
        turned = pltpu.roll(part, 64, 1)
        if y % 2 == 0:
            lo, hi = part, turned
        else:
            lo, hi = turned, part
        mean_ref[0, y : y + 1, :] = jnp.where(left, lo[0:1], hi[1:2])
        c = jnp.where(left, lo[2:3], hi[3:4])
        num = c * elev_ref[0, y : y + 1, :]
        pair = jnp.concatenate([num, c], axis=0)
        pair_hi = pair.astype(BF).astype(F32)
        vals = jnp.concatenate([pair_hi, pair - pair_hi, jnp.zeros((4, 128), F32)], axis=0)
        hot = jnp.where(cell_iota == cell_ref[0, y : y + 1, :], 1.0, 0.0).astype(BF)
        binned = lax.dot_general(vals.astype(BF), hot, NT, preferred_element_type=F32)
        got = binned[0:2] + binned[2:4]
        rows_ref[0, 0, y : y + 1, 0:128] = got[0:1]
        rows_ref[0, 0, y : y + 1, 128:256] = got[1:2]


def sweep_steps(first_step, steps, slot, ownT, ohT, o0, o1, up, down, stats, sl, pat, masks, w2, flip, elev, cell, o1_by_slot):
    images = ownT.shape[0]
    st = first_step
    in_specs = [
        pl.BlockSpec((1, 1, 144, 256), lambda n, k, s: (k, n + st, 0, 0)),
        pl.BlockSpec((1, 1, 144, 128), lambda n, k, s: (k, n + st, 0, 0)),
        pl.BlockSpec((1, 1, 256, 128), lambda n, k, s: (s[k], n + st, 0, 0)),
        pl.BlockSpec((1, 1, 256, 128), (lambda n, k, s: (s[k], n + st + 1, 0, 0)) if o1_by_slot else (lambda n, k, s: (s[k], 0, 0, 0))),
    ]
    u0, u1 = up
    d0, d1 = down
    s0, s1 = stats
    near = lambda n, k, s: (k, n + st, 0, 0)
    far = (lambda n, k, s: (k, n + st + 1, 0, 0)) if o1_by_slot else (lambda n, k, s: (k, 0, 0, 0))
    in_specs += [
        pl.BlockSpec((1, 1, 64, 128), near), pl.BlockSpec((1, 1, 64, 128), far),
        pl.BlockSpec((1, 1, 64, 128), near), pl.BlockSpec((1, 1, 64, 128), far),
        pl.BlockSpec((1, 1, 8, 128), near), pl.BlockSpec((1, 1, 8, 128), far),
        pl.BlockSpec((1, 1, 64, 128), near),
        pl.BlockSpec((128, 1536), lambda n, k, s: (0, 0)),
        pl.BlockSpec((16, 256), lambda n, k, s: (0, 0)),
        pl.BlockSpec((8, 256), lambda n, k, s: (0, 0)),
        pl.BlockSpec((128, 128), lambda n, k, s: (0, 0)),
        pl.BlockSpec((1, 4, 128), lambda n, k, s: (k, 0, n + st)),
        pl.BlockSpec((1, 4, 128), lambda n, k, s: (k, 0, n + st)),
    ]
    return pl.pallas_call(
        sweep_kernel,
        grid_spec=pltpu.PrefetchScalarGridSpec(
            num_scalar_prefetch=1,
            grid=(steps, images),
            in_specs=in_specs,
            out_specs=[
                pl.BlockSpec((1, 4, 128), lambda n, k, s: (k, 0, n)),
                pl.BlockSpec((1, 1, 4, 256), lambda n, k, s: (n, k, 0, 0)),
            ],
            scratch_shapes=[pltpu.VMEM((4, 72, 128), F32)],
        ),
        out_shape=[
            jax.ShapeDtypeStruct((images, 4, steps * 128), F32),
            jax.ShapeDtypeStruct((steps, images, 4, 256), F32),
        ],
        compiler_params=pltpu.CompilerParams(vmem_limit_bytes=32 * 1024 * 1024),
        cost_estimate=pl.CostEstimate(flops=steps * images * 200_000_000, bytes_accessed=steps * images * 400_000, transcendentals=0),
        name="sweep",
    )(slot, ownT, ohT, o0, o1, u0, u1, d0, d1, s0, s1, sl, pat, masks, w2, flip, elev, cell)


def depth_weights(planes):
    high = lax.reduce_precision(planes, 8, 7)
    mid = lax.reduce_precision(planes - high, 8, 7)
    zero = jnp.zeros_like(planes)
    rows = []
    for v in (jnp.ones_like(planes), high, mid, planes - high - mid):
        rows.append(jnp.concatenate([v, zero]))
        rows.append(jnp.concatenate([zero, v]))
    w = jnp.stack(rows)
    return jnp.concatenate([w, w], axis=1).astype(BF)


def collect_kernel(list_ref, count_ref, rows_ref, out_ref):
    owners = out_ref.shape[0]
    for o in range(owners):

        def move(e, carry):
            out_ref[o, pl.ds(e, 1), :] = rows_ref[pl.ds(list_ref[o, e], 1), :]
            return carry

        lax.fori_loop(0, count_ref[o], move, 0)


def collect(row_list, counts, rows):
    owners, cap = row_list.shape
    return pl.pallas_call(
        collect_kernel,
        grid_spec=pltpu.PrefetchScalarGridSpec(
            num_scalar_prefetch=2,
            grid=(1,),
            in_specs=[pl.BlockSpec(rows.shape, lambda i, a, b: (0, 0))],
            out_specs=pl.BlockSpec((owners, cap, 2 * CELLS), lambda i, a, b: (0, 0, 0)),
        ),
        out_shape=jax.ShapeDtypeStruct((owners, cap, 2 * CELLS), F32),
        name="collect",
    )(row_list, counts, rows)


def place_kernel(slot_ref, count_ref, got_ref, out_ref):
    out_ref[...] = jnp.zeros_like(out_ref)
    for t in range(got_ref.shape[0]):

        def add(e, carry):
            at = pl.ds(slot_ref[t, e], 1)
            out_ref[at, :] = out_ref[at, :] + got_ref[t, pl.ds(e, 1), :]
            return carry

        lax.fori_loop(0, count_ref[t], add, 0)


def place(slots, counts, got, total):
    return pl.pallas_call(
        place_kernel,
        grid_spec=pltpu.PrefetchScalarGridSpec(
            num_scalar_prefetch=2,
            grid=(1,),
            in_specs=[pl.BlockSpec(got.shape, lambda i, a, b: (0, 0, 0))],
            out_specs=pl.BlockSpec((total, 2 * CELLS), lambda i, a, b: (0, 0)),
        ),
        out_shape=jax.ShapeDtypeStruct((total, 2 * CELLS), F32),
        name="place",
    )(slots, counts, got)


def neighbour_rows(head, tail):
    count = lax.axis_size("tile")
    above = lax.ppermute(tail, "tile", [(i, i + 1) for i in range(count - 1)])
    below = lax.ppermute(head, "tile", [(i + 1, i) for i in range(count - 1)])
    return above, below


def on_device(
    features, partner_ids, depth_planes, cam_height, ray_down, depth_index, cell_index,
    block_list, block_slot, block_count,
):
    group_count = lax.axis_size("img")
    owners = lax.axis_size("tile")
    my_group = lax.axis_index("img")
    my_tile = lax.axis_index("tile")
    images = features.shape[0]
    table = partner_ids.reshape(group_count, images)
    source_of = table // images
    chosen = jnp.sum(jnp.where(source_of == my_group, table % images, 0), axis=1)
    slot = lax.dynamic_index_in_dim(source_of, my_group, 0, False)

    def exchange(a):
        return lax.all_to_all(a, "img", split_axis=0, concat_axis=0, tiled=True)

    main = exchange(pick(chosen, features, 0, 4))
    last = exchange(pick(chosen, features, 4, 1))

    every = jnp.arange(images, dtype=jnp.int32)
    own = jnp.concatenate([pick(every, features, 0, 4), pick(every, features, 4, 1)], axis=1)
    own_head, own_tail, own_stats = edges(every, own)
    own_up, own_down = neighbour_rows(own_head, own_tail)
    own_turned, edge_turned, own_table = prepare(own, own_up, own_down, own_stats, depth_index)

    hyp = jnp.arange(NDEPTH, dtype=jnp.int32)[:, None, None, None]
    plane_at = jnp.sum(
        jnp.where(hyp == depth_index[None], depth_planes[:, None, None, None], 0.0), 0
    )
    elevation = cam_height[:, None, None] - ray_down * plane_at

    meta = jnp.concatenate(
        [block_slot[0, 0], jnp.broadcast_to(block_count[0, 0][:, None], (owners, 128))], axis=1
    )
    metas = [lax.dynamic_slice_in_dim(meta, my_tile, 1, 0)]
    for s in range(1, owners):
        mine = lax.dynamic_slice_in_dim(meta, (my_tile + s) % owners, 1, 0)
        metas.append(lax.ppermute(mine, "tile", [(i, (i + s) % owners) for i in range(owners)]))
    metas = jnp.concatenate(metas, axis=0)
    metas = jnp.take(metas, (my_tile - jnp.arange(owners)) % owners, axis=0)

    w2 = depth_weights(depth_planes)
    pat, masks, flip = table_patterns(), row_masks(), flips()

    head, tail, stats = edges(slot, main)
    up, down = neighbour_rows(head, tail)
    common = (own_table, pat, masks, w2, flip, elevation, cell_index)
    mean_a, rows_a = sweep_steps(
        0, 3, slot, own_turned, edge_turned, main, main, (up, up), (down, down), (stats, stats),
        *common, True,
    )
    head_l, tail_l, stats_l = edges(slot, last)
    up_l, down_l = neighbour_rows(head_l, tail_l)
    mean_b, rows_b = sweep_steps(
        3, 1, slot, own_turned, edge_turned, main, last, (up, up_l), (down, down_l),
        (stats, stats_l), *common, False,
    )
    mean_range = jnp.concatenate([mean_a, mean_b], axis=2)
    rows = jnp.concatenate([rows_a, rows_b], axis=0).reshape(-1, 2 * CELLS)

    lists = block_list[0, 0]
    blocks_per_step = rows.shape[0] // STEPS
    send = collect(lists % STEPS * blocks_per_step + lists // STEPS, block_count[0, 0], rows)
    got = lax.all_to_all(send, "tile", split_axis=0, concat_axis=0, tiled=True)
    dense = place(metas[:, :128], metas[:, 128], got, group_count * PATCH_DEV)
    parts = exchange(dense.reshape(group_count, PATCH_DEV, 2 * CELLS))
    total = jnp.sum(parts, axis=0)
    return mean_range, total[:, :CELLS] / (total[:, CELLS:] + 1.0)


def solution(mesh):
    return jax.shard_map(
        on_device,
        mesh=mesh,
        in_specs=(
            P("img", None, "tile", None),
            P(),
            P(),
            P("img"),
            P("img", "tile", None),
            P("img", "tile", None),
            P("img", "tile", None),
            P("img", "tile", None, None),
            P("img", "tile", None, None),
            P("img", "tile", None),
        ),
        out_specs=(P("img", "tile", None), P(("img", "tile"), None)),
        check_vma=False,
    )
```

```python
import math

import numpy as np
import jax
import jax.numpy as jnp
from jax import lax
from jax.experimental import pallas as pl
from jax.experimental.pallas import tpu as pltpu
from jax.sharding import PartitionSpec as P

NDEPTH = 64
CELLS = 128
PATCH_DEV = 16
STEPS = 4
WIN = 144
LOG2E = math.log2(math.e)
BF = jnp.bfloat16
F32 = jnp.float32
NT = (((1,), (1,)), ((), ()))
PARAMS = pltpu.CompilerParams(vmem_limit_bytes=60 * 1024 * 1024)


def dot(a, b):
    return jnp.dot(a, b, preferred_element_type=F32)


def dot_nt(a, b):
    return lax.dot_general(a, b, NT, preferred_element_type=F32)


def table_patterns():
    pat = np.zeros((128, 12, 128), np.float32)
    for half in range(2):
        lanes = slice(64 * half, 64 * half + 64)
        for y in range(4):
            for q in range(2):
                for s in range(3):
                    pat[half * 32 + s * 8 + q * 4 + y, y * 3 + q, lanes] = 1.0
            pat[half * 32 + 24 + y, y * 3 + 2, lanes] = 1.0
    return jnp.asarray(pat.reshape(128, 12 * 128), BF)


def row_masks():
    y = np.arange(16)[:, None]
    k = np.arange(256)[None, :] % 4
    return jnp.asarray((np.abs(k - y) <= 1) & (y < 4), BF)


def flips():
    m = np.zeros((128, 128), np.float32)
    for i in range(128):
        m[i, i // 64 * 64 + 63 - i % 64] = 1.0
    return jnp.asarray(m, BF)


def reversal():
    m = np.zeros((WIN, 256), np.float32)
    for i in range(WIN):
        m[i, WIN - 1 - i] = 1.0
    return jnp.asarray(m, BF)


def edge_constants():
    sel = np.zeros((128, 256), np.float32)
    for c in range(64):
        sel[c, 4 * c] = 1.0
        sel[64 + c, 4 * c + 3] = 1.0
    stat = np.zeros((16, 256), np.float32)
    for y in range(4):
        stat[y, y::4] = 1.0
        stat[12 + y, y::4] = 1.0
    return jnp.asarray(sel, BF), jnp.asarray(stat, BF)


def split2(a):
    high = a.astype(BF)
    return high, (a - high.astype(F32)).astype(BF)


def boxed_stats(stats, up, down):
    upf = up.astype(F32)
    downf = down.astype(F32)
    sums = [jnp.sum(upf, 0, keepdims=True)] + [stats[y : y + 1] for y in range(4)]
    sums.append(jnp.sum(downf, 0, keepdims=True))
    sqs = [jnp.sum(upf * upf, 0, keepdims=True)] + [stats[4 + y : 5 + y] for y in range(4)]
    sqs.append(jnp.sum(downf * downf, 0, keepdims=True))
    tall = jnp.concatenate(
        [v[y] + v[y + 1] + v[y + 2] for v in (sums, sqs) for y in range(4)], axis=0
    )
    boxed = (tall + pltpu.roll(tall, 255, 1) + pltpu.roll(tall, 254, 1)) * (1.0 / 576.0)
    mean = boxed[0:4]
    return mean, lax.rsqrt(boxed[4:8] - mean * mean + 1e-5)


DEPTH = 8
PART = 4
PACKED = 136


def pick(idx, features, blocks):
    count = idx.shape[0]
    _, channels, rows, _ = features.shape
    ahead = DEPTH // 2

    def kernel(idx_ref, features_ref, out_ref, strips, in_sem, out_sem):
        def read(s):
            return pltpu.make_async_copy(
                features_ref.at[idx_ref[s], :, :, pl.ds(0, 128 * blocks)],
                strips.at[s % DEPTH],
                in_sem.at[s % DEPTH],
            )

        def write(s, j):
            return pltpu.make_async_copy(
                strips.at[s % DEPTH, :, :, pl.ds(128 * j, 128)],
                out_ref.at[s, j],
                out_sem.at[s % DEPTH, j],
            )

        for s in range(DEPTH):
            read(s).start()
        for s in range(count):
            read(s).wait()
            for j in range(blocks):
                write(s, j).start()
            later = s + ahead
            if DEPTH <= later < count:
                for j in range(blocks):
                    write(later - DEPTH, j).wait()
                read(later).start()
        for s in range(count - DEPTH, count):
            for j in range(blocks):
                write(s, j).wait()

    out = pl.pallas_call(
        kernel,
        grid_spec=pltpu.PrefetchScalarGridSpec(
            num_scalar_prefetch=1,
            grid=(1,),
            in_specs=[pl.BlockSpec(memory_space=pl.ANY)],
            out_specs=pl.BlockSpec(memory_space=pl.ANY),
            scratch_shapes=[
                pltpu.VMEM((DEPTH, channels, rows, 128 * blocks), BF),
                pltpu.SemaphoreType.DMA((DEPTH,)),
                pltpu.SemaphoreType.DMA((DEPTH, blocks)),
            ],
        ),
        out_shape=jax.ShapeDtypeStruct((count, blocks, channels, rows, 128), BF),
        compiler_params=PARAMS,
        cost_estimate=pl.CostEstimate(
            flops=0, bytes_accessed=count * blocks * 131072, transcendentals=0
        ),
        name="pick",
    )(idx, features)
    return out.reshape(count, blocks, channels * rows, 128)


def pack_constants():
    spread = np.zeros((128, 256), np.float32)
    for i in range(64):
        spread[i, i] = 1.0
        spread[64 + i, 128 + i] = 1.0
    column = np.zeros((8, 128), np.float32)
    column[0, 64] = 1.0
    into = np.zeros((256, 128), np.float32)
    into[:, 64] = 1.0
    return tuple(jnp.asarray(m, BF) for m in (spread, column, into, np.eye(256)))


def pack_kernel(idx_ref, *refs):
    blocks, (spread_ref, column_ref, out_ref) = refs[:PART], refs[PART:]
    for g in range(PART):
        block = blocks[g][0, 0]
        out_ref[g, 0:128, :] = (
            dot_nt(block[0:128], spread_ref[:, 0:128]) + dot_nt(block[128:256], spread_ref[:, 128:])
        ).astype(BF)
        line = dot_nt(column_ref[...], block)
        out_ref[g, 128:136, :] = jnp.concatenate(
            [line[0:1, 0:128], line[0:1, 128:256], jnp.zeros((6, 128), F32)], axis=0
        ).astype(BF)


def pack(idx, own):
    count = idx.shape[0]
    spread, column, _, _ = pack_constants()

    def chosen(g):
        return lambda k, s: (s[PART * k + g], STEPS, 0, 0)

    return pl.pallas_call(
        pack_kernel,
        grid_spec=pltpu.PrefetchScalarGridSpec(
            num_scalar_prefetch=1,
            grid=(count // PART,),
            in_specs=[pl.BlockSpec((1, 1, 256, 128), chosen(g)) for g in range(PART)]
            + [
                pl.BlockSpec((128, 256), lambda k, s: (0, 0)),
                pl.BlockSpec((8, 128), lambda k, s: (0, 0)),
            ],
            out_specs=pl.BlockSpec((PART, PACKED, 128), lambda k, s: (k, 0, 0)),
        ),
        out_shape=jax.ShapeDtypeStruct((count, PACKED, 128), BF),
        compiler_params=PARAMS,
        name="pack",
    )(idx, *[own] * PART, spread, column)


def block_edges(block, sel_ref, stat_ref):
    rows = dot(sel_ref[...], block).astype(BF)
    value = block.astype(F32)
    high, low = split2(value * value)
    stats = dot(stat_ref[0:8], block) + dot(stat_ref[8:16], high) + dot(stat_ref[8:16], low)
    return rows[0:64], rows[64:128], stats


def edge_kernel(slot_ref, *refs):
    blocks, (sel_ref, stat_ref, head_ref, tail_ref, stats_ref) = refs[:PART], refs[PART:]
    for g in range(PART):
        for j in range(stats_ref.shape[1]):
            head, tail, stats = block_edges(blocks[g][0, j], sel_ref, stat_ref)
            head_ref[g, j] = head
            tail_ref[g, j] = tail
            stats_ref[g, j] = stats


def unpack_kernel(slot_ref, *refs):
    packed = refs[:PART]
    (
        spread_ref, into_ref, eye_ref, sel_ref, stat_ref, head_ref, tail_ref, stats_ref, block_ref,
    ) = refs[PART:]
    for g in range(PART):
        wide = dot(packed[g][0, 0:128, :], spread_ref[...])
        line = packed[g][0, 128:136, :]
        line = jnp.concatenate([line[0:1], line[1:2]], axis=1)
        column = dot(eye_ref[...] * line, into_ref[...])
        block = jnp.concatenate([wide[:, :128], wide[:, 128:]], axis=0) + column
        block = block.astype(BF)
        block_ref[g, 0] = block
        head, tail, stats = block_edges(block, sel_ref, stat_ref)
        head_ref[g, 0] = head
        tail_ref[g, 0] = tail
        stats_ref[g, 0] = stats


def edge_outputs(images, blocks):
    specs = [
        pl.BlockSpec((PART, blocks, 64, 128), lambda k, s: (k, 0, 0, 0)),
        pl.BlockSpec((PART, blocks, 64, 128), lambda k, s: (k, 0, 0, 0)),
        pl.BlockSpec((PART, blocks, 8, 128), lambda k, s: (k, 0, 0, 0)),
    ]
    shapes = [
        jax.ShapeDtypeStruct((images, blocks, 64, 128), BF),
        jax.ShapeDtypeStruct((images, blocks, 64, 128), BF),
        jax.ShapeDtypeStruct((images, blocks, 8, 128), F32),
    ]
    return specs, shapes


def whole_spec(a):
    return pl.BlockSpec(a.shape, lambda k, s: (0,) * a.ndim)


def edges(slot, recv):
    images, blocks = slot.shape[0], recv.shape[1]
    constants = edge_constants()
    specs, shapes = edge_outputs(images, blocks)

    def by_slot(g):
        return lambda k, s: (s[PART * k + g], 0, 0, 0)

    return pl.pallas_call(
        edge_kernel,
        grid_spec=pltpu.PrefetchScalarGridSpec(
            num_scalar_prefetch=1,
            grid=(images // PART,),
            in_specs=[pl.BlockSpec((1, blocks, 256, 128), by_slot(g)) for g in range(PART)]
            + [whole_spec(a) for a in constants],
            out_specs=specs,
        ),
        out_shape=shapes,
        cost_estimate=pl.CostEstimate(
            flops=images * blocks * 20_000_000, bytes_accessed=images * blocks * 100_000,
            transcendentals=0,
        ),
        compiler_params=PARAMS,
        name="edges",
    )(slot, *[recv] * PART, *constants)


def unpack(slot, packed):
    images = slot.shape[0]
    spread, _, into, eye = pack_constants()
    constants = (spread, into, eye) + edge_constants()
    specs, shapes = edge_outputs(images, 1)

    def by_slot(g):
        return lambda k, s: (s[PART * k + g], 0, 0)

    return pl.pallas_call(
        unpack_kernel,
        grid_spec=pltpu.PrefetchScalarGridSpec(
            num_scalar_prefetch=1,
            grid=(images // PART,),
            in_specs=[pl.BlockSpec((1, PACKED, 128), by_slot(g)) for g in range(PART)]
            + [whole_spec(a) for a in constants],
            out_specs=specs + [pl.BlockSpec((PART, 1, 256, 128), lambda k, s: (k, 0, 0, 0))],
        ),
        out_shape=shapes + [jax.ShapeDtypeStruct((images, 1, 256, 128), BF)],
        compiler_params=PARAMS,
        name="unpack",
    )(slot, *[packed] * PART, *constants)


def prepare_kernel(
    own_ref, up_ref, down_ref, stat_ref, index_ref, rev_ref, flip_ref, own_out, edge_out, table_out
):
    mean_inv = 24.0 * LOG2E
    for n in range(STEPS):
        block = jnp.concatenate([own_ref[0, n], own_ref[0, n + 1]], axis=1)
        up = jnp.concatenate([up_ref[0, n], up_ref[0, n + 1]], axis=1)
        down = jnp.concatenate([down_ref[0, n], down_ref[0, n + 1]], axis=1)
        own_out[0, n] = dot_nt(rev_ref[...], block).astype(BF)
        edge_out[0, n] = dot_nt(rev_ref[...], jnp.concatenate([up, down], axis=0)).astype(BF)
        stats = jnp.concatenate([stat_ref[0, n], stat_ref[0, n + 1]], axis=1)
        mean, inv = boxed_stats(stats, up, down)
        scaled = inv * mean_inv
        both = jnp.concatenate([scaled * (1.0 / 576.0), scaled * mean], axis=0)[:, :128]
        high = both.astype(BF).astype(F32)
        mid = (both - high).astype(BF).astype(F32)
        index = index_ref[0, :, 128 * n : 128 * n + 128].astype(F32)
        rows = jnp.concatenate(
            [high, mid, both - high - mid, index, jnp.zeros((4, 128), F32)], axis=0
        ).astype(BF)
        blank = jnp.zeros((64, 64), F32)
        left = dot_nt(flip_ref[0:64, :], rows)
        right = dot_nt(flip_ref[64:128, :], rows)
        table_out[0, n] = jnp.concatenate([left, right, blank], axis=1).astype(BF)


def prepare(own, up, down, stats, depth_index):
    images, blocks = own.shape[0], own.shape[1]
    return pl.pallas_call(
        prepare_kernel,
        grid=(images,),
        in_specs=[
            pl.BlockSpec((1, blocks, 256, 128), lambda k: (k, 0, 0, 0)),
            pl.BlockSpec((1, blocks, 64, 128), lambda k: (k, 0, 0, 0)),
            pl.BlockSpec((1, blocks, 64, 128), lambda k: (k, 0, 0, 0)),
            pl.BlockSpec((1, blocks, 8, 128), lambda k: (k, 0, 0, 0)),
            pl.BlockSpec((1, 4, 512), lambda k: (k, 0, 0)),
            pl.BlockSpec((WIN, 256), lambda k: (0, 0)),
            pl.BlockSpec((128, 128), lambda k: (0, 0)),
        ],
        out_specs=[
            pl.BlockSpec((1, STEPS, WIN, 256), lambda k: (k, 0, 0, 0)),
            pl.BlockSpec((1, STEPS, WIN, 128), lambda k: (k, 0, 0, 0)),
            pl.BlockSpec((1, STEPS, 64, 128), lambda k: (k, 0, 0, 0)),
        ],
        out_shape=[
            jax.ShapeDtypeStruct((images, STEPS, WIN, 256), BF),
            jax.ShapeDtypeStruct((images, STEPS, WIN, 128), BF),
            jax.ShapeDtypeStruct((images, STEPS, 64, 128), BF),
        ],
        cost_estimate=pl.CostEstimate(
            flops=images * STEPS * 40_000_000, bytes_accessed=images * 1_000_000, transcendentals=0
        ),
        compiler_params=PARAMS,
        name="prepare",
    )(own, up, down, stats, depth_index, reversal(), flips())


GROUP = 8


def skewed(left, right, column, lane, shift):
    return pltpu.roll(jnp.where(lane < column, right, left), shift, 1, stride=1, stride_axis=0)


def sweep_kernel(slot_ref, *refs):
    near_refs, far_refs = refs[:GROUP], refs[GROUP : 2 * GROUP]
    (
        own_ref, edge_ref, u0_ref, u1_ref, d0_ref, d1_ref, s0_ref, s1_ref, table_ref, pat_ref,
        mask_ref, w2_ref, flip_ref, elev_ref, cell_ref, mean_ref, rows_ref, skew,
    ) = refs[2 * GROUP :]
    column = 63 - lax.broadcasted_iota(jnp.int32, (64, 128), 0)
    lane = lax.broadcasted_iota(jnp.int32, (64, 128), 1)
    wrapped = lane < column
    first = lane < column + 64
    column8 = 7 - lax.broadcasted_iota(jnp.int32, (8, 128), 0)
    lane8 = lax.broadcasted_iota(jnp.int32, (8, 128), 1)
    hyp = (lane % 64).astype(F32)
    tables = dot(table_ref[:, 0].reshape(GROUP * 64, 128), pat_ref[...])

    soft = []
    chosen = []
    for g in range(GROUP):
        rhs = jnp.concatenate([near_refs[g][0, 0], far_refs[g][0, 0]], axis=1)
        up = jnp.concatenate([u0_ref[g, 0], u1_ref[g, 0]], axis=1)
        down = jnp.concatenate([d0_ref[g, 0], d1_ref[g, 0]], axis=1)
        stats = jnp.concatenate([s0_ref[g, 0], s1_ref[g, 0]], axis=1)
        mean_b, inv_b = boxed_stats(stats, up, down)
        own = own_ref[g, 0]
        masked = jnp.concatenate([own * mask_ref[y : y + 1, :] for y in range(4)], axis=0)
        product = dot(masked, rhs)
        above = dot(edge_ref[g, 0][:, 0:64], up)
        below = dot(edge_ref[g, 0][:, 64:128], down)
        for y in range(4):
            p = product[WIN * y : WIN * y + WIN]
            if y == 0:
                p = p + above
            if y == 3:
                p = p + below
            z = jnp.where(
                wrapped, p[16:80, 128:], jnp.where(first, p[80:144, :128], p[16:80, :128])
            )
            z8 = jnp.where(
                lane8 < column8,
                p[72:80, 128:],
                jnp.where(lane8 < column8 + 64, p[8:16, 128:], p[72:80, :128]),
            )
            at = 4 * g + y
            skew[at, 0:8, :] = pltpu.roll(z8, 57, 1, stride=1, stride_axis=0)
            skew[at, 8:72, :] = pltpu.roll(z, 65, 1, stride=1, stride_axis=0)
            cross = skew[at, 8:72, :] + skew[at, 7:71, :] + skew[at, 6:70, :]
            mb = skewed(mean_b[y : y + 1, :128], mean_b[y : y + 1, 128:], column, lane, 65)
            rb = skewed(inv_b[y : y + 1, :128], inv_b[y : y + 1, 128:], column, lane, 65)
            a1, a2, index = (
                tables[64 * g : 64 * g + 64, (3 * y + q) * 128 : (3 * y + q + 1) * 128]
                for q in range(3)
            )
            weight = jnp.exp2((cross * a1 - a2 * mb) * rb)
            picked = jnp.where(index == hyp, weight, 0.0)
            soft.append(jnp.concatenate(split2(weight), axis=1))
            chosen.append(jnp.concatenate(split2(picked), axis=1))
    soft = jnp.concatenate(soft, axis=0)
    chosen = jnp.concatenate(chosen, axis=0)
    r = dot_nt(w2_ref[...], soft)
    rc = dot_nt(w2_ref[...], chosen)
    inv = 1.0 / r[0:2]
    both = jnp.concatenate([(r[2:4] + r[4:6] + r[6:8]) * inv, rc[0:2] * inv], axis=0)
    both = jnp.concatenate([both[:, 128 * v : 128 * v + 128] for v in range(2 * GROUP)], axis=0)
    high = both.astype(BF)
    rest = both - high.astype(F32)
    mid = rest.astype(BF)
    low = (rest - mid.astype(F32)).astype(BF)
    both = dot(jnp.concatenate([high, mid, low], axis=0), flip_ref[...])
    both = both[0 : 8 * GROUP] + both[8 * GROUP : 16 * GROUP] + both[16 * GROUP : 24 * GROUP]
    turned = pltpu.roll(both, 64, 1)
    left = lax.broadcasted_iota(jnp.int32, (1, 128), 1) < 64
    cell_iota = lax.broadcasted_iota(jnp.int32, (128, 128), 0)
    for g in range(GROUP):
        for y in range(4):
            at = (2 * g + y // 2) * 4
            lo, hi = (both, turned) if y % 2 == 0 else (turned, both)
            mean_ref[g, y : y + 1, :] = jnp.where(left, lo[at : at + 1], hi[at + 1 : at + 2])
            c = jnp.where(left, lo[at + 2 : at + 3], hi[at + 3 : at + 4])
            pair = jnp.concatenate([c * elev_ref[g, y : y + 1, :], c], axis=0)
            pair_hi = pair.astype(BF).astype(F32)
            vals = jnp.concatenate([pair_hi, pair - pair_hi, jnp.zeros((4, 128), F32)], axis=0)
            hot = jnp.where(cell_iota == cell_ref[g, y : y + 1, :], 1.0, 0.0).astype(BF)
            binned = dot_nt(vals.astype(BF), hot)
            got = binned[0:2] + binned[2:4]
            at = 4 * g + y
            rows_ref[0, at : at + 1, 0:128] = got[0:1]
            rows_ref[0, at : at + 1, 128:256] = got[1:2]


def sweep_steps(
    first, steps, slot, own, edge, main, far_blocks, up, down, stats, table, pat, masks, w2, flip,
    elev, cell, far_in_main,
):
    images = own.shape[0]

    def slot_near(g):
        return lambda n, k, s: (s[GROUP * k + g], n + first, 0, 0)

    def slot_far(g):
        if far_in_main:
            return lambda n, k, s: (s[GROUP * k + g], n + first + 1, 0, 0)
        return lambda n, k, s: (GROUP * k + g, 0, 0, 0)

    def near(n, k, s):
        return (k, n + first, 0, 0)

    def far(n, k, s):
        return (k, n + first + 1, 0, 0) if far_in_main else (k, 0, 0, 0)

    def whole(n, k, s):
        return (0, 0)

    def pixels(n, k, s):
        return (k, 0, n + first)

    in_specs = [pl.BlockSpec((1, 1, 256, 128), slot_near(g)) for g in range(GROUP)]
    in_specs += [pl.BlockSpec((1, 1, 256, 128), slot_far(g)) for g in range(GROUP)]
    in_specs += [
        pl.BlockSpec((GROUP, 1, WIN, 256), near),
        pl.BlockSpec((GROUP, 1, WIN, 128), near),
        pl.BlockSpec((GROUP, 1, 64, 128), near),
        pl.BlockSpec((GROUP, 1, 64, 128), far),
        pl.BlockSpec((GROUP, 1, 64, 128), near),
        pl.BlockSpec((GROUP, 1, 64, 128), far),
        pl.BlockSpec((GROUP, 1, 8, 128), near),
        pl.BlockSpec((GROUP, 1, 8, 128), far),
        pl.BlockSpec((GROUP, 1, 64, 128), near),
        pl.BlockSpec((128, 1536), whole),
        pl.BlockSpec((16, 256), whole),
        pl.BlockSpec((8, 256), whole),
        pl.BlockSpec((128, 128), whole),
        pl.BlockSpec((GROUP, 4, 128), pixels),
        pl.BlockSpec((GROUP, 4, 128), pixels),
    ]
    return pl.pallas_call(
        sweep_kernel,
        grid_spec=pltpu.PrefetchScalarGridSpec(
            num_scalar_prefetch=1,
            grid=(steps, images // GROUP),
            in_specs=in_specs,
            out_specs=[
                pl.BlockSpec((GROUP, 4, 128), lambda n, k, s: (k, 0, n)),
                pl.BlockSpec((1, 4 * GROUP, 256), lambda n, k, s: (n, k, 0)),
            ],
            scratch_shapes=[pltpu.VMEM((4 * GROUP, 72, 128), F32)],
        ),
        out_shape=[
            jax.ShapeDtypeStruct((images, 4, steps * 128), F32),
            jax.ShapeDtypeStruct((steps, images * 4, 256), F32),
        ],
        compiler_params=PARAMS,
        cost_estimate=pl.CostEstimate(
            flops=steps * images * 200_000_000, bytes_accessed=steps * images * 400_000,
            transcendentals=0,
        ),
        name="sweep",
    )(
        slot, *[main] * GROUP, *[far_blocks] * GROUP, own, edge, up[0], up[1], down[0], down[1],
        stats[0], stats[1], table, pat, masks, w2, flip, elev, cell,
    )


def depth_weights(planes):
    high = lax.reduce_precision(planes, 8, 7)
    mid = lax.reduce_precision(planes - high, 8, 7)
    zero = jnp.zeros_like(planes)
    rows = []
    for v in (jnp.ones_like(planes), high, mid, planes - high - mid):
        rows.append(jnp.concatenate([v, zero]))
        rows.append(jnp.concatenate([zero, v]))
    w = jnp.stack(rows)
    return jnp.concatenate([w, w], axis=1).astype(BF)


def collect_kernel(list_ref, count_ref, a_ref, b_ref, c_ref, out_ref, rows):
    at = 0
    for part in (a_ref, b_ref, c_ref):
        for n in range(part.shape[0]):
            rows[at : at + part.shape[1], :] = part[n]
            at += part.shape[1]
    for o in range(out_ref.shape[0]):

        def move(step, carry):
            for i in range(8):
                e = step * 8 + i
                out_ref[o, pl.ds(e, 1), :] = rows[pl.ds(list_ref[o, e], 1), :]
            return carry

        lax.fori_loop(0, (count_ref[o] + 7) // 8, move, 0)


def collect(row_list, counts, parts):
    owners, cap = row_list.shape
    total = sum(p.shape[0] * p.shape[1] for p in parts)
    return pl.pallas_call(
        collect_kernel,
        grid_spec=pltpu.PrefetchScalarGridSpec(
            num_scalar_prefetch=2,
            grid=(1,),
            in_specs=[pl.BlockSpec(p.shape, lambda i, a, b: (0, 0, 0)) for p in parts],
            out_specs=pl.BlockSpec((owners, cap, 2 * CELLS), lambda i, a, b: (0, 0, 0)),
            scratch_shapes=[pltpu.VMEM((total, 2 * CELLS), F32)],
        ),
        out_shape=jax.ShapeDtypeStruct((owners, cap, 2 * CELLS), F32),
        compiler_params=PARAMS,
        name="collect",
    )(row_list, counts, *parts)


def place_kernel(slot_ref, count_ref, got_ref, out_ref):
    out_ref[...] = jnp.zeros_like(out_ref)
    for t in range(got_ref.shape[0]):
        count = count_ref[t]

        def add(step, carry):
            for i in range(8):
                e = step * 8 + i
                at = pl.ds(slot_ref[t, e], 1)
                row = jnp.where(e < count, got_ref[t, pl.ds(e, 1), :], 0.0)
                out_ref[at, :] = out_ref[at, :] + row
            return carry

        lax.fori_loop(0, (count + 7) // 8, add, 0)


def place(slots, counts, got, total):
    return pl.pallas_call(
        place_kernel,
        grid_spec=pltpu.PrefetchScalarGridSpec(
            num_scalar_prefetch=2,
            grid=(1,),
            in_specs=[pl.BlockSpec(got.shape, lambda i, a, b: (0, 0, 0))],
            out_specs=pl.BlockSpec((total, 2 * CELLS), lambda i, a, b: (0, 0)),
        ),
        out_shape=jax.ShapeDtypeStruct((total, 2 * CELLS), F32),
        compiler_params=PARAMS,
        name="place",
    )(slots, counts, got)


def neighbour_rows(head, tail):
    count = lax.axis_size("tile")
    above = lax.ppermute(tail, "tile", [(i, i + 1) for i in range(count - 1)])
    below = lax.ppermute(head, "tile", [(i + 1, i) for i in range(count - 1)])
    return above, below


def on_device(
    features, partner_ids, depth_planes, cam_height, ray_down, depth_index, cell_index,
    block_list, block_slot, block_count,
):
    group_count = lax.axis_size("img")
    owners = lax.axis_size("tile")
    my_group = lax.axis_index("img")
    my_tile = lax.axis_index("tile")
    images = features.shape[0]
    table = partner_ids.reshape(group_count, images)
    source_of = table // images
    chosen = jnp.sum(jnp.where(source_of == my_group, table % images, 0), axis=1)
    slot = lax.dynamic_index_in_dim(source_of, my_group, 0, False)

    def exchange(a):
        return lax.all_to_all(a, "img", split_axis=0, concat_axis=0, tiled=True)

    main = exchange(pick(chosen, features, STEPS))

    every = jnp.arange(images, dtype=jnp.int32)
    own = pick(every, features, STEPS + 1)
    own_head, own_tail, own_stats = edges(every, own)
    own_up, own_down = neighbour_rows(own_head, own_tail)
    own_turned, edge_turned, own_table = prepare(own, own_up, own_down, own_stats, depth_index)
    packed = pack(chosen, own)

    hyp = jnp.arange(NDEPTH, dtype=jnp.int32)[:, None, None, None]
    plane_at = jnp.sum(
        jnp.where(hyp == depth_index[None], depth_planes[:, None, None, None], 0.0), 0
    )
    elevation = cam_height[:, None, None] - ray_down * plane_at

    meta = jnp.concatenate(
        [block_slot[0, 0], jnp.broadcast_to(block_count[0, 0][:, None], (owners, 128))], axis=1
    )
    metas = [lax.dynamic_slice_in_dim(meta, my_tile, 1, 0)]
    for s in range(1, owners):
        mine = lax.dynamic_slice_in_dim(meta, (my_tile + s) % owners, 1, 0)
        metas.append(lax.ppermute(mine, "tile", [(i, (i + s) % owners) for i in range(owners)]))
    metas = jnp.concatenate(metas, axis=0)
    metas = jnp.take(metas, (my_tile - jnp.arange(owners)) % owners, axis=0)

    w2 = depth_weights(depth_planes)
    pat, masks, flip = table_patterns(), row_masks(), flips()

    last = exchange(packed)
    main, _, own_turned, edge_turned, own_table, elevation, metas, w2 = lax.optimization_barrier(
        (main, packed, own_turned, edge_turned, own_table, elevation, metas, w2)
    )
    head, tail, stats = edges(slot, main)
    up, down = neighbour_rows(head, tail)
    common = (own_table, pat, masks, w2, flip, elevation, cell_index)

    def inner(first, steps):
        return sweep_steps(
            first, steps, slot, own_turned, edge_turned, main, main, (up, up), (down, down),
            (stats, stats), *common, True,
        )

    mean_a, rows_a = inner(0, 2)
    last, mean_a = lax.optimization_barrier((last, mean_a))
    head_l, tail_l, stats_l, far = unpack(slot, last)
    up_l, down_l = neighbour_rows(head_l, tail_l)
    mean_b, rows_b = inner(2, 1)
    mean_c, rows_c = sweep_steps(
        3, 1, slot, own_turned, edge_turned, main, far, (up, up_l), (down, down_l),
        (stats, stats_l), *common, False,
    )
    mean_range = jnp.concatenate([mean_a, mean_b, mean_c], axis=2)

    lists = block_list[0, 0]
    row_list = lists % STEPS * rows_c.shape[1] + lists // STEPS
    send = collect(row_list, block_count[0, 0], (rows_a, rows_b, rows_c))
    got = lax.all_to_all(send, "tile", split_axis=0, concat_axis=0, tiled=True)
    dense = place(metas[:, :128], metas[:, 128], got, group_count * PATCH_DEV)
    parts = exchange(dense.reshape(group_count, PATCH_DEV, 2 * CELLS))
    total = jnp.sum(parts, axis=0)
    return mean_range, total[:, :CELLS] / (total[:, CELLS:] + 1.0)


def solution(mesh):
    return jax.shard_map(
        on_device,
        mesh=mesh,
        in_specs=(
            P("img", None, "tile", None),
            P(),
            P(),
            P("img"),
            P("img", "tile", None),
            P("img", "tile", None),
            P("img", "tile", None),
            P("img", "tile", None, None),
            P("img", "tile", None, None),
            P("img", "tile", None),
        ),
        out_specs=(P("img", "tile", None), P(("img", "tile"), None)),
        check_vma=False,
    )
```

```python
import functools
import math

import numpy as np
import jax
import jax.numpy as jnp
from jax import lax
from jax.experimental import pallas as pl
from jax.experimental.pallas import tpu as pltpu
from jax.sharding import PartitionSpec as P

NDEPTH = 64
CELLS = 128
PATCH_DEV = 16
STEPS = 4
WIN = 144
LOG2E = math.log2(math.e)
BF = jnp.bfloat16
F32 = jnp.float32
NT = (((1,), (1,)), ((), ()))
PARAMS = pltpu.CompilerParams(vmem_limit_bytes=60 * 1024 * 1024)


def dot(a, b):
    return jnp.dot(a, b, preferred_element_type=F32)


def dot_nt(a, b):
    return lax.dot_general(a, b, NT, preferred_element_type=F32)


def table_patterns(ys):
    pat = np.zeros((128, 3 * len(ys), 128), np.float32)
    for half in range(2):
        lanes = slice(64 * half, 64 * half + 64)
        for i, y in enumerate(ys):
            for q in range(2):
                for s in range(3):
                    pat[half * 32 + s * 8 + q * 4 + y, i * 3 + q, lanes] = 1.0
            pat[half * 32 + 24 + y, i * 3 + 2, lanes] = 1.0
    return jnp.asarray(pat.reshape(128, -1), BF)


def row_masks():
    y = np.arange(16)[:, None]
    k = np.arange(256)[None, :] % 4
    return jnp.asarray((np.abs(k - y) <= 1) & (y < 4), BF)


def flips():
    m = np.zeros((128, 128), np.float32)
    for i in range(128):
        m[i, i // 64 * 64 + 63 - i % 64] = 1.0
    return jnp.asarray(m, BF)


def reversal():
    m = np.zeros((WIN, 256), np.float32)
    for i in range(WIN):
        m[i, WIN - 1 - i] = 1.0
    return jnp.asarray(m, BF)


def edge_constants():
    sel = np.zeros((128, 256), np.float32)
    for c in range(64):
        sel[c, 4 * c] = 1.0
        sel[64 + c, 4 * c + 3] = 1.0
    stat = np.zeros((16, 256), np.float32)
    for y in range(4):
        stat[y, y::4] = 1.0
        stat[12 + y, y::4] = 1.0
    return jnp.asarray(sel, BF), jnp.asarray(stat, BF)


def split2(a):
    high = a.astype(BF)
    return high, (a - high.astype(F32)).astype(BF)


def boxed_stats(stats, up, down):
    blank = jnp.zeros((1, 256), F32)
    sums = [blank] + [stats[y : y + 1] for y in range(4)] + [blank]
    sqs = [blank] + [stats[4 + y : 5 + y] for y in range(4)] + [blank]
    if up is not None:
        for at, halo in ((0, up.astype(F32)), (5, down.astype(F32))):
            sums[at] = jnp.sum(halo, 0, keepdims=True)
            sqs[at] = jnp.sum(halo * halo, 0, keepdims=True)
    tall = jnp.concatenate(
        [v[y] + v[y + 1] + v[y + 2] for v in (sums, sqs) for y in range(4)], axis=0
    )
    boxed = (tall + pltpu.roll(tall, 255, 1) + pltpu.roll(tall, 254, 1)) * (1.0 / 576.0)
    mean = boxed[0:4]
    return mean, lax.rsqrt(boxed[4:8] - mean * mean + 1e-5)


DEPTH = 8
PART = 4
PACKED = 136
FIRST = 3


def pick(idx, features, blocks):
    count = idx.shape[0]
    _, channels, rows, _ = features.shape
    ahead = DEPTH // 2

    def kernel(idx_ref, features_ref, out_ref, strips, in_sem, out_sem):
        def read(s):
            return pltpu.make_async_copy(
                features_ref.at[idx_ref[s], :, :, pl.ds(0, 128 * blocks)],
                strips.at[s % DEPTH],
                in_sem.at[s % DEPTH],
            )

        def write(s, j):
            return pltpu.make_async_copy(
                strips.at[s % DEPTH, :, :, pl.ds(128 * j, 128)],
                out_ref.at[s, j],
                out_sem.at[s % DEPTH, j],
            )

        for s in range(DEPTH):
            read(s).start()
        for s in range(count):
            read(s).wait()
            for j in range(blocks):
                write(s, j).start()
            later = s + ahead
            if DEPTH <= later < count:
                for j in range(blocks):
                    write(later - DEPTH, j).wait()
                read(later).start()
        for s in range(count - DEPTH, count):
            for j in range(blocks):
                write(s, j).wait()

    out = pl.pallas_call(
        kernel,
        grid_spec=pltpu.PrefetchScalarGridSpec(
            num_scalar_prefetch=1,
            grid=(1,),
            in_specs=[pl.BlockSpec(memory_space=pl.ANY)],
            out_specs=pl.BlockSpec(memory_space=pl.ANY),
            scratch_shapes=[
                pltpu.VMEM((DEPTH, channels, rows, 128 * blocks), BF),
                pltpu.SemaphoreType.DMA((DEPTH,)),
                pltpu.SemaphoreType.DMA((DEPTH, blocks)),
            ],
        ),
        out_shape=jax.ShapeDtypeStruct((count, blocks, channels, rows, 128), BF),
        compiler_params=PARAMS,
        cost_estimate=pl.CostEstimate(
            flops=0, bytes_accessed=count * blocks * 131072, transcendentals=0
        ),
        name="pick",
    )(idx, features)
    return out.reshape(count, blocks, channels * rows, 128)


def pack_constants():
    spread = np.zeros((128, 256), np.float32)
    for i in range(64):
        spread[i, i] = 1.0
        spread[64 + i, 128 + i] = 1.0
    column = np.zeros((8, 128), np.float32)
    column[0, 64] = 1.0
    into = np.zeros((256, 128), np.float32)
    into[:, 64] = 1.0
    return tuple(jnp.asarray(m, BF) for m in (spread, column, into, np.eye(256)))


def pack_kernel(idx_ref, *refs):
    whole, part = refs[:PART], refs[PART : 2 * PART]
    spread_ref, column_ref, out_ref = refs[2 * PART :]
    for g in range(PART):
        out_ref[g, 0:256, :] = whole[g][0, 0]
        block = part[g][0, 0]
        out_ref[g, 256:384, :] = (
            dot_nt(block[0:128], spread_ref[:, 0:128]) + dot_nt(block[128:256], spread_ref[:, 128:])
        ).astype(BF)
        line = dot_nt(column_ref[...], block)
        out_ref[g, 384:392, :] = jnp.concatenate(
            [line[0:1, 0:128], line[0:1, 128:256], jnp.zeros((6, 128), F32)], axis=0
        ).astype(BF)


def pack(idx, own):
    count = idx.shape[0]
    spread, column, _, _ = pack_constants()

    def chosen(g, j):
        return lambda k, s: (s[PART * k + g], j, 0, 0)

    return pl.pallas_call(
        pack_kernel,
        grid_spec=pltpu.PrefetchScalarGridSpec(
            num_scalar_prefetch=1,
            grid=(count // PART,),
            in_specs=[
                pl.BlockSpec((1, 1, 256, 128), chosen(g, j))
                for j in (FIRST, FIRST + 1)
                for g in range(PART)
            ]
            + [
                pl.BlockSpec((128, 256), lambda k, s: (0, 0)),
                pl.BlockSpec((8, 128), lambda k, s: (0, 0)),
            ],
            out_specs=pl.BlockSpec((PART, 256 + PACKED, 128), lambda k, s: (k, 0, 0)),
        ),
        out_shape=jax.ShapeDtypeStruct((count, 256 + PACKED, 128), BF),
        compiler_params=PARAMS,
        name="pack",
    )(idx, *[own] * (2 * PART), spread, column)


def block_edges(block, sel_ref, stat_ref):
    rows = dot(sel_ref[...], block).astype(BF)
    value = block.astype(F32)
    high, low = split2(value * value)
    stats = dot(stat_ref[0:8], block) + dot(stat_ref[8:16], high) + dot(stat_ref[8:16], low)
    return rows[0:64], rows[64:128], stats


def edge_kernel(slot_ref, *refs):
    blocks, (sel_ref, stat_ref, head_ref, tail_ref, stats_ref) = refs[:PART], refs[PART:]
    for g in range(PART):
        for j in range(stats_ref.shape[1]):
            head, tail, stats = block_edges(blocks[g][0, j], sel_ref, stat_ref)
            head_ref[g, j] = head
            tail_ref[g, j] = tail
            stats_ref[g, j] = stats


def unpack_kernel(slot_ref, *refs):
    packed, before = refs[:PART], refs[PART : 2 * PART]
    (
        spread_ref, into_ref, eye_ref, sel_ref, stat_ref, head_ref, tail_ref, stats_ref, block_ref,
    ) = refs[2 * PART :]
    for g in range(PART):
        wide = dot(packed[g][0, 256:384, :], spread_ref[...])
        line = packed[g][0, 384:392, :]
        line = jnp.concatenate([line[0:1], line[1:2]], axis=1)
        column = dot(eye_ref[...] * line, into_ref[...])
        block = jnp.concatenate([wide[:, :128], wide[:, 128:]], axis=0) + column
        blocks = (packed[g][0, 0:256, :], block.astype(BF))
        block_ref[g, 0] = before[g][0, 0]
        for j in range(2):
            block_ref[g, j + 1] = blocks[j]
            head, tail, stats = block_edges(blocks[j], sel_ref, stat_ref)
            head_ref[g, j] = head
            tail_ref[g, j] = tail
            stats_ref[g, j] = stats


def edge_outputs(images, blocks):
    specs = [
        pl.BlockSpec((PART, blocks, 64, 128), lambda k, s: (k, 0, 0, 0)),
        pl.BlockSpec((PART, blocks, 64, 128), lambda k, s: (k, 0, 0, 0)),
        pl.BlockSpec((PART, blocks, 8, 128), lambda k, s: (k, 0, 0, 0)),
    ]
    shapes = [
        jax.ShapeDtypeStruct((images, blocks, 64, 128), BF),
        jax.ShapeDtypeStruct((images, blocks, 64, 128), BF),
        jax.ShapeDtypeStruct((images, blocks, 8, 128), F32),
    ]
    return specs, shapes


def whole_spec(a):
    return pl.BlockSpec(a.shape, lambda k, s: (0,) * a.ndim)


def edges(slot, recv):
    images, blocks = slot.shape[0], recv.shape[1]
    constants = edge_constants()
    specs, shapes = edge_outputs(images, blocks)

    def by_slot(g):
        return lambda k, s: (s[PART * k + g], 0, 0, 0)

    return pl.pallas_call(
        edge_kernel,
        grid_spec=pltpu.PrefetchScalarGridSpec(
            num_scalar_prefetch=1,
            grid=(images // PART,),
            in_specs=[pl.BlockSpec((1, blocks, 256, 128), by_slot(g)) for g in range(PART)]
            + [whole_spec(a) for a in constants],
            out_specs=specs,
        ),
        out_shape=shapes,
        cost_estimate=pl.CostEstimate(
            flops=images * blocks * 20_000_000, bytes_accessed=images * blocks * 100_000,
            transcendentals=0,
        ),
        compiler_params=PARAMS,
        name="edges",
    )(slot, *[recv] * PART, *constants)


def unpack(slot, packed, main):
    images = slot.shape[0]
    spread, _, into, eye = pack_constants()
    constants = (spread, into, eye) + edge_constants()
    specs, shapes = edge_outputs(images, 2)

    def by_slot(g):
        return lambda k, s: (s[PART * k + g], 0, 0)

    def before(g):
        return lambda k, s: (s[PART * k + g], FIRST - 1, 0, 0)

    return pl.pallas_call(
        unpack_kernel,
        grid_spec=pltpu.PrefetchScalarGridSpec(
            num_scalar_prefetch=1,
            grid=(images // PART,),
            in_specs=[pl.BlockSpec((1, 256 + PACKED, 128), by_slot(g)) for g in range(PART)]
            + [pl.BlockSpec((1, 1, 256, 128), before(g)) for g in range(PART)]
            + [whole_spec(a) for a in constants],
            out_specs=specs + [pl.BlockSpec((PART, 3, 256, 128), lambda k, s: (k, 0, 0, 0))],
        ),
        out_shape=shapes + [jax.ShapeDtypeStruct((images, 3, 256, 128), BF)],
        compiler_params=PARAMS,
        name="unpack",
    )(slot, *[packed] * PART, *[main] * PART, *constants)


def prepare_kernel(
    own_ref, up_ref, down_ref, stat_ref, index_ref, rev_ref, flip_ref, own_out, edge_out, table_out
):
    mean_inv = 24.0 * LOG2E
    for n in range(STEPS):
        block = jnp.concatenate([own_ref[0, n], own_ref[0, n + 1]], axis=1)
        up = jnp.concatenate([up_ref[0, n], up_ref[0, n + 1]], axis=1)
        down = jnp.concatenate([down_ref[0, n], down_ref[0, n + 1]], axis=1)
        own_out[0, n] = dot_nt(rev_ref[...], block).astype(BF)
        edge_out[0, n] = dot_nt(rev_ref[...], jnp.concatenate([up, down], axis=0)).astype(BF)
        stats = jnp.concatenate([stat_ref[0, n], stat_ref[0, n + 1]], axis=1)
        mean, inv = boxed_stats(stats, up, down)
        scaled = inv * mean_inv
        both = jnp.concatenate([scaled * (1.0 / 576.0), scaled * mean], axis=0)[:, :128]
        high = both.astype(BF).astype(F32)
        mid = (both - high).astype(BF).astype(F32)
        index = index_ref[0, :, 128 * n : 128 * n + 128].astype(F32)
        rows = jnp.concatenate(
            [high, mid, both - high - mid, index, jnp.zeros((4, 128), F32)], axis=0
        ).astype(BF)
        blank = jnp.zeros((64, 64), F32)
        left = dot_nt(flip_ref[0:64, :], rows)
        right = dot_nt(flip_ref[64:128, :], rows)
        table_out[0, n] = jnp.concatenate([left, right, blank], axis=1).astype(BF)


def prepare(own, up, down, stats, depth_index):
    images, blocks = own.shape[0], own.shape[1]
    return pl.pallas_call(
        prepare_kernel,
        grid=(images,),
        in_specs=[
            pl.BlockSpec((1, blocks, 256, 128), lambda k: (k, 0, 0, 0)),
            pl.BlockSpec((1, blocks, 64, 128), lambda k: (k, 0, 0, 0)),
            pl.BlockSpec((1, blocks, 64, 128), lambda k: (k, 0, 0, 0)),
            pl.BlockSpec((1, blocks, 8, 128), lambda k: (k, 0, 0, 0)),
            pl.BlockSpec((1, 4, 512), lambda k: (k, 0, 0)),
            pl.BlockSpec((WIN, 256), lambda k: (0, 0)),
            pl.BlockSpec((128, 128), lambda k: (0, 0)),
        ],
        out_specs=[
            pl.BlockSpec((1, STEPS, WIN, 256), lambda k: (k, 0, 0, 0)),
            pl.BlockSpec((1, STEPS, WIN, 128), lambda k: (k, 0, 0, 0)),
            pl.BlockSpec((1, STEPS, 64, 128), lambda k: (k, 0, 0, 0)),
        ],
        out_shape=[
            jax.ShapeDtypeStruct((images, STEPS, WIN, 256), BF),
            jax.ShapeDtypeStruct((images, STEPS, WIN, 128), BF),
            jax.ShapeDtypeStruct((images, STEPS, 64, 128), BF),
        ],
        cost_estimate=pl.CostEstimate(
            flops=images * STEPS * 40_000_000, bytes_accessed=images * 1_000_000, transcendentals=0
        ),
        compiler_params=PARAMS,
        name="prepare",
    )(own, up, down, stats, depth_index, reversal(), flips())


def skewed(left, right, column, lane, shift):
    return pltpu.roll(jnp.where(lane < column, right, left), shift, 1, stride=1, stride_axis=0)


def sweep_kernel(group, ys, halo, late, *refs):
    refs = list(refs[1:])

    def take(count):
        out = refs[:count]
        del refs[:count]
        return out

    count = len(ys)
    near_refs, far_refs = take(group), take(group)
    own_ref, table_ref, pat_ref, mask_ref, w2_ref, flip_ref, elev_ref, cell_ref = take(8)

    def pair(g):
        if late:
            early, before, after = ref_sets[0]
            first = jnp.where(pl.program_id(0) == 0, early[g, 0].astype(F32), before[g, 0].astype(F32))
            return jnp.concatenate([first.astype(early.dtype), after[g, 0]], axis=1)
        before, after = ref_sets[0]
        return jnp.concatenate([before[g, 0], after[g, 0]], axis=1)

    width = 3 if late else 2
    stat_refs = take(width)
    up_refs = take(width) if halo else None
    down_refs = take(width) if halo else None
    edge_ref = take(1)[0] if halo else None
    mean_ref, rows_ref, skew = refs

    def joined(set_refs, g):
        ref_sets[0] = set_refs
        return pair(g)

    ref_sets = [None]
    column = 63 - lax.broadcasted_iota(jnp.int32, (64, 128), 0)
    lane = lax.broadcasted_iota(jnp.int32, (64, 128), 1)
    wrapped = lane < column
    first = lane < column + 64
    column8 = 7 - lax.broadcasted_iota(jnp.int32, (8, 128), 0)
    lane8 = lax.broadcasted_iota(jnp.int32, (8, 128), 1)
    hyp = (lane % 64).astype(F32)
    tables = dot(table_ref[:, 0].reshape(group * 64, 128), pat_ref[...])

    soft = []
    chosen = []
    for g in range(group):
        rhs = jnp.concatenate([near_refs[g][0, 0], far_refs[g][0, 0]], axis=1)
        stats = joined(stat_refs, g)
        if halo:
            up = joined(up_refs, g)
            down = joined(down_refs, g)
            above = dot(edge_ref[g, 0][:, 0:64], up)
            below = dot(edge_ref[g, 0][:, 64:128], down)
        else:
            up = down = None
        mean_b, inv_b = boxed_stats(stats, up, down)
        own = own_ref[g, 0]
        masked = jnp.concatenate([own * mask_ref[y : y + 1, :] for y in ys], axis=0)
        product = dot(masked, rhs)
        for i, y in enumerate(ys):
            p = product[WIN * i : WIN * i + WIN]
            if y == 0:
                p = p + above
            if y == 3:
                p = p + below
            z = jnp.where(
                wrapped, p[16:80, 128:], jnp.where(first, p[80:144, :128], p[16:80, :128])
            )
            z8 = jnp.where(
                lane8 < column8,
                p[72:80, 128:],
                jnp.where(lane8 < column8 + 64, p[8:16, 128:], p[72:80, :128]),
            )
            at = count * g + i
            skew[at, 0:8, :] = pltpu.roll(z8, 57, 1, stride=1, stride_axis=0)
            skew[at, 8:72, :] = pltpu.roll(z, 65, 1, stride=1, stride_axis=0)
            cross = skew[at, 8:72, :] + skew[at, 7:71, :] + skew[at, 6:70, :]
            mb = skewed(mean_b[y : y + 1, :128], mean_b[y : y + 1, 128:], column, lane, 65)
            rb = skewed(inv_b[y : y + 1, :128], inv_b[y : y + 1, 128:], column, lane, 65)
            a1, a2, index = (
                tables[64 * g : 64 * g + 64, (3 * i + q) * 128 : (3 * i + q + 1) * 128]
                for q in range(3)
            )
            weight = jnp.exp2((cross * a1 - a2 * mb) * rb)
            picked = jnp.where(index == hyp, weight, 0.0)
            soft.append(jnp.concatenate(split2(weight), axis=1))
            chosen.append(jnp.concatenate(split2(picked), axis=1))
    soft = jnp.concatenate(soft, axis=0)
    chosen = jnp.concatenate(chosen, axis=0)
    r = dot_nt(w2_ref[...], soft)
    rc = dot_nt(w2_ref[...], chosen)
    inv = 1.0 / r[0:2]
    both = jnp.concatenate([(r[2:4] + r[4:6] + r[6:8]) * inv, rc[0:2] * inv], axis=0)
    pieces = group * count // 2
    both = jnp.concatenate([both[:, 128 * v : 128 * v + 128] for v in range(pieces)], axis=0)
    high = both.astype(BF)
    rest = both - high.astype(F32)
    mid = rest.astype(BF)
    low = (rest - mid.astype(F32)).astype(BF)
    both = dot(jnp.concatenate([high, mid, low], axis=0), flip_ref[...])
    both = both[0 : 4 * pieces] + both[4 * pieces : 8 * pieces] + both[8 * pieces :]
    turned = pltpu.roll(both, 64, 1)
    left = lax.broadcasted_iota(jnp.int32, (1, 128), 1) < 64
    cell_iota = lax.broadcasted_iota(jnp.int32, (128, 128), 0)
    for g in range(group):
        for i, y in enumerate(ys):
            at = (count * g + i) // 2 * 4
            lo, hi = (both, turned) if i % 2 == 0 else (turned, both)
            mean_ref[g, i : i + 1, :] = jnp.where(left, lo[at : at + 1], hi[at + 1 : at + 2])
            c = jnp.where(left, lo[at + 2 : at + 3], hi[at + 3 : at + 4])
            values = jnp.concatenate([c * elev_ref[g, y : y + 1, :], c], axis=0)
            value_hi = values.astype(BF).astype(F32)
            values = jnp.concatenate([value_hi, values - value_hi, jnp.zeros((4, 128), F32)], axis=0)
            hot = jnp.where(cell_iota == cell_ref[g, y : y + 1, :], 1.0, 0.0).astype(BF)
            binned = dot_nt(values.astype(BF), hot)
            got = binned[0:2] + binned[2:4]
            at = count * g + i
            rows_ref[0, at : at + 1, 0:128] = got[0:1]
            rows_ref[0, at : at + 1, 128:256] = got[1:2]


def sweep_steps(
    first, steps, ys, group, slot, blocks, stats, ups, downs, own, edge, table, w2, elev, cell, late
):
    images = own.shape[0]
    halo = ups is not None
    count = len(ys)

    def slot_block(g, j):
        return lambda n, k, s: (s[group * k + g], n + first + j, 0, 0)

    def compact_block(g, j):
        return lambda n, k, s: (group * k + g, n + j, 0, 0)

    block_at = compact_block if late else slot_block

    def near(n, k, s):
        return (k, n + first, 0, 0)

    def whole(n, k, s):
        return (0, 0)

    def pixels(n, k, s):
        return (k, 0, n + first)

    def pair_specs(rows):
        if late:
            maps = (
                lambda n, k, s: (k, FIRST - 1, 0, 0),
                lambda n, k, s: (k, 0, 0, 0),
                lambda n, k, s: (k, n, 0, 0),
            )
        else:
            maps = (near, lambda n, k, s: (k, n + first + 1, 0, 0))
        return [pl.BlockSpec((group, 1, rows, 128), m) for m in maps]

    def pair_args(arrays):
        return [arrays[0], arrays[1], arrays[1]] if late else [arrays[0], arrays[0]]

    in_specs = [pl.BlockSpec((1, 1, 256, 128), block_at(g, j)) for j in range(2) for g in range(group)]
    in_specs += [
        pl.BlockSpec((group, 1, WIN, 256), near),
        pl.BlockSpec((group, 1, 64, 128), near),
        pl.BlockSpec((128, 3 * 128 * count), whole),
        pl.BlockSpec((16, 256), whole),
        pl.BlockSpec((8, 256), whole),
        pl.BlockSpec((128, 128), whole),
        pl.BlockSpec((group, 4, 128), pixels),
        pl.BlockSpec((group, 4, 128), pixels),
    ] + pair_specs(8)
    args = [blocks] * (2 * group) + [
        own, table, table_patterns(ys), row_masks(), w2, flips(), elev, cell,
    ] + pair_args(stats)
    if halo:
        in_specs += pair_specs(64) + pair_specs(64) + [pl.BlockSpec((group, 1, WIN, 128), near)]
        args += pair_args(ups) + pair_args(downs) + [edge]
    work = steps * images * count // 4
    return pl.pallas_call(
        functools.partial(sweep_kernel, group, ys, halo, late),
        grid_spec=pltpu.PrefetchScalarGridSpec(
            num_scalar_prefetch=1,
            grid=(steps, images // group),
            in_specs=in_specs,
            out_specs=[
                pl.BlockSpec((group, count, 128), lambda n, k, s: (k, 0, n)),
                pl.BlockSpec((1, count * group, 256), lambda n, k, s: (n, k, 0)),
            ],
            scratch_shapes=[pltpu.VMEM((count * group, 72, 128), F32)],
        ),
        out_shape=[
            jax.ShapeDtypeStruct((images, count, steps * 128), F32),
            jax.ShapeDtypeStruct((steps, images * count, 256), F32),
        ],
        compiler_params=PARAMS,
        cost_estimate=pl.CostEstimate(
            flops=work * 200_000_000, bytes_accessed=work * 400_000, transcendentals=0
        ),
        name="sweep",
    )(slot, *args)


def depth_weights(planes):
    high = lax.reduce_precision(planes, 8, 7)
    mid = lax.reduce_precision(planes - high, 8, 7)
    zero = jnp.zeros_like(planes)
    rows = []
    for v in (jnp.ones_like(planes), high, mid, planes - high - mid):
        rows.append(jnp.concatenate([v, zero]))
        rows.append(jnp.concatenate([zero, v]))
    w = jnp.stack(rows)
    return jnp.concatenate([w, w], axis=1).astype(BF)


def collect_kernel(list_ref, count_ref, a_ref, b_ref, c_ref, out_ref, rows):
    at = 0
    for part in (a_ref, b_ref, c_ref):
        for n in range(part.shape[0]):
            rows[at : at + part.shape[1], :] = part[n]
            at += part.shape[1]
    for o in range(out_ref.shape[0]):

        def move(step, carry):
            for i in range(8):
                e = step * 8 + i
                out_ref[o, pl.ds(e, 1), :] = rows[pl.ds(list_ref[o, e], 1), :]
            return carry

        lax.fori_loop(0, (count_ref[o] + 7) // 8, move, 0)


def collect(row_list, counts, parts):
    owners, cap = row_list.shape
    total = sum(p.shape[0] * p.shape[1] for p in parts)
    return pl.pallas_call(
        collect_kernel,
        grid_spec=pltpu.PrefetchScalarGridSpec(
            num_scalar_prefetch=2,
            grid=(1,),
            in_specs=[pl.BlockSpec(p.shape, lambda i, a, b: (0, 0, 0)) for p in parts],
            out_specs=pl.BlockSpec((owners, cap, 2 * CELLS), lambda i, a, b: (0, 0, 0)),
            scratch_shapes=[pltpu.VMEM((total, 2 * CELLS), F32)],
        ),
        out_shape=jax.ShapeDtypeStruct((owners, cap, 2 * CELLS), F32),
        compiler_params=PARAMS,
        name="collect",
    )(row_list, counts, *parts)


def place_kernel(slot_ref, count_ref, got_ref, out_ref):
    out_ref[...] = jnp.zeros_like(out_ref)
    for t in range(got_ref.shape[0]):
        count = count_ref[t]

        def add(step, carry):
            for i in range(8):
                e = step * 8 + i
                at = pl.ds(slot_ref[t, e], 1)
                row = jnp.where(e < count, got_ref[t, pl.ds(e, 1), :], 0.0)
                out_ref[at, :] = out_ref[at, :] + row
            return carry

        lax.fori_loop(0, (count + 7) // 8, add, 0)


def place(slots, counts, got, total):
    return pl.pallas_call(
        place_kernel,
        grid_spec=pltpu.PrefetchScalarGridSpec(
            num_scalar_prefetch=2,
            grid=(1,),
            in_specs=[pl.BlockSpec(got.shape, lambda i, a, b: (0, 0, 0))],
            out_specs=pl.BlockSpec((total, 2 * CELLS), lambda i, a, b: (0, 0)),
        ),
        out_shape=jax.ShapeDtypeStruct((total, 2 * CELLS), F32),
        compiler_params=PARAMS,
        name="place",
    )(slots, counts, got)


def neighbour_rows(head, tail):
    count = lax.axis_size("tile")
    above = lax.ppermute(tail, "tile", [(i, i + 1) for i in range(count - 1)])
    below = lax.ppermute(head, "tile", [(i + 1, i) for i in range(count - 1)])
    return above, below


def on_device(
    features, partner_ids, depth_planes, cam_height, ray_down, depth_index, cell_index,
    block_list, block_slot, block_count,
):
    group_count = lax.axis_size("img")
    owners = lax.axis_size("tile")
    my_group = lax.axis_index("img")
    my_tile = lax.axis_index("tile")
    images = features.shape[0]
    table = partner_ids.reshape(group_count, images)
    source_of = table // images
    chosen = jnp.sum(jnp.where(source_of == my_group, table % images, 0), axis=1)
    slot = lax.dynamic_index_in_dim(source_of, my_group, 0, False)

    def exchange(a):
        return lax.all_to_all(a, "img", split_axis=0, concat_axis=0, tiled=True)

    main = exchange(pick(chosen, features, FIRST))

    every = jnp.arange(images, dtype=jnp.int32)
    own = pick(every, features, STEPS + 1)
    own_head, own_tail, own_stats = edges(every, own)
    own_up, own_down = neighbour_rows(own_head, own_tail)
    own_turned, edge_turned, own_table = prepare(own, own_up, own_down, own_stats, depth_index)
    packed = pack(chosen, own)

    hyp = jnp.arange(NDEPTH, dtype=jnp.int32)[:, None, None, None]
    plane_at = jnp.sum(
        jnp.where(hyp == depth_index[None], depth_planes[:, None, None, None], 0.0), 0
    )
    elevation = cam_height[:, None, None] - ray_down * plane_at

    meta = jnp.concatenate(
        [block_slot[0, 0], jnp.broadcast_to(block_count[0, 0][:, None], (owners, 128))], axis=1
    )
    metas = [lax.dynamic_slice_in_dim(meta, my_tile, 1, 0)]
    for s in range(1, owners):
        mine = lax.dynamic_slice_in_dim(meta, (my_tile + s) % owners, 1, 0)
        metas.append(lax.ppermute(mine, "tile", [(i, (i + s) % owners) for i in range(owners)]))
    metas = jnp.concatenate(metas, axis=0)
    metas = jnp.take(metas, (my_tile - jnp.arange(owners)) % owners, axis=0)

    w2 = depth_weights(depth_planes)

    packed, own_turned, edge_turned, own_table, elevation, metas, w2 = lax.optimization_barrier(
        (packed, own_turned, edge_turned, own_table, elevation, metas, w2)
    )
    last = exchange(packed)
    head, tail, stats = edges(slot, main)
    up, down = neighbour_rows(head, tail)
    shared = (own_turned, edge_turned, own_table, w2, elevation, cell_index)
    mean_a, rows_a = sweep_steps(
        0, 2, (0, 1, 2, 3), 8, slot, main, (stats,), (up,), (down,), *shared, False
    )
    last, mean_a = lax.optimization_barrier((last, mean_a))
    head_l, tail_l, stats_l, late = unpack(slot, last, main)
    up_l, down_l = neighbour_rows(head_l, tail_l)
    both = (stats, stats_l)
    mean_b, rows_b = sweep_steps(2, 2, (1, 2), 8, slot, late, both, None, None, *shared, True)
    mean_c, rows_c = sweep_steps(
        2, 2, (0, 3), 8, slot, late, both, (up, up_l), (down, down_l), *shared, True
    )
    mean_bc = jnp.concatenate([mean_c[:, 0:1], mean_b, mean_c[:, 1:2]], axis=1)
    mean_range = jnp.concatenate([mean_a, mean_bc], axis=2)

    lists = block_list[0, 0]
    n, r, k = lists % STEPS, lists // STEPS % 4, lists // (4 * STEPS)
    half = (n - 2) * 2 * images + 2 * k
    row_list = jnp.where(
        n < 2,
        n * 4 * images + 4 * k + r,
        jnp.where((r == 1) | (r == 2), 8 * images + half + r - 1, 12 * images + half + r // 3),
    )
    send = collect(row_list, block_count[0, 0], (rows_a, rows_b, rows_c))
    got = lax.all_to_all(send, "tile", split_axis=0, concat_axis=0, tiled=True)
    dense = place(metas[:, :128], metas[:, 128], got, group_count * PATCH_DEV)
    parts = exchange(dense.reshape(group_count, PATCH_DEV, 2 * CELLS))
    total = jnp.sum(parts, axis=0)
    return mean_range, total[:, :CELLS] / (total[:, CELLS:] + 1.0)


def solution(mesh):
    return jax.shard_map(
        on_device,
        mesh=mesh,
        in_specs=(
            P("img", None, "tile", None),
            P(),
            P(),
            P("img"),
            P("img", "tile", None),
            P("img", "tile", None),
            P("img", "tile", None),
            P("img", "tile", None, None),
            P("img", "tile", None, None),
            P("img", "tile", None),
        ),
        out_specs=(P("img", "tile", None), P(("img", "tile"), None)),
        check_vma=False,
    )
```

```python
import functools
import math

import numpy as np
import jax
import jax.numpy as jnp
from jax import lax
from jax.experimental import pallas as pl
from jax.experimental.pallas import tpu as pltpu
from jax.sharding import PartitionSpec as P

NDEPTH = 64
CELLS = 128
PATCH_DEV = 16
STEPS = 4
WIN = 144
LOG2E = math.log2(math.e)
BF = jnp.bfloat16
F32 = jnp.float32
NT = (((1,), (1,)), ((), ()))
PARAMS = pltpu.CompilerParams(vmem_limit_bytes=60 * 1024 * 1024)


def dot(a, b):
    return jnp.dot(a, b, preferred_element_type=F32)


def dot_nt(a, b):
    return lax.dot_general(a, b, NT, preferred_element_type=F32)


def table_patterns(ys):
    pat = np.zeros((128, 3 * len(ys), 128), np.float32)
    for half in range(2):
        lanes = slice(64 * half, 64 * half + 64)
        for i, y in enumerate(ys):
            for q in range(2):
                for s in range(3):
                    pat[half * 32 + s * 8 + q * 4 + y, i * 3 + q, lanes] = 1.0
            pat[half * 32 + 24 + y, i * 3 + 2, lanes] = 1.0
    return jnp.asarray(pat.reshape(128, -1), BF)


def row_masks():
    y = np.arange(16)[:, None]
    k = np.arange(256)[None, :] % 4
    return jnp.asarray((np.abs(k - y) <= 1) & (y < 4), BF)


def flips():
    m = np.zeros((128, 128), np.float32)
    for i in range(128):
        m[i, i // 64 * 64 + 63 - i % 64] = 1.0
    return jnp.asarray(m, BF)


def reversal():
    m = np.zeros((WIN, 256), np.float32)
    for i in range(WIN):
        m[i, WIN - 1 - i] = 1.0
    return jnp.asarray(m, BF)


def edge_constants():
    sel = np.zeros((128, 256), np.float32)
    for c in range(64):
        sel[c, 4 * c] = 1.0
        sel[64 + c, 4 * c + 3] = 1.0
    stat = np.zeros((16, 256), np.float32)
    for y in range(4):
        stat[y, y::4] = 1.0
        stat[12 + y, y::4] = 1.0
    return jnp.asarray(sel, BF), jnp.asarray(stat, BF)


def split2(a):
    high = a.astype(BF)
    return high, (a - high.astype(F32)).astype(BF)


def boxed_stats(stats, up, down):
    blank = jnp.zeros((1, 256), F32)
    sums = [blank] + [stats[y : y + 1] for y in range(4)] + [blank]
    sqs = [blank] + [stats[4 + y : 5 + y] for y in range(4)] + [blank]
    if up is not None:
        for at, halo in ((0, up.astype(F32)), (5, down.astype(F32))):
            sums[at] = jnp.sum(halo, 0, keepdims=True)
            sqs[at] = jnp.sum(halo * halo, 0, keepdims=True)
    tall = jnp.concatenate(
        [v[y] + v[y + 1] + v[y + 2] for v in (sums, sqs) for y in range(4)], axis=0
    )
    boxed = (tall + pltpu.roll(tall, 255, 1) + pltpu.roll(tall, 254, 1)) * (1.0 / 576.0)
    mean = boxed[0:4]
    return mean, lax.rsqrt(boxed[4:8] - mean * mean + 1e-5)


PART = 8
PACKED = 136
FIRST = 3


def pick(idx, features, blocks):
    count = idx.shape[0]
    images, channels, rows, _ = features.shape

    def kernel(idx_ref, features_ref, out_ref, strips, in_sem, out_sem):
        def read(k):
            return pltpu.make_async_copy(
                features_ref.at[k, :, :, pl.ds(0, 128 * blocks)], strips.at[k], in_sem.at[k]
            )

        def write(s, j):
            return pltpu.make_async_copy(
                strips.at[idx_ref[s], :, :, pl.ds(128 * j, 128)], out_ref.at[s, j], out_sem.at[s, j]
            )

        for k in range(images):
            read(k).start()
        for k in range(images):
            read(k).wait()
        for s in range(count):
            for j in range(blocks):
                write(s, j).start()
        for s in range(count):
            for j in range(blocks):
                write(s, j).wait()

    out = pl.pallas_call(
        kernel,
        grid_spec=pltpu.PrefetchScalarGridSpec(
            num_scalar_prefetch=1,
            grid=(1,),
            in_specs=[pl.BlockSpec(memory_space=pl.ANY)],
            out_specs=pl.BlockSpec(memory_space=pl.ANY),
            scratch_shapes=[
                pltpu.VMEM((images, channels, rows, 128 * blocks), BF),
                pltpu.SemaphoreType.DMA((images,)),
                pltpu.SemaphoreType.DMA((count, blocks)),
            ],
        ),
        out_shape=jax.ShapeDtypeStruct((count, blocks, channels, rows, 128), BF),
        compiler_params=PARAMS,
        cost_estimate=pl.CostEstimate(
            flops=0, bytes_accessed=count * blocks * 131072, transcendentals=0
        ),
        name="pick",
    )(idx, features)
    return out.reshape(count, blocks, channels * rows, 128)


def pack_constants():
    spread = np.zeros((128, 256), np.float32)
    for i in range(64):
        spread[i, i] = 1.0
        spread[64 + i, 128 + i] = 1.0
    column = np.zeros((8, 128), np.float32)
    column[0, 64] = 1.0
    into = np.zeros((256, 128), np.float32)
    into[:, 64] = 1.0
    return tuple(jnp.asarray(m, BF) for m in (spread, column, into, np.eye(256)))


def pack_kernel(idx_ref, *refs):
    whole, part = refs[:PART], refs[PART : 2 * PART]
    spread_ref, column_ref, out_ref = refs[2 * PART :]
    for g in range(PART):
        out_ref[g, 0:256, :] = whole[g][0, 0]
        block = part[g][0, 0]
        out_ref[g, 256:384, :] = (
            dot_nt(block[0:128], spread_ref[:, 0:128]) + dot_nt(block[128:256], spread_ref[:, 128:])
        ).astype(BF)
        line = dot_nt(column_ref[...], block)
        out_ref[g, 384:392, :] = jnp.concatenate(
            [line[0:1, 0:128], line[0:1, 128:256], jnp.zeros((6, 128), F32)], axis=0
        ).astype(BF)


def pack(idx, own):
    count = idx.shape[0]
    spread, column, _, _ = pack_constants()

    def chosen(g, j):
        return lambda k, s: (s[PART * k + g], j, 0, 0)

    return pl.pallas_call(
        pack_kernel,
        grid_spec=pltpu.PrefetchScalarGridSpec(
            num_scalar_prefetch=1,
            grid=(count // PART,),
            in_specs=[
                pl.BlockSpec((1, 1, 256, 128), chosen(g, j))
                for j in (FIRST, FIRST + 1)
                for g in range(PART)
            ]
            + [
                pl.BlockSpec((128, 256), lambda k, s: (0, 0)),
                pl.BlockSpec((8, 128), lambda k, s: (0, 0)),
            ],
            out_specs=pl.BlockSpec((PART, 256 + PACKED, 128), lambda k, s: (k, 0, 0)),
        ),
        out_shape=jax.ShapeDtypeStruct((count, 256 + PACKED, 128), BF),
        compiler_params=PARAMS,
        name="pack",
    )(idx, *[own] * (2 * PART), spread, column)


def block_edges(block, sel_ref, stat_ref):
    rows = dot(sel_ref[...], block).astype(BF)
    value = block.astype(F32)
    high, low = split2(value * value)
    stats = dot(stat_ref[0:8], block) + dot(stat_ref[8:16], high) + dot(stat_ref[8:16], low)
    return rows[0:64], rows[64:128], stats


def edge_kernel(slot_ref, *refs):
    blocks, (sel_ref, stat_ref, head_ref, tail_ref, stats_ref, *kept) = refs[:PART], refs[PART:]
    for g in range(PART):
        if kept:
            kept[0][g, 0] = blocks[g][0, blocks[g].shape[1] - 1]
        for j in range(stats_ref.shape[1]):
            head, tail, stats = block_edges(blocks[g][0, j], sel_ref, stat_ref)
            head_ref[g, j] = head
            tail_ref[g, j] = tail
            stats_ref[g, j] = stats


def unpack_kernel(slot_ref, *refs):
    packed = refs[:PART]
    (
        spread_ref, into_ref, eye_ref, sel_ref, stat_ref, head_ref, tail_ref, stats_ref, block_ref,
    ) = refs[PART:]
    for g in range(PART):
        wide = dot(packed[g][0, 256:384, :], spread_ref[...])
        line = packed[g][0, 384:392, :]
        line = jnp.concatenate([line[0:1], line[1:2]], axis=1)
        column = dot(eye_ref[...] * line, into_ref[...])
        block = jnp.concatenate([wide[:, :128], wide[:, 128:]], axis=0) + column
        blocks = (packed[g][0, 0:256, :], block.astype(BF))
        for j in range(2):
            block_ref[g, j] = blocks[j]
            head, tail, stats = block_edges(blocks[j], sel_ref, stat_ref)
            head_ref[g, j] = head
            tail_ref[g, j] = tail
            stats_ref[g, j] = stats


def edge_outputs(images, blocks):
    specs = [
        pl.BlockSpec((PART, blocks, 64, 128), lambda k, s: (k, 0, 0, 0)),
        pl.BlockSpec((PART, blocks, 64, 128), lambda k, s: (k, 0, 0, 0)),
        pl.BlockSpec((PART, blocks, 8, 128), lambda k, s: (k, 0, 0, 0)),
    ]
    shapes = [
        jax.ShapeDtypeStruct((images, blocks, 64, 128), BF),
        jax.ShapeDtypeStruct((images, blocks, 64, 128), BF),
        jax.ShapeDtypeStruct((images, blocks, 8, 128), F32),
    ]
    return specs, shapes


def whole_spec(a):
    return pl.BlockSpec(a.shape, lambda k, s: (0,) * a.ndim)


def edges(slot, recv, keep_last):
    images, blocks = slot.shape[0], recv.shape[1]
    constants = edge_constants()
    specs, shapes = edge_outputs(images, blocks)
    if keep_last:
        specs = specs + [pl.BlockSpec((PART, 1, 256, 128), lambda k, s: (k, 0, 0, 0))]
        shapes = shapes + [jax.ShapeDtypeStruct((images, 1, 256, 128), BF)]

    def by_slot(g):
        return lambda k, s: (s[PART * k + g], 0, 0, 0)

    return pl.pallas_call(
        edge_kernel,
        grid_spec=pltpu.PrefetchScalarGridSpec(
            num_scalar_prefetch=1,
            grid=(images // PART,),
            in_specs=[pl.BlockSpec((1, blocks, 256, 128), by_slot(g)) for g in range(PART)]
            + [whole_spec(a) for a in constants],
            out_specs=specs,
        ),
        out_shape=shapes,
        cost_estimate=pl.CostEstimate(
            flops=images * blocks * 20_000_000, bytes_accessed=images * blocks * 100_000,
            transcendentals=0,
        ),
        compiler_params=PARAMS,
        name="edges",
    )(slot, *[recv] * PART, *constants)


def unpack(slot, packed):
    images = slot.shape[0]
    spread, _, into, eye = pack_constants()
    constants = (spread, into, eye) + edge_constants()
    specs, shapes = edge_outputs(images, 2)

    def by_slot(g):
        return lambda k, s: (s[PART * k + g], 0, 0)

    return pl.pallas_call(
        unpack_kernel,
        grid_spec=pltpu.PrefetchScalarGridSpec(
            num_scalar_prefetch=1,
            grid=(images // PART,),
            in_specs=[pl.BlockSpec((1, 256 + PACKED, 128), by_slot(g)) for g in range(PART)]
            + [whole_spec(a) for a in constants],
            out_specs=specs + [pl.BlockSpec((PART, 2, 256, 128), lambda k, s: (k, 0, 0, 0))],
        ),
        out_shape=shapes + [jax.ShapeDtypeStruct((images, 2, 256, 128), BF)],
        compiler_params=PARAMS,
        name="unpack",
    )(slot, *[packed] * PART, *constants)


def prepare_kernel(
    own_ref, up_ref, down_ref, stat_ref, index_ref, rev_ref, flip_ref, own_out, edge_out, table_out
):
    mean_inv = 24.0 * LOG2E
    for n in range(STEPS):
        block = jnp.concatenate([own_ref[0, n], own_ref[0, n + 1]], axis=1)
        up = jnp.concatenate([up_ref[0, n], up_ref[0, n + 1]], axis=1)
        down = jnp.concatenate([down_ref[0, n], down_ref[0, n + 1]], axis=1)
        own_out[0, n] = dot_nt(rev_ref[...], block).astype(BF)
        edge_out[0, n] = dot_nt(rev_ref[...], jnp.concatenate([up, down], axis=0)).astype(BF)
        stats = jnp.concatenate([stat_ref[0, n], stat_ref[0, n + 1]], axis=1)
        mean, inv = boxed_stats(stats, up, down)
        scaled = inv * mean_inv
        both = jnp.concatenate([scaled * (1.0 / 576.0), scaled * mean], axis=0)[:, :128]
        high = both.astype(BF).astype(F32)
        mid = (both - high).astype(BF).astype(F32)
        index = index_ref[0, :, 128 * n : 128 * n + 128].astype(F32)
        rows = jnp.concatenate(
            [high, mid, both - high - mid, index, jnp.zeros((4, 128), F32)], axis=0
        ).astype(BF)
        blank = jnp.zeros((64, 64), F32)
        left = dot_nt(flip_ref[0:64, :], rows)
        right = dot_nt(flip_ref[64:128, :], rows)
        table_out[0, n] = jnp.concatenate([left, right, blank], axis=1).astype(BF)


def prepare(own, up, down, stats, depth_index):
    images, blocks = own.shape[0], own.shape[1]
    return pl.pallas_call(
        prepare_kernel,
        grid=(images,),
        in_specs=[
            pl.BlockSpec((1, blocks, 256, 128), lambda k: (k, 0, 0, 0)),
            pl.BlockSpec((1, blocks, 64, 128), lambda k: (k, 0, 0, 0)),
            pl.BlockSpec((1, blocks, 64, 128), lambda k: (k, 0, 0, 0)),
            pl.BlockSpec((1, blocks, 8, 128), lambda k: (k, 0, 0, 0)),
            pl.BlockSpec((1, 4, 512), lambda k: (k, 0, 0)),
            pl.BlockSpec((WIN, 256), lambda k: (0, 0)),
            pl.BlockSpec((128, 128), lambda k: (0, 0)),
        ],
        out_specs=[
            pl.BlockSpec((1, STEPS, WIN, 256), lambda k: (k, 0, 0, 0)),
            pl.BlockSpec((1, STEPS, WIN, 128), lambda k: (k, 0, 0, 0)),
            pl.BlockSpec((1, STEPS, 64, 128), lambda k: (k, 0, 0, 0)),
        ],
        out_shape=[
            jax.ShapeDtypeStruct((images, STEPS, WIN, 256), BF),
            jax.ShapeDtypeStruct((images, STEPS, WIN, 128), BF),
            jax.ShapeDtypeStruct((images, STEPS, 64, 128), BF),
        ],
        cost_estimate=pl.CostEstimate(
            flops=images * STEPS * 40_000_000, bytes_accessed=images * 1_000_000, transcendentals=0
        ),
        compiler_params=PARAMS,
        name="prepare",
    )(own, up, down, stats, depth_index, reversal(), flips())


def skewed(left, right, column, lane, shift):
    return pltpu.roll(jnp.where(lane < column, right, left), shift, 1, stride=1, stride_axis=0)


def sweep_kernel(group, ys, halo, late, *refs):
    refs = list(refs[1:])

    def take(count):
        out = refs[:count]
        del refs[:count]
        return out

    count = len(ys)
    block_refs = take(3) if late else (take(group), take(group))
    own_ref, table_ref, pat_ref, mask_ref, w2_ref, flip_ref, elev_ref, cell_ref = take(8)

    def joined(three, g):
        if late:
            early, before, after = three
            near = jnp.where(pl.program_id(0) == 0, early[g, 0], before[g, 0])
        else:
            near, after = three[0][g, 0], three[1]
        return jnp.concatenate([near, after[g, 0]], axis=1)

    width = 3 if late else 2
    stat_refs = take(width)
    up_refs = take(width) if halo else None
    down_refs = take(width) if halo else None
    edge_ref = take(1)[0] if halo else None
    mean_ref, rows_ref, skew = refs

    column = 63 - lax.broadcasted_iota(jnp.int32, (64, 128), 0)
    lane = lax.broadcasted_iota(jnp.int32, (64, 128), 1)
    wrapped = lane < column
    first = lane < column + 64
    column8 = 7 - lax.broadcasted_iota(jnp.int32, (8, 128), 0)
    lane8 = lax.broadcasted_iota(jnp.int32, (8, 128), 1)
    hyp = (lane % 64).astype(F32)
    tables = dot(table_ref[:, 0].reshape(group * 64, 128), pat_ref[...])

    soft = []
    chosen = []
    for g in range(group):
        if late:
            rhs = joined(block_refs, g)
        else:
            rhs = jnp.concatenate([block_refs[0][g][0, 0], block_refs[1][g][0, 0]], axis=1)
        stats = joined(stat_refs, g)
        if halo:
            up = joined(up_refs, g)
            down = joined(down_refs, g)
            above = dot(edge_ref[g, 0][:, 0:64], up)
            below = dot(edge_ref[g, 0][:, 64:128], down)
        else:
            up = down = None
        mean_b, inv_b = boxed_stats(stats, up, down)
        own = own_ref[g, 0]
        masked = jnp.concatenate([own * mask_ref[y : y + 1, :] for y in ys], axis=0)
        product = dot(masked, rhs)
        for i, y in enumerate(ys):
            p = product[WIN * i : WIN * i + WIN]
            if y == 0:
                p = p + above
            if y == 3:
                p = p + below
            z = jnp.where(
                wrapped, p[16:80, 128:], jnp.where(first, p[80:144, :128], p[16:80, :128])
            )
            z8 = jnp.where(
                lane8 < column8,
                p[72:80, 128:],
                jnp.where(lane8 < column8 + 64, p[8:16, 128:], p[72:80, :128]),
            )
            at = count * g + i
            skew[at, 0:8, :] = pltpu.roll(z8, 57, 1, stride=1, stride_axis=0)
            skew[at, 8:72, :] = pltpu.roll(z, 65, 1, stride=1, stride_axis=0)
            cross = skew[at, 8:72, :] + skew[at, 7:71, :] + skew[at, 6:70, :]
            mb = skewed(mean_b[y : y + 1, :128], mean_b[y : y + 1, 128:], column, lane, 65)
            rb = skewed(inv_b[y : y + 1, :128], inv_b[y : y + 1, 128:], column, lane, 65)
            a1, a2, index = (
                tables[64 * g : 64 * g + 64, (3 * i + q) * 128 : (3 * i + q + 1) * 128]
                for q in range(3)
            )
            weight = jnp.exp2((cross * a1 - a2 * mb) * rb)
            picked = jnp.where(index == hyp, weight, 0.0)
            soft.append(jnp.concatenate(split2(weight), axis=1))
            chosen.append(jnp.concatenate(split2(picked), axis=1))
    soft = jnp.concatenate(soft, axis=0)
    chosen = jnp.concatenate(chosen, axis=0)
    r = dot_nt(w2_ref[...], soft)
    rc = dot_nt(w2_ref[...], chosen)
    inv = 1.0 / r[0:2]
    both = jnp.concatenate([(r[2:4] + r[4:6] + r[6:8]) * inv, rc[0:2] * inv], axis=0)
    pieces = group * count // 2
    both = jnp.concatenate([both[:, 128 * v : 128 * v + 128] for v in range(pieces)], axis=0)
    high = both.astype(BF)
    rest = both - high.astype(F32)
    mid = rest.astype(BF)
    low = (rest - mid.astype(F32)).astype(BF)
    both = dot(jnp.concatenate([high, mid, low], axis=0), flip_ref[...])
    both = both[0 : 4 * pieces] + both[4 * pieces : 8 * pieces] + both[8 * pieces :]
    turned = pltpu.roll(both, 64, 1)
    left = lax.broadcasted_iota(jnp.int32, (1, 128), 1) < 64
    cell_iota = lax.broadcasted_iota(jnp.int32, (128, 128), 0)
    for g in range(group):
        for i, y in enumerate(ys):
            at = (count * g + i) // 2 * 4
            lo, hi = (both, turned) if i % 2 == 0 else (turned, both)
            mean_ref[g, i : i + 1, :] = jnp.where(left, lo[at : at + 1], hi[at + 1 : at + 2])
            c = jnp.where(left, lo[at + 2 : at + 3], hi[at + 3 : at + 4])
            values = jnp.concatenate([c * elev_ref[g, y : y + 1, :], c], axis=0)
            value_hi = values.astype(BF).astype(F32)
            values = jnp.concatenate([value_hi, values - value_hi, jnp.zeros((4, 128), F32)], axis=0)
            hot = jnp.where(cell_iota == cell_ref[g, y : y + 1, :], 1.0, 0.0).astype(BF)
            binned = dot_nt(values.astype(BF), hot)
            got = binned[0:2] + binned[2:4]
            at = count * g + i
            rows_ref[0, at : at + 1, 0:128] = got[0:1]
            rows_ref[0, at : at + 1, 128:256] = got[1:2]


def sweep_steps(
    first, steps, ys, group, slot, blocks, stats, ups, downs, own, edge, table, w2, elev, cell, late
):
    images = own.shape[0]
    halo = ups is not None
    count = len(ys)

    def slot_block(g, j):
        return lambda n, k, s: (s[group * k + g], n + first + j, 0, 0)

    def near(n, k, s):
        return (k, n + first, 0, 0)

    def whole(n, k, s):
        return (0, 0)

    def pixels(n, k, s):
        return (k, 0, n + first)

    def pair_specs(rows, kept=FIRST - 1):
        if late:
            maps = (
                lambda n, k, s: (k, kept, 0, 0),
                lambda n, k, s: (k, 0, 0, 0),
                lambda n, k, s: (k, n, 0, 0),
            )
        else:
            maps = (near, lambda n, k, s: (k, n + first + 1, 0, 0))
        return [pl.BlockSpec((group, 1, rows, 128), m) for m in maps]

    def pair_args(arrays):
        return [arrays[0], arrays[1], arrays[1]] if late else [arrays[0], arrays[0]]

    if late:
        in_specs = pair_specs(256, 0)
        args = pair_args(blocks)
    else:
        in_specs = [
            pl.BlockSpec((1, 1, 256, 128), slot_block(g, j)) for j in range(2) for g in range(group)
        ]
        args = [blocks] * (2 * group)
    in_specs += [
        pl.BlockSpec((group, 1, WIN, 256), near),
        pl.BlockSpec((group, 1, 64, 128), near),
        pl.BlockSpec((128, 3 * 128 * count), whole),
        pl.BlockSpec((16, 256), whole),
        pl.BlockSpec((8, 256), whole),
        pl.BlockSpec((128, 128), whole),
        pl.BlockSpec((group, 4, 128), pixels),
        pl.BlockSpec((group, 4, 128), pixels),
    ] + pair_specs(8)
    args += [
        own, table, table_patterns(ys), row_masks(), w2, flips(), elev, cell,
    ] + pair_args(stats)
    if halo:
        in_specs += pair_specs(64) + pair_specs(64) + [pl.BlockSpec((group, 1, WIN, 128), near)]
        args += pair_args(ups) + pair_args(downs) + [edge]
    work = steps * images * count // 4
    return pl.pallas_call(
        functools.partial(sweep_kernel, group, ys, halo, late),
        grid_spec=pltpu.PrefetchScalarGridSpec(
            num_scalar_prefetch=1,
            grid=(steps, images // group),
            in_specs=in_specs,
            out_specs=[
                pl.BlockSpec((group, count, 128), lambda n, k, s: (k, 0, n)),
                pl.BlockSpec((1, count * group, 256), lambda n, k, s: (n, k, 0)),
            ],
            scratch_shapes=[pltpu.VMEM((count * group, 72, 128), F32)],
        ),
        out_shape=[
            jax.ShapeDtypeStruct((images, count, steps * 128), F32),
            jax.ShapeDtypeStruct((steps, images * count, 256), F32),
        ],
        compiler_params=PARAMS,
        cost_estimate=pl.CostEstimate(
            flops=work * 200_000_000, bytes_accessed=work * 400_000, transcendentals=0
        ),
        name="sweep",
    )(slot, *args)


def depth_weights(planes):
    high = lax.reduce_precision(planes, 8, 7)
    mid = lax.reduce_precision(planes - high, 8, 7)
    zero = jnp.zeros_like(planes)
    rows = []
    for v in (jnp.ones_like(planes), high, mid, planes - high - mid):
        rows.append(jnp.concatenate([v, zero]))
        rows.append(jnp.concatenate([zero, v]))
    w = jnp.stack(rows)
    return jnp.concatenate([w, w], axis=1).astype(BF)


def collect_kernel(list_ref, count_ref, a_ref, b_ref, c_ref, d_ref, out_ref, rows):
    at = 0
    for part in (a_ref, b_ref, c_ref, d_ref):
        for n in range(part.shape[0]):
            rows[at : at + part.shape[1], :] = part[n]
            at += part.shape[1]
    for o in range(out_ref.shape[0]):

        def move(step, carry):
            for i in range(8):
                e = step * 8 + i
                out_ref[o, pl.ds(e, 1), :] = rows[pl.ds(list_ref[o, e], 1), :]
            return carry

        lax.fori_loop(0, (count_ref[o] + 7) // 8, move, 0)


def collect(row_list, counts, parts):
    owners, cap = row_list.shape
    total = sum(p.shape[0] * p.shape[1] for p in parts)
    return pl.pallas_call(
        collect_kernel,
        grid_spec=pltpu.PrefetchScalarGridSpec(
            num_scalar_prefetch=2,
            grid=(1,),
            in_specs=[pl.BlockSpec(p.shape, lambda i, a, b: (0, 0, 0)) for p in parts],
            out_specs=pl.BlockSpec((owners, cap, 2 * CELLS), lambda i, a, b: (0, 0, 0)),
            scratch_shapes=[pltpu.VMEM((total, 2 * CELLS), F32)],
        ),
        out_shape=jax.ShapeDtypeStruct((owners, cap, 2 * CELLS), F32),
        compiler_params=PARAMS,
        name="collect",
    )(row_list, counts, *parts)


def place_kernel(slot_ref, count_ref, got_ref, out_ref):
    out_ref[...] = jnp.zeros_like(out_ref)
    for t in range(got_ref.shape[0]):
        count = count_ref[t]

        def add(step, carry):
            for i in range(8):
                e = step * 8 + i
                at = pl.ds(slot_ref[t, e], 1)
                row = jnp.where(e < count, got_ref[t, pl.ds(e, 1), :], 0.0)
                out_ref[at, :] = out_ref[at, :] + row
            return carry

        lax.fori_loop(0, (count + 7) // 8, add, 0)


def place(slots, counts, got, total):
    return pl.pallas_call(
        place_kernel,
        grid_spec=pltpu.PrefetchScalarGridSpec(
            num_scalar_prefetch=2,
            grid=(1,),
            in_specs=[pl.BlockSpec(got.shape, lambda i, a, b: (0, 0, 0))],
            out_specs=pl.BlockSpec((total, 2 * CELLS), lambda i, a, b: (0, 0)),
        ),
        out_shape=jax.ShapeDtypeStruct((total, 2 * CELLS), F32),
        compiler_params=PARAMS,
        name="place",
    )(slots, counts, got)


def neighbour_rows(head, tail):
    count = lax.axis_size("tile")
    above = lax.ppermute(tail, "tile", [(i, i + 1) for i in range(count - 1)])
    below = lax.ppermute(head, "tile", [(i + 1, i) for i in range(count - 1)])
    return above, below


def on_device(
    features, partner_ids, depth_planes, cam_height, ray_down, depth_index, cell_index,
    block_list, block_slot, block_count,
):
    group_count = lax.axis_size("img")
    owners = lax.axis_size("tile")
    my_group = lax.axis_index("img")
    my_tile = lax.axis_index("tile")
    images = features.shape[0]
    table = partner_ids.reshape(group_count, images)
    source_of = table // images
    chosen = jnp.sum(jnp.where(source_of == my_group, table % images, 0), axis=1)
    slot = lax.dynamic_index_in_dim(source_of, my_group, 0, False)

    def exchange(a):
        return lax.all_to_all(a, "img", split_axis=0, concat_axis=0, tiled=True)

    main = exchange(pick(chosen, features, FIRST))

    every = jnp.arange(images, dtype=jnp.int32)
    own = pick(every, features, STEPS + 1)
    own_head, own_tail, own_stats = edges(every, own, False)
    own_up, own_down = neighbour_rows(own_head, own_tail)
    own_turned, edge_turned, own_table = prepare(own, own_up, own_down, own_stats, depth_index)
    packed = pack(chosen, own)

    hyp = jnp.arange(NDEPTH, dtype=jnp.int32)[:, None, None, None]
    plane_at = jnp.sum(
        jnp.where(hyp == depth_index[None], depth_planes[:, None, None, None], 0.0), 0
    )
    elevation = cam_height[:, None, None] - ray_down * plane_at

    meta = jnp.concatenate(
        [block_slot[0, 0], jnp.broadcast_to(block_count[0, 0][:, None], (owners, 128))], axis=1
    )
    metas = [lax.dynamic_slice_in_dim(meta, my_tile, 1, 0)]
    for s in range(1, owners):
        mine = lax.dynamic_slice_in_dim(meta, (my_tile + s) % owners, 1, 0)
        metas.append(lax.ppermute(mine, "tile", [(i, (i + s) % owners) for i in range(owners)]))
    metas = jnp.concatenate(metas, axis=0)
    metas = jnp.take(metas, (my_tile - jnp.arange(owners)) % owners, axis=0)

    w2 = depth_weights(depth_planes)

    packed, own_turned, edge_turned, own_table, elevation, metas, w2 = lax.optimization_barrier(
        (packed, own_turned, edge_turned, own_table, elevation, metas, w2)
    )
    last = exchange(packed)
    head, tail, stats, early = edges(slot, main, True)
    up, down = neighbour_rows(head, tail)
    shared = (own_turned, edge_turned, own_table, w2, elevation, cell_index)
    shared = (own_turned, edge_turned, own_table, w2, elevation, cell_index)
    inner, outer = (1, 2), (0, 3)
    one = (stats,)
    mean_i, rows_i = sweep_steps(0, 2, inner, 16, slot, main, one, None, None, *shared, False)
    up, down, mean_i = lax.optimization_barrier((up, down, mean_i))
    mean_o, rows_o = sweep_steps(0, 2, outer, 16, slot, main, one, (up,), (down,), *shared, False)
    last, mean_o = lax.optimization_barrier((last, mean_o))
    head_l, tail_l, stats_l, late = unpack(slot, last)
    up_l, down_l = neighbour_rows(head_l, tail_l)
    blocks, both = (early, late), (stats, stats_l)
    mean_il, rows_il = sweep_steps(2, 2, inner, 16, slot, blocks, both, None, None, *shared, True)
    mean_ol, rows_ol = sweep_steps(
        2, 2, outer, 16, slot, blocks, both, (up, up_l), (down, down_l), *shared, True
    )
    mean_i = jnp.concatenate([mean_i, mean_il], axis=2)
    mean_o = jnp.concatenate([mean_o, mean_ol], axis=2)
    mean_range = jnp.concatenate([mean_o[:, 0:1], mean_i, mean_o[:, 1:2]], axis=1)

    lists = block_list[0, 0]
    n, r, k = lists % STEPS, lists // STEPS % 4, lists // (4 * STEPS)
    inside = (r == 1) | (r == 2)
    row_list = 2 * images * n + 2 * k + jnp.where(inside, r - 1, 8 * images + r // 3)
    send = collect(row_list, block_count[0, 0], (rows_i, rows_il, rows_o, rows_ol))
    got = lax.all_to_all(send, "tile", split_axis=0, concat_axis=0, tiled=True)
    dense = place(metas[:, :128], metas[:, 128], got, group_count * PATCH_DEV)
    parts = exchange(dense.reshape(group_count, PATCH_DEV, 2 * CELLS))
    total = jnp.sum(parts, axis=0)
    return mean_range, total[:, :CELLS] / (total[:, CELLS:] + 1.0)


def solution(mesh):
    return jax.shard_map(
        on_device,
        mesh=mesh,
        in_specs=(
            P("img", None, "tile", None),
            P(),
            P(),
            P("img"),
            P("img", "tile", None),
            P("img", "tile", None),
            P("img", "tile", None),
            P("img", "tile", None, None),
            P("img", "tile", None, None),
            P("img", "tile", None),
        ),
        out_specs=(P("img", "tile", None), P(("img", "tile"), None)),
        check_vma=False,
    )
```

```python
import functools
import math

import numpy as np
import jax
import jax.numpy as jnp
from jax import lax
from jax.experimental import pallas as pl
from jax.experimental.pallas import tpu as pltpu
from jax.sharding import PartitionSpec as P

NDEPTH = 64
CELLS = 128
PATCH_DEV = 16
STEPS = 4
WIN = 144
LOG2E = math.log2(math.e)
BF = jnp.bfloat16
F32 = jnp.float32
NT = (((1,), (1,)), ((), ()))
PARAMS = pltpu.CompilerParams(vmem_limit_bytes=60 * 1024 * 1024)
SMALL = pltpu.CompilerParams(vmem_limit_bytes=24 * 1024 * 1024)


def dot(a, b):
    return jnp.dot(a, b, preferred_element_type=F32)


def dot_nt(a, b):
    return lax.dot_general(a, b, NT, preferred_element_type=F32)


def table_patterns(ys):
    pat = np.zeros((128, 3 * len(ys), 128), np.float32)
    for half in range(2):
        lanes = slice(64 * half, 64 * half + 64)
        for i, y in enumerate(ys):
            for q in range(2):
                for s in range(3):
                    pat[half * 32 + s * 8 + q * 4 + y, i * 3 + q, lanes] = 1.0
            pat[half * 32 + 24 + y, i * 3 + 2, lanes] = 1.0
    return jnp.asarray(pat.reshape(128, -1), BF)


def row_masks():
    y = np.arange(16)[:, None]
    k = np.arange(256)[None, :] % 4
    return jnp.asarray((np.abs(k - y) <= 1) & (y < 4), BF)


def flips():
    m = np.zeros((128, 128), np.float32)
    for i in range(128):
        m[i, i // 64 * 64 + 63 - i % 64] = 1.0
    return jnp.asarray(m, BF)


def reversal():
    m = np.zeros((WIN, 256), np.float32)
    for i in range(WIN):
        m[i, WIN - 1 - i] = 1.0
    return jnp.asarray(m, BF)


def edge_constants():
    sel = np.zeros((128, 256), np.float32)
    for c in range(64):
        sel[c, 4 * c] = 1.0
        sel[64 + c, 4 * c + 3] = 1.0
    return (jnp.asarray(sel, BF),)


def split2(a):
    high = a.astype(BF)
    return high, (a - high.astype(F32)).astype(BF)


def boxed_stats(stats, up, down):
    blank = jnp.zeros((1, 256), F32)
    sums = [blank] + [stats[y : y + 1] for y in range(4)] + [blank]
    sqs = [blank] + [stats[4 + y : 5 + y] for y in range(4)] + [blank]
    if up is not None:
        for at, halo in ((0, up.astype(F32)), (5, down.astype(F32))):
            sums[at] = jnp.sum(halo, 0, keepdims=True)
            sqs[at] = jnp.sum(halo * halo, 0, keepdims=True)
    tall = jnp.concatenate(
        [v[y] + v[y + 1] + v[y + 2] for v in (sums, sqs) for y in range(4)], axis=0
    )
    boxed = (tall + pltpu.roll(tall, 255, 1) + pltpu.roll(tall, 254, 1)) * (1.0 / 576.0)
    mean = boxed[0:4]
    return mean, lax.rsqrt(boxed[4:8] - mean * mean + 1e-5)


PART = 8
PACKED = 136
FIRST = 3


def pick(idx, features, blocks):
    count = idx.shape[0]
    images, channels, rows, _ = features.shape

    def kernel(idx_ref, features_ref, out_ref, strips, in_sem, out_sem):
        def read(k):
            return pltpu.make_async_copy(
                features_ref.at[k, :, :, pl.ds(0, 128 * blocks)], strips.at[k], in_sem.at[k]
            )

        def write(s, j):
            return pltpu.make_async_copy(
                strips.at[idx_ref[s], :, :, pl.ds(128 * j, 128)], out_ref.at[s, j], out_sem.at[s, j]
            )

        for k in range(images):
            read(k).start()
        for k in range(images):
            read(k).wait()
        for s in range(count):
            for j in range(blocks):
                write(s, j).start()
        for s in range(count):
            for j in range(blocks):
                write(s, j).wait()

    out = pl.pallas_call(
        kernel,
        grid_spec=pltpu.PrefetchScalarGridSpec(
            num_scalar_prefetch=1,
            grid=(1,),
            in_specs=[pl.BlockSpec(memory_space=pl.ANY)],
            out_specs=pl.BlockSpec(memory_space=pl.ANY),
            scratch_shapes=[
                pltpu.VMEM((images, channels, rows, 128 * blocks), BF),
                pltpu.SemaphoreType.DMA((images,)),
                pltpu.SemaphoreType.DMA((count, blocks)),
            ],
        ),
        out_shape=jax.ShapeDtypeStruct((count, blocks, channels, rows, 128), BF),
        compiler_params=PARAMS,
        cost_estimate=pl.CostEstimate(
            flops=0, bytes_accessed=count * blocks * 131072, transcendentals=0
        ),
        name="pick",
    )(idx, features)
    return out.reshape(count, blocks, channels * rows, 128)


def pack_constants():
    spread = np.zeros((128, 256), np.float32)
    for i in range(64):
        spread[i, i] = 1.0
        spread[64 + i, 128 + i] = 1.0
    column = np.zeros((8, 128), np.float32)
    column[0, 64] = 1.0
    into = np.zeros((256, 128), np.float32)
    into[:, 64] = 1.0
    return tuple(jnp.asarray(m, BF) for m in (spread, column, into, np.eye(256)))


def pack_kernel(idx_ref, *refs):
    whole, part = refs[:PART], refs[PART : 2 * PART]
    spread_ref, column_ref, out_ref = refs[2 * PART :]
    for g in range(PART):
        out_ref[g, 0:256, :] = whole[g][0, 0]
        block = part[g][0, 0]
        out_ref[g, 256:384, :] = (
            dot_nt(block[0:128], spread_ref[:, 0:128]) + dot_nt(block[128:256], spread_ref[:, 128:])
        ).astype(BF)
        line = dot_nt(column_ref[...], block)
        out_ref[g, 384:392, :] = jnp.concatenate(
            [line[0:1, 0:128], line[0:1, 128:256], jnp.zeros((6, 128), F32)], axis=0
        ).astype(BF)


def pack(idx, own):
    count = idx.shape[0]
    spread, column, _, _ = pack_constants()

    def chosen(g, j):
        return lambda k, s: (s[PART * k + g], j, 0, 0)

    return pl.pallas_call(
        pack_kernel,
        grid_spec=pltpu.PrefetchScalarGridSpec(
            num_scalar_prefetch=1,
            grid=(count // PART,),
            in_specs=[
                pl.BlockSpec((1, 1, 256, 128), chosen(g, j))
                for j in (FIRST, FIRST + 1)
                for g in range(PART)
            ]
            + [
                pl.BlockSpec((128, 256), lambda k, s: (0, 0)),
                pl.BlockSpec((8, 128), lambda k, s: (0, 0)),
            ],
            out_specs=pl.BlockSpec((PART, 256 + PACKED, 128), lambda k, s: (k, 0, 0)),
        ),
        out_shape=jax.ShapeDtypeStruct((count, 256 + PACKED, 128), BF),
        compiler_params=PARAMS,
        name="pack",
    )(idx, *[own] * (2 * PART), spread, column)


def block_edges(block, sel_ref):
    rows = dot(sel_ref[...], block).astype(BF)
    value = block.astype(F32).reshape(32, 8, 128)
    total = jnp.sum(value, 0)
    square = jnp.sum(value * value, 0)
    stats = jnp.concatenate([total[0:4] + total[4:8], square[0:4] + square[4:8]], axis=0)
    return rows[0:64], rows[64:128], stats


def edge_kernel(slot_ref, *refs):
    blocks, (sel_ref, head_ref, tail_ref, stats_ref, *kept) = refs[:PART], refs[PART:]
    for g in range(PART):
        if kept:
            kept[0][g, 0] = blocks[g][0, blocks[g].shape[1] - 1]
        for j in range(stats_ref.shape[1]):
            head, tail, stats = block_edges(blocks[g][0, j], sel_ref)
            head_ref[g, j] = head
            tail_ref[g, j] = tail
            stats_ref[g, j] = stats


def unpack_kernel(slot_ref, *refs):
    packed = refs[:PART]
    (
        spread_ref, into_ref, eye_ref, sel_ref, head_ref, tail_ref, stats_ref, block_ref,
    ) = refs[PART:]
    for g in range(PART):
        wide = dot(packed[g][0, 256:384, :], spread_ref[...])
        line = packed[g][0, 384:392, :]
        line = jnp.concatenate([line[0:1], line[1:2]], axis=1)
        column = dot(eye_ref[...] * line, into_ref[...])
        block = jnp.concatenate([wide[:, :128], wide[:, 128:]], axis=0) + column
        blocks = (packed[g][0, 0:256, :], block.astype(BF))
        for j in range(2):
            block_ref[g, j] = blocks[j]
            head, tail, stats = block_edges(blocks[j], sel_ref)
            head_ref[g, j] = head
            tail_ref[g, j] = tail
            stats_ref[g, j] = stats


def edge_outputs(images, blocks):
    specs = [
        pl.BlockSpec((PART, blocks, 64, 128), lambda k, s: (k, 0, 0, 0)),
        pl.BlockSpec((PART, blocks, 64, 128), lambda k, s: (k, 0, 0, 0)),
        pl.BlockSpec((PART, blocks, 8, 128), lambda k, s: (k, 0, 0, 0)),
    ]
    shapes = [
        jax.ShapeDtypeStruct((images, blocks, 64, 128), BF),
        jax.ShapeDtypeStruct((images, blocks, 64, 128), BF),
        jax.ShapeDtypeStruct((images, blocks, 8, 128), F32),
    ]
    return specs, shapes


def whole_spec(a):
    return pl.BlockSpec(a.shape, lambda k, s: (0,) * a.ndim)


def edges(slot, recv, keep_last):
    images, blocks = slot.shape[0], recv.shape[1]
    constants = edge_constants()
    specs, shapes = edge_outputs(images, blocks)
    if keep_last:
        specs = specs + [pl.BlockSpec((PART, 1, 256, 128), lambda k, s: (k, 0, 0, 0))]
        shapes = shapes + [jax.ShapeDtypeStruct((images, 1, 256, 128), BF)]

    def by_slot(g):
        return lambda k, s: (s[PART * k + g], 0, 0, 0)

    return pl.pallas_call(
        edge_kernel,
        grid_spec=pltpu.PrefetchScalarGridSpec(
            num_scalar_prefetch=1,
            grid=(images // PART,),
            in_specs=[pl.BlockSpec((1, blocks, 256, 128), by_slot(g)) for g in range(PART)]
            + [whole_spec(a) for a in constants],
            out_specs=specs,
        ),
        out_shape=shapes,
        cost_estimate=pl.CostEstimate(
            flops=images * blocks * 20_000_000, bytes_accessed=images * blocks * 100_000,
            transcendentals=0,
        ),
        compiler_params=PARAMS,
        name="edges",
    )(slot, *[recv] * PART, *constants)


def unpack(slot, packed):
    images = slot.shape[0]
    spread, _, into, eye = pack_constants()
    constants = (spread, into, eye) + edge_constants()
    specs, shapes = edge_outputs(images, 2)

    def by_slot(g):
        return lambda k, s: (s[PART * k + g], 0, 0)

    return pl.pallas_call(
        unpack_kernel,
        grid_spec=pltpu.PrefetchScalarGridSpec(
            num_scalar_prefetch=1,
            grid=(images // PART,),
            in_specs=[pl.BlockSpec((1, 256 + PACKED, 128), by_slot(g)) for g in range(PART)]
            + [whole_spec(a) for a in constants],
            out_specs=specs + [pl.BlockSpec((PART, 2, 256, 128), lambda k, s: (k, 0, 0, 0))],
        ),
        out_shape=shapes + [jax.ShapeDtypeStruct((images, 2, 256, 128), BF)],
        compiler_params=SMALL,
        name="unpack",
    )(slot, *[packed] * PART, *constants)


def prepare_kernel(
    own_ref, up_ref, up_last_ref, down_ref, down_last_ref, stat_ref, index_ref, rev_ref, flip_ref, own_out, edge_out, table_out
):
    mean_inv = 24.0 * LOG2E
    for n in range(STEPS):
        block = jnp.concatenate([own_ref[0, n], own_ref[0, n + 1]], axis=1)
        final = n + 1 == STEPS
        up = jnp.concatenate([up_ref[0, n], up_last_ref[0] if final else up_ref[0, n + 1]], axis=1)
        down = jnp.concatenate(
            [down_ref[0, n], down_last_ref[0] if final else down_ref[0, n + 1]], axis=1
        )
        own_out[0, n] = dot_nt(rev_ref[...], block).astype(BF)
        edge_out[0, n] = dot_nt(rev_ref[...], jnp.concatenate([up, down], axis=0)).astype(BF)
        stats = jnp.concatenate([stat_ref[0, n], stat_ref[0, n + 1]], axis=1)
        mean, inv = boxed_stats(stats, up, down)
        scaled = inv * mean_inv
        both = jnp.concatenate([scaled * (1.0 / 576.0), scaled * mean], axis=0)[:, :128]
        high = both.astype(BF).astype(F32)
        mid = (both - high).astype(BF).astype(F32)
        index = index_ref[0, :, 128 * n : 128 * n + 128].astype(F32)
        rows = jnp.concatenate(
            [high, mid, both - high - mid, index, jnp.zeros((4, 128), F32)], axis=0
        ).astype(BF)
        blank = jnp.zeros((64, 64), F32)
        left = dot_nt(flip_ref[0:64, :], rows)
        right = dot_nt(flip_ref[64:128, :], rows)
        table_out[0, n] = jnp.concatenate([left, right, blank], axis=1).astype(BF)


def prepare(own, up, up_last, down, down_last, stats, depth_index):
    images, blocks = own.shape[0], own.shape[1]
    return pl.pallas_call(
        prepare_kernel,
        grid=(images,),
        in_specs=[
            pl.BlockSpec((1, blocks, 256, 128), lambda k: (k, 0, 0, 0)),
            pl.BlockSpec((1, STEPS, 64, 128), lambda k: (k, 0, 0, 0)),
            pl.BlockSpec((1, 64, 128), lambda k: (k, 0, 0)),
            pl.BlockSpec((1, STEPS, 64, 128), lambda k: (k, 0, 0, 0)),
            pl.BlockSpec((1, 64, 128), lambda k: (k, 0, 0)),
            pl.BlockSpec((1, blocks, 8, 128), lambda k: (k, 0, 0, 0)),
            pl.BlockSpec((1, 4, 512), lambda k: (k, 0, 0)),
            pl.BlockSpec((WIN, 256), lambda k: (0, 0)),
            pl.BlockSpec((128, 128), lambda k: (0, 0)),
        ],
        out_specs=[
            pl.BlockSpec((1, STEPS, WIN, 256), lambda k: (k, 0, 0, 0)),
            pl.BlockSpec((1, STEPS, WIN, 128), lambda k: (k, 0, 0, 0)),
            pl.BlockSpec((1, STEPS, 64, 128), lambda k: (k, 0, 0, 0)),
        ],
        out_shape=[
            jax.ShapeDtypeStruct((images, STEPS, WIN, 256), BF),
            jax.ShapeDtypeStruct((images, STEPS, WIN, 128), BF),
            jax.ShapeDtypeStruct((images, STEPS, 64, 128), BF),
        ],
        cost_estimate=pl.CostEstimate(
            flops=images * STEPS * 40_000_000, bytes_accessed=images * 1_000_000, transcendentals=0
        ),
        compiler_params=PARAMS,
        name="prepare",
    )(own, up, up_last, down, down_last, stats, depth_index, reversal(), flips())


def skewed(left, right, column, lane, shift):
    return pltpu.roll(jnp.where(lane < column, right, left), shift, 1, stride=1, stride_axis=0)


def sweep_kernel(group, ys, halo, late, *refs):
    refs = list(refs[1:])

    def take(count):
        out = refs[:count]
        del refs[:count]
        return out

    count = len(ys)
    block_refs = take(3) if late else (take(group), take(group))
    own_ref, table_ref, pat_ref, mask_ref, w2_ref, flip_ref, elev_ref, cell_ref = take(8)

    def joined(three, g):
        if late:
            early, before, after = three
            near = jnp.where(pl.program_id(0) == 0, early[g, 0], before[g, 0])
        else:
            near, after = three[0][g, 0], three[1]
        return jnp.concatenate([near, after[g, 0]], axis=1)

    width = 3 if late else 2
    stat_refs = take(width)
    up_refs = take(width) if halo else None
    down_refs = take(width) if halo else None
    edge_ref = take(1)[0] if halo else None
    mean_ref, rows_ref, skew = refs

    column = 63 - lax.broadcasted_iota(jnp.int32, (64, 128), 0)
    lane = lax.broadcasted_iota(jnp.int32, (64, 128), 1)
    wrapped = lane < column
    first = lane < column + 64
    column8 = 7 - lax.broadcasted_iota(jnp.int32, (8, 128), 0)
    lane8 = lax.broadcasted_iota(jnp.int32, (8, 128), 1)
    hyp = (lane % 64).astype(F32)
    tables = dot(table_ref[:, 0].reshape(group * 64, 128), pat_ref[...])

    soft = []
    chosen = []
    for g in range(group):
        if late:
            rhs = joined(block_refs, g)
        else:
            rhs = jnp.concatenate([block_refs[0][g][0, 0], block_refs[1][g][0, 0]], axis=1)
        stats = joined(stat_refs, g)
        if halo:
            up = joined(up_refs, g)
            down = joined(down_refs, g)
            above = dot(edge_ref[g, 0][:, 0:64], up)
            below = dot(edge_ref[g, 0][:, 64:128], down)
        else:
            up = down = None
        mean_b, inv_b = boxed_stats(stats, up, down)
        own = own_ref[g, 0]
        masked = jnp.concatenate([own * mask_ref[y : y + 1, :] for y in ys], axis=0)
        product = dot(masked, rhs)
        for i, y in enumerate(ys):
            p = product[WIN * i : WIN * i + WIN]
            if y == 0:
                p = p + above
            if y == 3:
                p = p + below
            z = jnp.where(
                wrapped, p[16:80, 128:], jnp.where(first, p[80:144, :128], p[16:80, :128])
            )
            z8 = jnp.where(
                lane8 < column8,
                p[72:80, 128:],
                jnp.where(lane8 < column8 + 64, p[8:16, 128:], p[72:80, :128]),
            )
            at = count * g + i
            skew[at, 0:8, :] = pltpu.roll(z8, 57, 1, stride=1, stride_axis=0)
            skew[at, 8:72, :] = pltpu.roll(z, 65, 1, stride=1, stride_axis=0)
            cross = skew[at, 8:72, :] + skew[at, 7:71, :] + skew[at, 6:70, :]
            mb = skewed(mean_b[y : y + 1, :128], mean_b[y : y + 1, 128:], column, lane, 65)
            rb = skewed(inv_b[y : y + 1, :128], inv_b[y : y + 1, 128:], column, lane, 65)
            a1, a2, index = (
                tables[64 * g : 64 * g + 64, (3 * i + q) * 128 : (3 * i + q + 1) * 128]
                for q in range(3)
            )
            weight = jnp.exp2((cross * a1 - a2 * mb) * rb)
            picked = jnp.where(index == hyp, weight, 0.0)
            soft.append(jnp.concatenate(split2(weight), axis=1))
            chosen.append(jnp.concatenate(split2(picked), axis=1))
    soft = jnp.concatenate(soft, axis=0)
    chosen = jnp.concatenate(chosen, axis=0)
    r = dot_nt(w2_ref[...], soft)
    rc = dot_nt(w2_ref[...], chosen)
    inv = 1.0 / r[0:2]
    both = jnp.concatenate([(r[2:4] + r[4:6] + r[6:8]) * inv, rc[0:2] * inv], axis=0)
    pieces = group * count // 2
    both = jnp.concatenate([both[:, 128 * v : 128 * v + 128] for v in range(pieces)], axis=0)
    high = both.astype(BF)
    rest = both - high.astype(F32)
    mid = rest.astype(BF)
    low = (rest - mid.astype(F32)).astype(BF)
    both = dot(jnp.concatenate([high, mid, low], axis=0), flip_ref[...])
    both = both[0 : 4 * pieces] + both[4 * pieces : 8 * pieces] + both[8 * pieces :]
    turned = pltpu.roll(both, 64, 1)
    left = lax.broadcasted_iota(jnp.int32, (1, 128), 1) < 64
    cell_iota = lax.broadcasted_iota(jnp.int32, (128, 128), 0)
    for g in range(group):
        for i, y in enumerate(ys):
            at = (count * g + i) // 2 * 4
            lo, hi = (both, turned) if i % 2 == 0 else (turned, both)
            mean_ref[g, i : i + 1, :] = jnp.where(left, lo[at : at + 1], hi[at + 1 : at + 2])
            c = jnp.where(left, lo[at + 2 : at + 3], hi[at + 3 : at + 4])
            values = jnp.concatenate([c * elev_ref[g, y : y + 1, :], c], axis=0)
            value_hi = values.astype(BF).astype(F32)
            values = jnp.concatenate([value_hi, values - value_hi, jnp.zeros((4, 128), F32)], axis=0)
            hot = jnp.where(cell_iota == cell_ref[g, y : y + 1, :], 1.0, 0.0).astype(BF)
            binned = dot_nt(values.astype(BF), hot)
            got = binned[0:2] + binned[2:4]
            at = count * g + i
            rows_ref[0, at : at + 1, 0:128] = got[0:1]
            rows_ref[0, at : at + 1, 128:256] = got[1:2]


def sweep_steps(
    first, steps, ys, group, slot, blocks, stats, ups, downs, own, edge, table, w2, elev, cell, late
):
    images = own.shape[0]
    halo = ups is not None
    count = len(ys)

    def slot_block(g, j):
        return lambda n, k, s: (s[group * k + g], n + first + j, 0, 0)

    def near(n, k, s):
        return (k, n + first, 0, 0)

    def whole(n, k, s):
        return (0, 0)

    def pixels(n, k, s):
        return (k, 0, n + first)

    def pair_specs(rows, kept=FIRST - 1):
        if late:
            maps = (
                lambda n, k, s: (k, kept, 0, 0),
                lambda n, k, s: (k, 0, 0, 0),
                lambda n, k, s: (k, n, 0, 0),
            )
        else:
            maps = (near, lambda n, k, s: (k, n + first + 1, 0, 0))
        return [pl.BlockSpec((group, 1, rows, 128), m) for m in maps]

    def pair_args(arrays):
        return [arrays[0], arrays[1], arrays[1]] if late else [arrays[0], arrays[0]]

    if late:
        in_specs = pair_specs(256, 0)
        args = pair_args(blocks)
    else:
        in_specs = [
            pl.BlockSpec((1, 1, 256, 128), slot_block(g, j)) for j in range(2) for g in range(group)
        ]
        args = [blocks] * (2 * group)
    in_specs += [
        pl.BlockSpec((group, 1, WIN, 256), near),
        pl.BlockSpec((group, 1, 64, 128), near),
        pl.BlockSpec((128, 3 * 128 * count), whole),
        pl.BlockSpec((16, 256), whole),
        pl.BlockSpec((8, 256), whole),
        pl.BlockSpec((128, 128), whole),
        pl.BlockSpec((group, 4, 128), pixels),
        pl.BlockSpec((group, 4, 128), pixels),
    ] + pair_specs(8)
    args += [
        own, table, table_patterns(ys), row_masks(), w2, flips(), elev, cell,
    ] + pair_args(stats)
    if halo:
        in_specs += pair_specs(64) + pair_specs(64) + [pl.BlockSpec((group, 1, WIN, 128), near)]
        args += pair_args(ups) + pair_args(downs) + [edge]
    work = steps * images * count // 4
    return pl.pallas_call(
        functools.partial(sweep_kernel, group, ys, halo, late),
        grid_spec=pltpu.PrefetchScalarGridSpec(
            num_scalar_prefetch=1,
            grid=(steps, images // group),
            in_specs=in_specs,
            out_specs=[
                pl.BlockSpec((group, count, 128), lambda n, k, s: (k, 0, n)),
                pl.BlockSpec((1, count * group, 256), lambda n, k, s: (n, k, 0)),
            ],
            scratch_shapes=[pltpu.VMEM((count * group, 72, 128), F32)],
        ),
        out_shape=[
            jax.ShapeDtypeStruct((images, count, steps * 128), F32),
            jax.ShapeDtypeStruct((steps, images * count, 256), F32),
        ],
        compiler_params=PARAMS,
        cost_estimate=pl.CostEstimate(
            flops=work * 200_000_000, bytes_accessed=work * 400_000, transcendentals=0
        ),
        name="sweep",
    )(slot, *args)


def depth_weights(planes):
    high = lax.reduce_precision(planes, 8, 7)
    mid = lax.reduce_precision(planes - high, 8, 7)
    zero = jnp.zeros_like(planes)
    rows = []
    for v in (jnp.ones_like(planes), high, mid, planes - high - mid):
        rows.append(jnp.concatenate([v, zero]))
        rows.append(jnp.concatenate([zero, v]))
    w = jnp.stack(rows)
    return jnp.concatenate([w, w], axis=1).astype(BF)


def collect_kernel(list_ref, count_ref, a_ref, b_ref, c_ref, d_ref, out_ref, rows):
    at = 0
    for part in (a_ref, b_ref, c_ref, d_ref):
        for n in range(part.shape[0]):
            rows[at : at + part.shape[1], :] = part[n]
            at += part.shape[1]
    for o in range(out_ref.shape[0]):

        def move(step, carry):
            for i in range(8):
                e = step * 8 + i
                out_ref[o, pl.ds(e, 1), :] = rows[pl.ds(list_ref[o, e], 1), :]
            return carry

        lax.fori_loop(0, (count_ref[o] + 7) // 8, move, 0)


def collect(row_list, counts, parts):
    owners, cap = row_list.shape
    total = sum(p.shape[0] * p.shape[1] for p in parts)
    return pl.pallas_call(
        collect_kernel,
        grid_spec=pltpu.PrefetchScalarGridSpec(
            num_scalar_prefetch=2,
            grid=(1,),
            in_specs=[pl.BlockSpec(p.shape, lambda i, a, b: (0, 0, 0)) for p in parts],
            out_specs=pl.BlockSpec((owners, cap, 2 * CELLS), lambda i, a, b: (0, 0, 0)),
            scratch_shapes=[pltpu.VMEM((total, 2 * CELLS), F32)],
        ),
        out_shape=jax.ShapeDtypeStruct((owners, cap, 2 * CELLS), F32),
        compiler_params=SMALL,
        name="collect",
    )(row_list, counts, *parts)


def place_kernel(slot_ref, count_ref, got_ref, out_ref):
    out_ref[...] = jnp.zeros_like(out_ref)
    for t in range(got_ref.shape[0]):
        count = count_ref[t]

        def add(step, carry):
            for i in range(8):
                e = step * 8 + i
                at = pl.ds(slot_ref[t, e], 1)
                row = jnp.where(e < count, got_ref[t, pl.ds(e, 1), :], 0.0)
                out_ref[at, :] = out_ref[at, :] + row
            return carry

        lax.fori_loop(0, (count + 7) // 8, add, 0)


def place(slots, counts, got, total):
    return pl.pallas_call(
        place_kernel,
        grid_spec=pltpu.PrefetchScalarGridSpec(
            num_scalar_prefetch=2,
            grid=(1,),
            in_specs=[pl.BlockSpec(got.shape, lambda i, a, b: (0, 0, 0))],
            out_specs=pl.BlockSpec((total, 2 * CELLS), lambda i, a, b: (0, 0)),
        ),
        out_shape=jax.ShapeDtypeStruct((total, 2 * CELLS), F32),
        compiler_params=SMALL,
        name="place",
    )(slots, counts, got)


def neighbour_rows(head, tail):
    count = lax.axis_size("tile")
    above = lax.ppermute(tail, "tile", [(i, i + 1) for i in range(count - 1)])
    below = lax.ppermute(head, "tile", [(i + 1, i) for i in range(count - 1)])
    return above, below


def on_device(
    features, partner_ids, depth_planes, cam_height, ray_down, depth_index, cell_index,
    block_list, block_slot, block_count,
):
    group_count = lax.axis_size("img")
    owners = lax.axis_size("tile")
    my_group = lax.axis_index("img")
    my_tile = lax.axis_index("tile")
    images = features.shape[0]
    table = partner_ids.reshape(group_count, images)
    source_of = table // images
    chosen = jnp.sum(jnp.where(source_of == my_group, table % images, 0), axis=1)
    slot = lax.dynamic_index_in_dim(source_of, my_group, 0, False)

    def exchange(a):
        return lax.all_to_all(a, "img", split_axis=0, concat_axis=0, tiled=True)

    main = exchange(pick(chosen, features, FIRST))

    every = jnp.arange(images, dtype=jnp.int32)
    own = pick(every, features, STEPS + 1)
    own_head, own_tail, own_stats = edges(every, own, False)
    own_up, own_down = neighbour_rows(own_head[:, :STEPS], own_tail[:, :STEPS])
    ends = [jnp.transpose(v[:, STEPS, :, :2], (0, 2, 1)).reshape(images, -1) for v in (own_head, own_tail)]
    ends = [v.reshape(images, 2, -1) for v in neighbour_rows(*ends)]
    up_last, down_last = (
        jnp.pad(jnp.transpose(v, (0, 2, 1)), ((0, 0), (0, 0), (0, 126))) for v in ends
    )
    own_turned, edge_turned, own_table = prepare(
        own, own_up, up_last, own_down, down_last, own_stats, depth_index
    )
    packed = pack(chosen, own)

    hyp = jnp.arange(NDEPTH, dtype=jnp.int32)[:, None, None, None]
    plane_at = jnp.sum(
        jnp.where(hyp == depth_index[None], depth_planes[:, None, None, None], 0.0), 0
    )
    elevation = cam_height[:, None, None] - ray_down * plane_at

    meta = jnp.concatenate(
        [block_slot[0, 0], jnp.broadcast_to(block_count[0, 0][:, None], (owners, 128))], axis=1
    )
    metas = [lax.dynamic_slice_in_dim(meta, my_tile, 1, 0)]
    for s in range(1, owners):
        mine = lax.dynamic_slice_in_dim(meta, (my_tile + s) % owners, 1, 0)
        metas.append(lax.ppermute(mine, "tile", [(i, (i + s) % owners) for i in range(owners)]))
    metas = jnp.concatenate(metas, axis=0)
    metas = jnp.take(metas, (my_tile - jnp.arange(owners)) % owners, axis=0)

    w2 = depth_weights(depth_planes)

    packed, own_turned, edge_turned, own_table, elevation, metas, w2 = lax.optimization_barrier(
        (packed, own_turned, edge_turned, own_table, elevation, metas, w2)
    )
    last = exchange(packed)
    head, tail, stats, early = edges(slot, main, True)
    up, down = neighbour_rows(head, tail)
    shared = (own_turned, edge_turned, own_table, w2, elevation, cell_index)
    shared = (own_turned, edge_turned, own_table, w2, elevation, cell_index)
    inner, outer = (1, 2), (0, 3)
    one = (stats,)
    mean_i, rows_i = sweep_steps(0, 2, inner, 16, slot, main, one, None, None, *shared, False)
    up, down, mean_i = lax.optimization_barrier((up, down, mean_i))
    mean_o, rows_o = sweep_steps(0, 2, outer, 16, slot, main, one, (up,), (down,), *shared, False)
    last, mean_o = lax.optimization_barrier((last, mean_o))
    head_l, tail_l, stats_l, late = unpack(slot, last)
    up_l, down_l = neighbour_rows(head_l, tail_l)
    blocks, both = (early, late), (stats, stats_l)
    mean_il, rows_il = sweep_steps(2, 2, inner, 16, slot, blocks, both, None, None, *shared, True)
    mean_ol, rows_ol = sweep_steps(
        2, 2, outer, 16, slot, blocks, both, (up, up_l), (down, down_l), *shared, True
    )
    mean_i = jnp.concatenate([mean_i, mean_il], axis=2)
    mean_o = jnp.concatenate([mean_o, mean_ol], axis=2)
    mean_range = jnp.concatenate([mean_o[:, 0:1], mean_i, mean_o[:, 1:2]], axis=1)

    lists = block_list[0, 0]
    n, r, k = lists % STEPS, lists // STEPS % 4, lists // (4 * STEPS)
    inside = (r == 1) | (r == 2)
    row_list = 2 * images * n + 2 * k + jnp.where(inside, r - 1, 8 * images + r // 3)
    send = collect(row_list, block_count[0, 0], (rows_i, rows_il, rows_o, rows_ol))
    got = lax.all_to_all(send, "tile", split_axis=0, concat_axis=0, tiled=True)
    dense = place(metas[:, :128], metas[:, 128], got, group_count * PATCH_DEV)
    parts = exchange(dense.reshape(group_count, PATCH_DEV, 2 * CELLS))
    total = jnp.sum(parts, axis=0)
    return mean_range, total[:, :CELLS] / (total[:, CELLS:] + 1.0)


def solution(mesh):
    return jax.shard_map(
        on_device,
        mesh=mesh,
        in_specs=(
            P("img", None, "tile", None),
            P(),
            P(),
            P("img"),
            P("img", "tile", None),
            P("img", "tile", None),
            P("img", "tile", None),
            P("img", "tile", None, None),
            P("img", "tile", None, None),
            P("img", "tile", None),
        ),
        out_specs=(P("img", "tile", None), P(("img", "tile"), None)),
        check_vma=False,
    )
```

```python
import functools
import math

import numpy as np
import jax
import jax.numpy as jnp
from jax import lax
from jax.experimental import pallas as pl
from jax.experimental.pallas import tpu as pltpu
from jax.sharding import PartitionSpec as P

NDEPTH = 64
CELLS = 128
PATCH_DEV = 16
STEPS = 4
WIN = 144
LOG2E = math.log2(math.e)
BF = jnp.bfloat16
F32 = jnp.float32
NT = (((1,), (1,)), ((), ()))
PARAMS = pltpu.CompilerParams(vmem_limit_bytes=60 * 1024 * 1024)
SMALL = pltpu.CompilerParams(vmem_limit_bytes=24 * 1024 * 1024)


def dot(a, b):
    return jnp.dot(a, b, preferred_element_type=F32)


def dot_nt(a, b):
    return lax.dot_general(a, b, NT, preferred_element_type=F32)


def table_patterns(ys):
    pat = np.zeros((128, 3 * len(ys), 128), np.float32)
    for half in range(2):
        lanes = slice(64 * half, 64 * half + 64)
        for i, y in enumerate(ys):
            for q in range(2):
                for s in range(3):
                    pat[half * 32 + s * 8 + q * 4 + y, i * 3 + q, lanes] = 1.0
            pat[half * 32 + 24 + y, i * 3 + 2, lanes] = 1.0
    return jnp.asarray(pat.reshape(128, -1), BF)


def row_masks():
    masks = np.zeros((16, 256), np.float32)
    for y in range(4):
        masks[y] = np.abs(np.arange(256) % 4 - y) <= 1
    masks[8, 0:64] = 1.0
    masks[11, 64:128] = 1.0
    return jnp.asarray(masks, BF)


def flips():
    m = np.zeros((128, 128), np.float32)
    for i in range(128):
        m[i, i // 64 * 64 + 63 - i % 64] = 1.0
    return jnp.asarray(m, BF)


def reversal():
    m = np.zeros((WIN, 256), np.float32)
    for i in range(WIN):
        m[i, WIN - 1 - i] = 1.0
    return jnp.asarray(m, BF)


def edge_constants():
    sel = np.zeros((128, 256), np.float32)
    for c in range(64):
        sel[c, 4 * c] = 1.0
        sel[64 + c, 4 * c + 3] = 1.0
    return (jnp.asarray(sel, BF),)


def split2(a):
    high = a.astype(BF)
    return high, (a - high.astype(F32)).astype(BF)


def boxed_stats(stats, up, down):
    blank = jnp.zeros((1, 256), F32)
    sums = [blank] + [stats[y : y + 1] for y in range(4)] + [blank]
    sqs = [blank] + [stats[4 + y : 5 + y] for y in range(4)] + [blank]
    if up is not None:
        for at, halo in ((0, up.astype(F32)), (5, down.astype(F32))):
            sums[at] = jnp.sum(halo, 0, keepdims=True)
            sqs[at] = jnp.sum(halo * halo, 0, keepdims=True)
    tall = jnp.concatenate(
        [v[y] + v[y + 1] + v[y + 2] for v in (sums, sqs) for y in range(4)], axis=0
    )
    boxed = (tall + pltpu.roll(tall, 255, 1) + pltpu.roll(tall, 254, 1)) * (1.0 / 576.0)
    mean = boxed[0:4]
    return mean, lax.rsqrt(boxed[4:8] - mean * mean + 1e-5)


PART = 8
PACKED = 136
FIRST = 3


def pick(idx, features, blocks):
    count = idx.shape[0]
    images, channels, rows, _ = features.shape

    def kernel(idx_ref, features_ref, out_ref, strips, in_sem, out_sem):
        def read(k):
            return pltpu.make_async_copy(
                features_ref.at[k, :, :, pl.ds(0, 128 * blocks)], strips.at[k], in_sem.at[k]
            )

        def write(s, j):
            return pltpu.make_async_copy(
                strips.at[idx_ref[s], :, :, pl.ds(128 * j, 128)], out_ref.at[s, j], out_sem.at[s, j]
            )

        for k in range(images):
            read(k).start()
        for k in range(images):
            read(k).wait()
        for s in range(count):
            for j in range(blocks):
                write(s, j).start()
        for s in range(count):
            for j in range(blocks):
                write(s, j).wait()

    out = pl.pallas_call(
        kernel,
        grid_spec=pltpu.PrefetchScalarGridSpec(
            num_scalar_prefetch=1,
            grid=(1,),
            in_specs=[pl.BlockSpec(memory_space=pl.ANY)],
            out_specs=pl.BlockSpec(memory_space=pl.ANY),
            scratch_shapes=[
                pltpu.VMEM((images, channels, rows, 128 * blocks), BF),
                pltpu.SemaphoreType.DMA((images,)),
                pltpu.SemaphoreType.DMA((count, blocks)),
            ],
        ),
        out_shape=jax.ShapeDtypeStruct((count, blocks, channels, rows, 128), BF),
        compiler_params=PARAMS,
        cost_estimate=pl.CostEstimate(
            flops=0, bytes_accessed=count * blocks * 131072, transcendentals=0
        ),
        name="pick",
    )(idx, features)
    return out.reshape(count, blocks, channels * rows, 128)


def pack_constants():
    spread = np.zeros((128, 256), np.float32)
    for i in range(64):
        spread[i, i] = 1.0
        spread[64 + i, 128 + i] = 1.0
    column = np.zeros((8, 128), np.float32)
    column[0, 64] = 1.0
    into = np.zeros((256, 128), np.float32)
    into[:, 64] = 1.0
    return tuple(jnp.asarray(m, BF) for m in (spread, column, into, np.eye(256)))


def pack_kernel(idx_ref, *refs):
    whole, part = refs[:PART], refs[PART : 2 * PART]
    spread_ref, column_ref, out_ref = refs[2 * PART :]
    for g in range(PART):
        out_ref[g, 0:256, :] = whole[g][0, 0]
        block = part[g][0, 0]
        out_ref[g, 256:384, :] = (
            dot_nt(block[0:128], spread_ref[:, 0:128]) + dot_nt(block[128:256], spread_ref[:, 128:])
        ).astype(BF)
        line = dot_nt(column_ref[...], block)
        out_ref[g, 384:392, :] = jnp.concatenate(
            [line[0:1, 0:128], line[0:1, 128:256], jnp.zeros((6, 128), F32)], axis=0
        ).astype(BF)


def pack(idx, own):
    count = idx.shape[0]
    spread, column, _, _ = pack_constants()

    def chosen(g, j):
        return lambda k, s: (s[PART * k + g], j, 0, 0)

    return pl.pallas_call(
        pack_kernel,
        grid_spec=pltpu.PrefetchScalarGridSpec(
            num_scalar_prefetch=1,
            grid=(count // PART,),
            in_specs=[
                pl.BlockSpec((1, 1, 256, 128), chosen(g, j))
                for j in (FIRST, FIRST + 1)
                for g in range(PART)
            ]
            + [
                pl.BlockSpec((128, 256), lambda k, s: (0, 0)),
                pl.BlockSpec((8, 128), lambda k, s: (0, 0)),
            ],
            out_specs=pl.BlockSpec((PART, 256 + PACKED, 128), lambda k, s: (k, 0, 0)),
        ),
        out_shape=jax.ShapeDtypeStruct((count, 256 + PACKED, 128), BF),
        compiler_params=PARAMS,
        name="pack",
    )(idx, *[own] * (2 * PART), spread, column)


def block_edges(block, sel_ref):
    rows = dot(sel_ref[...], block).astype(BF)
    value = block.astype(F32).reshape(32, 8, 128)
    total = jnp.sum(value, 0)
    square = jnp.sum(value * value, 0)
    stats = jnp.concatenate([total[0:4] + total[4:8], square[0:4] + square[4:8]], axis=0)
    return rows[0:64], rows[64:128], stats


def edge_kernel(slot_ref, *refs):
    blocks, (sel_ref, head_ref, tail_ref, stats_ref, *kept) = refs[:PART], refs[PART:]
    for g in range(PART):
        if kept:
            kept[0][g, 0] = blocks[g][0, blocks[g].shape[1] - 1]
        for j in range(stats_ref.shape[1]):
            head, tail, stats = block_edges(blocks[g][0, j], sel_ref)
            head_ref[g, j] = head
            tail_ref[g, j] = tail
            stats_ref[g, j] = stats


def unpack_kernel(slot_ref, *refs):
    packed = refs[:PART]
    (
        spread_ref, into_ref, eye_ref, sel_ref, head_ref, tail_ref, stats_ref, block_ref,
    ) = refs[PART:]
    for g in range(PART):
        wide = dot(packed[g][0, 256:384, :], spread_ref[...])
        line = packed[g][0, 384:392, :]
        line = jnp.concatenate([line[0:1], line[1:2]], axis=1)
        column = dot(eye_ref[...] * line, into_ref[...])
        block = jnp.concatenate([wide[:, :128], wide[:, 128:]], axis=0) + column
        blocks = (packed[g][0, 0:256, :], block.astype(BF))
        for j in range(2):
            block_ref[g, j] = blocks[j]
            head, tail, stats = block_edges(blocks[j], sel_ref)
            head_ref[g, j] = head
            tail_ref[g, j] = tail
            stats_ref[g, j] = stats


def edge_outputs(images, blocks):
    specs = [
        pl.BlockSpec((PART, blocks, 64, 128), lambda k, s: (k, 0, 0, 0)),
        pl.BlockSpec((PART, blocks, 64, 128), lambda k, s: (k, 0, 0, 0)),
        pl.BlockSpec((PART, blocks, 8, 128), lambda k, s: (k, 0, 0, 0)),
    ]
    shapes = [
        jax.ShapeDtypeStruct((images, blocks, 64, 128), BF),
        jax.ShapeDtypeStruct((images, blocks, 64, 128), BF),
        jax.ShapeDtypeStruct((images, blocks, 8, 128), F32),
    ]
    return specs, shapes


def whole_spec(a):
    return pl.BlockSpec(a.shape, lambda k, s: (0,) * a.ndim)


def edges(slot, recv, keep_last):
    images, blocks = slot.shape[0], recv.shape[1]
    constants = edge_constants()
    specs, shapes = edge_outputs(images, blocks)
    if keep_last:
        specs = specs + [pl.BlockSpec((PART, 1, 256, 128), lambda k, s: (k, 0, 0, 0))]
        shapes = shapes + [jax.ShapeDtypeStruct((images, 1, 256, 128), BF)]

    def by_slot(g):
        return lambda k, s: (s[PART * k + g], 0, 0, 0)

    return pl.pallas_call(
        edge_kernel,
        grid_spec=pltpu.PrefetchScalarGridSpec(
            num_scalar_prefetch=1,
            grid=(images // PART,),
            in_specs=[pl.BlockSpec((1, blocks, 256, 128), by_slot(g)) for g in range(PART)]
            + [whole_spec(a) for a in constants],
            out_specs=specs,
        ),
        out_shape=shapes,
        cost_estimate=pl.CostEstimate(
            flops=images * blocks * 20_000_000, bytes_accessed=images * blocks * 100_000,
            transcendentals=0,
        ),
        compiler_params=PARAMS,
        name="edges",
    )(slot, *[recv] * PART, *constants)


def unpack(slot, packed):
    images = slot.shape[0]
    spread, _, into, eye = pack_constants()
    constants = (spread, into, eye) + edge_constants()
    specs, shapes = edge_outputs(images, 2)

    def by_slot(g):
        return lambda k, s: (s[PART * k + g], 0, 0)

    return pl.pallas_call(
        unpack_kernel,
        grid_spec=pltpu.PrefetchScalarGridSpec(
            num_scalar_prefetch=1,
            grid=(images // PART,),
            in_specs=[pl.BlockSpec((1, 256 + PACKED, 128), by_slot(g)) for g in range(PART)]
            + [whole_spec(a) for a in constants],
            out_specs=specs + [pl.BlockSpec((PART, 2, 256, 128), lambda k, s: (k, 0, 0, 0))],
        ),
        out_shape=shapes + [jax.ShapeDtypeStruct((images, 2, 256, 128), BF)],
        compiler_params=SMALL,
        name="unpack",
    )(slot, *[packed] * PART, *constants)


def prepare_kernel(
    own_ref, up_ref, up_last_ref, down_ref, down_last_ref, stat_ref, index_ref, rev_ref, flip_ref, own_out, edge_out, table_out
):
    mean_inv = 24.0 * LOG2E
    for n in range(STEPS):
        block = jnp.concatenate([own_ref[0, n], own_ref[0, n + 1]], axis=1)
        final = n + 1 == STEPS
        up = jnp.concatenate([up_ref[0, n], up_last_ref[0] if final else up_ref[0, n + 1]], axis=1)
        down = jnp.concatenate(
            [down_ref[0, n], down_last_ref[0] if final else down_ref[0, n + 1]], axis=1
        )
        own_out[0, n] = dot_nt(rev_ref[...], block).astype(BF)
        edge_out[0, n] = dot_nt(rev_ref[...], jnp.concatenate([up, down], axis=0)).astype(BF)
        stats = jnp.concatenate([stat_ref[0, n], stat_ref[0, n + 1]], axis=1)
        mean, inv = boxed_stats(stats, up, down)
        scaled = inv * mean_inv
        both = jnp.concatenate([scaled * (1.0 / 576.0), scaled * mean], axis=0)[:, :128]
        high = both.astype(BF).astype(F32)
        mid = (both - high).astype(BF).astype(F32)
        index = index_ref[0, :, 128 * n : 128 * n + 128].astype(F32)
        rows = jnp.concatenate(
            [high, mid, both - high - mid, index, jnp.zeros((4, 128), F32)], axis=0
        ).astype(BF)
        blank = jnp.zeros((64, 64), F32)
        left = dot_nt(flip_ref[0:64, :], rows)
        right = dot_nt(flip_ref[64:128, :], rows)
        table_out[0, n] = jnp.concatenate([left, right, blank], axis=1).astype(BF)


def prepare(own, up, up_last, down, down_last, stats, depth_index):
    images, blocks = own.shape[0], own.shape[1]
    return pl.pallas_call(
        prepare_kernel,
        grid=(images,),
        in_specs=[
            pl.BlockSpec((1, blocks, 256, 128), lambda k: (k, 0, 0, 0)),
            pl.BlockSpec((1, STEPS, 64, 128), lambda k: (k, 0, 0, 0)),
            pl.BlockSpec((1, 64, 128), lambda k: (k, 0, 0)),
            pl.BlockSpec((1, STEPS, 64, 128), lambda k: (k, 0, 0, 0)),
            pl.BlockSpec((1, 64, 128), lambda k: (k, 0, 0)),
            pl.BlockSpec((1, blocks, 8, 128), lambda k: (k, 0, 0, 0)),
            pl.BlockSpec((1, 4, 512), lambda k: (k, 0, 0)),
            pl.BlockSpec((WIN, 256), lambda k: (0, 0)),
            pl.BlockSpec((128, 128), lambda k: (0, 0)),
        ],
        out_specs=[
            pl.BlockSpec((1, STEPS, WIN, 256), lambda k: (k, 0, 0, 0)),
            pl.BlockSpec((1, STEPS, WIN, 128), lambda k: (k, 0, 0, 0)),
            pl.BlockSpec((1, STEPS, 64, 128), lambda k: (k, 0, 0, 0)),
        ],
        out_shape=[
            jax.ShapeDtypeStruct((images, STEPS, WIN, 256), BF),
            jax.ShapeDtypeStruct((images, STEPS, WIN, 128), BF),
            jax.ShapeDtypeStruct((images, STEPS, 64, 128), BF),
        ],
        cost_estimate=pl.CostEstimate(
            flops=images * STEPS * 40_000_000, bytes_accessed=images * 1_000_000, transcendentals=0
        ),
        compiler_params=PARAMS,
        name="prepare",
    )(own, up, up_last, down, down_last, stats, depth_index, reversal(), flips())


def skewed(left, right, column, lane, shift):
    return pltpu.roll(jnp.where(lane < column, right, left), shift, 1, stride=1, stride_axis=0)


def sweep_kernel(group, ys, halo, late, *refs):
    refs = list(refs[1:])

    def take(count):
        out = refs[:count]
        del refs[:count]
        return out

    count = len(ys)
    block_refs = take(3) if late else (take(group), take(group))
    own_ref, table_ref, pat_ref, mask_ref, w2_ref, flip_ref, elev_ref, cell_ref = take(8)

    def joined(three, g):
        if late:
            early, before, after = three
            near = jnp.where(pl.program_id(0) == 0, early[g, 0], before[g, 0])
        else:
            near, after = three[0][g, 0], three[1]
        return jnp.concatenate([near, after[g, 0]], axis=1)

    width = 3 if late else 2
    stat_refs = take(width)
    up_refs = take(width) if halo else None
    down_refs = take(width) if halo else None
    edge_ref = take(1)[0] if halo else None
    mean_ref, rows_ref, skew = refs

    column = 63 - lax.broadcasted_iota(jnp.int32, (64, 128), 0)
    lane = lax.broadcasted_iota(jnp.int32, (64, 128), 1)
    wrapped = lane < column
    first = lane < column + 64
    column8 = 7 - lax.broadcasted_iota(jnp.int32, (8, 128), 0)
    lane8 = lax.broadcasted_iota(jnp.int32, (8, 128), 1)
    hyp = (lane % 64).astype(F32)
    tables = dot(table_ref[:, 0].reshape(group * 64, 128), pat_ref[...])

    soft = []
    chosen = []
    for g in range(group):
        if late:
            rhs = joined(block_refs, g)
        else:
            rhs = jnp.concatenate([block_refs[0][g][0, 0], block_refs[1][g][0, 0]], axis=1)
        stats = joined(stat_refs, g)
        if halo:
            up = joined(up_refs, g)
            down = joined(down_refs, g)
            rhs = jnp.concatenate([rhs, up, down], axis=0)
            sides = edge_ref[g, 0]
        else:
            up = down = None
        mean_b, inv_b = boxed_stats(stats, up, down)
        own = own_ref[g, 0]
        masked = jnp.concatenate([own * mask_ref[y : y + 1, :] for y in ys], axis=0)
        if halo:
            sides = jnp.concatenate([sides * mask_ref[8 + y : 9 + y, 0:128] for y in ys], axis=0)
            masked = jnp.concatenate([masked, sides], axis=1)
        product = dot(masked, rhs)
        for i, y in enumerate(ys):
            p = product[WIN * i : WIN * i + WIN]
            z = jnp.where(
                wrapped, p[16:80, 128:], jnp.where(first, p[80:144, :128], p[16:80, :128])
            )
            z8 = jnp.where(
                lane8 < column8,
                p[72:80, 128:],
                jnp.where(lane8 < column8 + 64, p[8:16, 128:], p[72:80, :128]),
            )
            at = count * g + i
            skew[at, 0:8, :] = pltpu.roll(z8, 57, 1, stride=1, stride_axis=0)
            skew[at, 8:72, :] = pltpu.roll(z, 65, 1, stride=1, stride_axis=0)
            cross = skew[at, 8:72, :] + skew[at, 7:71, :] + skew[at, 6:70, :]
            mb = skewed(mean_b[y : y + 1, :128], mean_b[y : y + 1, 128:], column, lane, 65)
            rb = skewed(inv_b[y : y + 1, :128], inv_b[y : y + 1, 128:], column, lane, 65)
            a1, a2, index = (
                tables[64 * g : 64 * g + 64, (3 * i + q) * 128 : (3 * i + q + 1) * 128]
                for q in range(3)
            )
            weight = jnp.exp2((cross * a1 - a2 * mb) * rb)
            picked = jnp.where(index == hyp, weight, 0.0)
            soft.append(jnp.concatenate(split2(weight), axis=1))
            chosen.append(jnp.concatenate(split2(picked), axis=1))
    soft = jnp.concatenate(soft, axis=0)
    chosen = jnp.concatenate(chosen, axis=0)
    r = dot_nt(w2_ref[...], soft)
    rc = dot_nt(w2_ref[...], chosen)
    inv = 1.0 / r[0:2]
    both = jnp.concatenate([(r[2:4] + r[4:6] + r[6:8]) * inv, rc[0:2] * inv], axis=0)
    pieces = group * count // 2
    both = jnp.concatenate([both[:, 128 * v : 128 * v + 128] for v in range(pieces)], axis=0)
    high = both.astype(BF)
    rest = both - high.astype(F32)
    mid = rest.astype(BF)
    low = (rest - mid.astype(F32)).astype(BF)
    both = dot(jnp.concatenate([high, mid, low], axis=0), flip_ref[...])
    both = both[0 : 4 * pieces] + both[4 * pieces : 8 * pieces] + both[8 * pieces :]
    turned = pltpu.roll(both, 64, 1)
    left = lax.broadcasted_iota(jnp.int32, (1, 128), 1) < 64
    cell_iota = lax.broadcasted_iota(jnp.int32, (128, 128), 0)
    blank = jnp.zeros((4, 128), F32)
    for g in range(group):
        for i in range(0, count, 2):
            lines = []
            hots = []
            for j, y in enumerate(ys[i : i + 2]):
                at = (count * g + i) // 2 * 4
                lo, hi = (both, turned) if j == 0 else (turned, both)
                mean = jnp.where(left, lo[at : at + 1], hi[at + 1 : at + 2])
                mean_ref[g, i + j : i + j + 1, :] = mean
                c = jnp.where(left, lo[at + 2 : at + 3], hi[at + 3 : at + 4])
                values = jnp.concatenate([c * elev_ref[g, y : y + 1, :], c], axis=0)
                value_hi = values.astype(BF).astype(F32)
                line = jnp.concatenate([value_hi, values - value_hi], axis=0)
                lines.append(jnp.concatenate([line, blank] if j == 0 else [blank, line], axis=1))
                hot = jnp.where(cell_iota == cell_ref[g, y : y + 1, :], 1.0, 0.0)
                hots.append(hot.astype(BF))
            binned = dot_nt(
                jnp.concatenate(lines, axis=0).astype(BF), jnp.concatenate(hots, axis=1)
            )
            for j in range(2):
                got = binned[4 * j : 4 * j + 2] + binned[4 * j + 2 : 4 * j + 4]
                at = count * g + i + j
                rows_ref[0, at : at + 1, 0:128] = got[0:1]
                rows_ref[0, at : at + 1, 128:256] = got[1:2]


def sweep_steps(
    first, steps, ys, group, slot, blocks, stats, ups, downs, own, edge, table, w2, elev, cell, late
):
    images = own.shape[0]
    halo = ups is not None
    count = len(ys)

    def slot_block(g, j):
        return lambda n, k, s: (s[group * k + g], n + first + j, 0, 0)

    def near(n, k, s):
        return (k, n + first, 0, 0)

    def whole(n, k, s):
        return (0, 0)

    def pixels(n, k, s):
        return (k, 0, n + first)

    def pair_specs(rows, kept=FIRST - 1):
        if late:
            maps = (
                lambda n, k, s: (k, kept, 0, 0),
                lambda n, k, s: (k, 0, 0, 0),
                lambda n, k, s: (k, n, 0, 0),
            )
        else:
            maps = (near, lambda n, k, s: (k, n + first + 1, 0, 0))
        return [pl.BlockSpec((group, 1, rows, 128), m) for m in maps]

    def pair_args(arrays):
        return [arrays[0], arrays[1], arrays[1]] if late else [arrays[0], arrays[0]]

    if late:
        in_specs = pair_specs(256, 0)
        args = pair_args(blocks)
    else:
        in_specs = [
            pl.BlockSpec((1, 1, 256, 128), slot_block(g, j)) for j in range(2) for g in range(group)
        ]
        args = [blocks] * (2 * group)
    in_specs += [
        pl.BlockSpec((group, 1, WIN, 256), near),
        pl.BlockSpec((group, 1, 64, 128), near),
        pl.BlockSpec((128, 3 * 128 * count), whole),
        pl.BlockSpec((16, 256), whole),
        pl.BlockSpec((8, 256), whole),
        pl.BlockSpec((128, 128), whole),
        pl.BlockSpec((group, 4, 128), pixels),
        pl.BlockSpec((group, 4, 128), pixels),
    ] + pair_specs(8)
    args += [
        own, table, table_patterns(ys), row_masks(), w2, flips(), elev, cell,
    ] + pair_args(stats)
    if halo:
        in_specs += pair_specs(64) + pair_specs(64) + [pl.BlockSpec((group, 1, WIN, 128), near)]
        args += pair_args(ups) + pair_args(downs) + [edge]
    work = steps * images * count // 4
    return pl.pallas_call(
        functools.partial(sweep_kernel, group, ys, halo, late),
        grid_spec=pltpu.PrefetchScalarGridSpec(
            num_scalar_prefetch=1,
            grid=(steps, images // group),
            in_specs=in_specs,
            out_specs=[
                pl.BlockSpec((group, count, 128), lambda n, k, s: (k, 0, n)),
                pl.BlockSpec((1, count * group, 256), lambda n, k, s: (n, k, 0)),
            ],
            scratch_shapes=[pltpu.VMEM((count * group, 72, 128), F32)],
        ),
        out_shape=[
            jax.ShapeDtypeStruct((images, count, steps * 128), F32),
            jax.ShapeDtypeStruct((steps, images * count, 256), F32),
        ],
        compiler_params=PARAMS,
        cost_estimate=pl.CostEstimate(
            flops=work * 200_000_000, bytes_accessed=work * 400_000, transcendentals=0
        ),
        name="sweep",
    )(slot, *args)


def depth_weights(planes):
    high = lax.reduce_precision(planes, 8, 7)
    mid = lax.reduce_precision(planes - high, 8, 7)
    zero = jnp.zeros_like(planes)
    rows = []
    for v in (jnp.ones_like(planes), high, mid, planes - high - mid):
        rows.append(jnp.concatenate([v, zero]))
        rows.append(jnp.concatenate([zero, v]))
    w = jnp.stack(rows)
    return jnp.concatenate([w, w], axis=1).astype(BF)


def collect_kernel(list_ref, count_ref, a_ref, b_ref, c_ref, d_ref, out_ref, rows):
    at = 0
    for part in (a_ref, b_ref, c_ref, d_ref):
        for n in range(part.shape[0]):
            rows[at : at + part.shape[1], :] = part[n]
            at += part.shape[1]
    for o in range(out_ref.shape[0]):

        def move(step, carry):
            for i in range(8):
                e = step * 8 + i
                out_ref[o, pl.ds(e, 1), :] = rows[pl.ds(list_ref[o, e], 1), :]
            return carry

        lax.fori_loop(0, (count_ref[o] + 7) // 8, move, 0)


def collect(row_list, counts, parts):
    owners, cap = row_list.shape
    total = sum(p.shape[0] * p.shape[1] for p in parts)
    return pl.pallas_call(
        collect_kernel,
        grid_spec=pltpu.PrefetchScalarGridSpec(
            num_scalar_prefetch=2,
            grid=(1,),
            in_specs=[pl.BlockSpec(p.shape, lambda i, a, b: (0, 0, 0)) for p in parts],
            out_specs=pl.BlockSpec((owners, cap, 2 * CELLS), lambda i, a, b: (0, 0, 0)),
            scratch_shapes=[pltpu.VMEM((total, 2 * CELLS), F32)],
        ),
        out_shape=jax.ShapeDtypeStruct((owners, cap, 2 * CELLS), F32),
        compiler_params=SMALL,
        name="collect",
    )(row_list, counts, *parts)


def place_kernel(slot_ref, count_ref, got_ref, out_ref):
    out_ref[...] = jnp.zeros_like(out_ref)
    for t in range(got_ref.shape[0]):
        count = count_ref[t]

        def add(step, carry):
            for i in range(8):
                e = step * 8 + i
                at = pl.ds(slot_ref[t, e], 1)
                row = jnp.where(e < count, got_ref[t, pl.ds(e, 1), :], 0.0)
                out_ref[at, :] = out_ref[at, :] + row
            return carry

        lax.fori_loop(0, (count + 7) // 8, add, 0)


def place(slots, counts, got, total):
    return pl.pallas_call(
        place_kernel,
        grid_spec=pltpu.PrefetchScalarGridSpec(
            num_scalar_prefetch=2,
            grid=(1,),
            in_specs=[pl.BlockSpec(got.shape, lambda i, a, b: (0, 0, 0))],
            out_specs=pl.BlockSpec((total, 2 * CELLS), lambda i, a, b: (0, 0)),
        ),
        out_shape=jax.ShapeDtypeStruct((total, 2 * CELLS), F32),
        compiler_params=SMALL,
        name="place",
    )(slots, counts, got)


def neighbour_rows(head, tail):
    count = lax.axis_size("tile")
    above = lax.ppermute(tail, "tile", [(i, i + 1) for i in range(count - 1)])
    below = lax.ppermute(head, "tile", [(i + 1, i) for i in range(count - 1)])
    return above, below


def on_device(
    features, partner_ids, depth_planes, cam_height, ray_down, depth_index, cell_index,
    block_list, block_slot, block_count,
):
    group_count = lax.axis_size("img")
    owners = lax.axis_size("tile")
    my_group = lax.axis_index("img")
    my_tile = lax.axis_index("tile")
    images = features.shape[0]
    table = partner_ids.reshape(group_count, images)
    source_of = table // images
    chosen = jnp.sum(jnp.where(source_of == my_group, table % images, 0), axis=1)
    slot = lax.dynamic_index_in_dim(source_of, my_group, 0, False)

    def exchange(a):
        return lax.all_to_all(a, "img", split_axis=0, concat_axis=0, tiled=True)

    main = exchange(pick(chosen, features, FIRST))

    every = jnp.arange(images, dtype=jnp.int32)
    own = pick(every, features, STEPS + 1)
    own_head, own_tail, own_stats = edges(every, own, False)
    own_up, own_down = neighbour_rows(own_head[:, :STEPS], own_tail[:, :STEPS])
    ends = [jnp.transpose(v[:, STEPS, :, :2], (0, 2, 1)).reshape(images, -1) for v in (own_head, own_tail)]
    ends = [v.reshape(images, 2, -1) for v in neighbour_rows(*ends)]
    up_last, down_last = (
        jnp.pad(jnp.transpose(v, (0, 2, 1)), ((0, 0), (0, 0), (0, 126))) for v in ends
    )
    own_turned, edge_turned, own_table = prepare(
        own, own_up, up_last, own_down, down_last, own_stats, depth_index
    )
    packed = pack(chosen, own)

    hyp = jnp.arange(NDEPTH, dtype=jnp.int32)[:, None, None, None]
    plane_at = jnp.sum(
        jnp.where(hyp == depth_index[None], depth_planes[:, None, None, None], 0.0), 0
    )
    elevation = cam_height[:, None, None] - ray_down * plane_at

    meta = jnp.concatenate(
        [block_slot[0, 0], jnp.broadcast_to(block_count[0, 0][:, None], (owners, 128))], axis=1
    )
    metas = [lax.dynamic_slice_in_dim(meta, my_tile, 1, 0)]
    for s in range(1, owners):
        mine = lax.dynamic_slice_in_dim(meta, (my_tile + s) % owners, 1, 0)
        metas.append(lax.ppermute(mine, "tile", [(i, (i + s) % owners) for i in range(owners)]))
    metas = jnp.concatenate(metas, axis=0)
    metas = jnp.take(metas, (my_tile - jnp.arange(owners)) % owners, axis=0)

    w2 = depth_weights(depth_planes)

    packed, own_turned, edge_turned, own_table, elevation, metas, w2 = lax.optimization_barrier(
        (packed, own_turned, edge_turned, own_table, elevation, metas, w2)
    )
    last = exchange(packed)
    head, tail, stats, early = edges(slot, main, True)
    up, down = neighbour_rows(head, tail)
    shared = (own_turned, edge_turned, own_table, w2, elevation, cell_index)
    shared = (own_turned, edge_turned, own_table, w2, elevation, cell_index)
    inner, outer = (1, 2), (0, 3)
    one = (stats,)
    mean_i, rows_i = sweep_steps(0, 2, inner, 16, slot, main, one, None, None, *shared, False)
    up, down, mean_i = lax.optimization_barrier((up, down, mean_i))
    mean_o, rows_o = sweep_steps(0, 2, outer, 16, slot, main, one, (up,), (down,), *shared, False)
    last, mean_o = lax.optimization_barrier((last, mean_o))
    head_l, tail_l, stats_l, late = unpack(slot, last)
    up_l, down_l = neighbour_rows(head_l, tail_l)
    blocks, both = (early, late), (stats, stats_l)
    mean_il, rows_il = sweep_steps(2, 2, inner, 16, slot, blocks, both, None, None, *shared, True)
    mean_ol, rows_ol = sweep_steps(
        2, 2, outer, 16, slot, blocks, both, (up, up_l), (down, down_l), *shared, True
    )
    mean_i = jnp.concatenate([mean_i, mean_il], axis=2)
    mean_o = jnp.concatenate([mean_o, mean_ol], axis=2)
    mean_range = jnp.concatenate([mean_o[:, 0:1], mean_i, mean_o[:, 1:2]], axis=1)

    lists = block_list[0, 0]
    n, r, k = lists % STEPS, lists // STEPS % 4, lists // (4 * STEPS)
    inside = (r == 1) | (r == 2)
    row_list = 2 * images * n + 2 * k + jnp.where(inside, r - 1, 8 * images + r // 3)
    send = collect(row_list, block_count[0, 0], (rows_i, rows_il, rows_o, rows_ol))
    got = lax.all_to_all(send, "tile", split_axis=0, concat_axis=0, tiled=True)
    dense = place(metas[:, :128], metas[:, 128], got, group_count * PATCH_DEV)
    parts = exchange(dense.reshape(group_count, PATCH_DEV, 2 * CELLS))
    total = jnp.sum(parts, axis=0)
    return mean_range, total[:, :CELLS] / (total[:, CELLS:] + 1.0)


def solution(mesh):
    return jax.shard_map(
        on_device,
        mesh=mesh,
        in_specs=(
            P("img", None, "tile", None),
            P(),
            P(),
            P("img"),
            P("img", "tile", None),
            P("img", "tile", None),
            P("img", "tile", None),
            P("img", "tile", None, None),
            P("img", "tile", None, None),
            P("img", "tile", None),
        ),
        out_specs=(P("img", "tile", None), P(("img", "tile"), None)),
        check_vma=False,
    )
```

```python
import functools
import math

import numpy as np
import jax
import jax.numpy as jnp
from jax import lax
from jax.experimental import pallas as pl
from jax.experimental.pallas import tpu as pltpu
from jax.sharding import PartitionSpec as P

NDEPTH = 64
CELLS = 128
PATCH_DEV = 16
STEPS = 4
WIN = 144
LOG2E = math.log2(math.e)
BF = jnp.bfloat16
F32 = jnp.float32
NT = (((1,), (1,)), ((), ()))
PARAMS = pltpu.CompilerParams(vmem_limit_bytes=60 * 1024 * 1024)
LATE = pltpu.CompilerParams(vmem_limit_bytes=40 * 1024 * 1024)
SMALL = pltpu.CompilerParams(vmem_limit_bytes=24 * 1024 * 1024)


def dot(a, b):
    return jnp.dot(a, b, preferred_element_type=F32)


def dot_nt(a, b):
    return lax.dot_general(a, b, NT, preferred_element_type=F32)


def table_patterns(ys):
    pat = np.zeros((128, 3 * len(ys), 128), np.float32)
    for half in range(2):
        lanes = slice(64 * half, 64 * half + 64)
        for i, y in enumerate(ys):
            for q in range(2):
                for s in range(3):
                    pat[half * 32 + s * 8 + q * 4 + y, i * 3 + q, lanes] = 1.0
            pat[half * 32 + 24 + y, i * 3 + 2, lanes] = 1.0
    return jnp.asarray(pat.reshape(128, -1), BF)


def row_masks():
    masks = np.zeros((16, 256), np.float32)
    for y in range(4):
        masks[y] = np.abs(np.arange(256) % 4 - y) <= 1
    masks[8, 0:64] = 1.0
    masks[11, 64:128] = 1.0
    return jnp.asarray(masks, BF)


def flips():
    m = np.zeros((128, 128), np.float32)
    for i in range(128):
        m[i, i // 64 * 64 + 63 - i % 64] = 1.0
    return jnp.asarray(m, BF)


def reversal():
    m = np.zeros((WIN, 256), np.float32)
    for i in range(WIN):
        m[i, WIN - 1 - i] = 1.0
    return jnp.asarray(m, BF)


def edge_constants():
    sel = np.zeros((128, 256), np.float32)
    for c in range(64):
        sel[c, 4 * c] = 1.0
        sel[64 + c, 4 * c + 3] = 1.0
    return (jnp.asarray(sel, BF),)


def split2(a):
    high = a.astype(BF)
    return high, (a - high.astype(F32)).astype(BF)


def boxed_stats(stats, up, down):
    blank = jnp.zeros((1, 256), F32)
    sums = [blank] + [stats[y : y + 1] for y in range(4)] + [blank]
    sqs = [blank] + [stats[4 + y : 5 + y] for y in range(4)] + [blank]
    if up is not None:
        for at, halo in ((0, up.astype(F32)), (5, down.astype(F32))):
            sums[at] = jnp.sum(halo, 0, keepdims=True)
            sqs[at] = jnp.sum(halo * halo, 0, keepdims=True)
    tall = jnp.concatenate(
        [v[y] + v[y + 1] + v[y + 2] for v in (sums, sqs) for y in range(4)], axis=0
    )
    boxed = (tall + pltpu.roll(tall, 255, 1) + pltpu.roll(tall, 254, 1)) * (1.0 / 576.0)
    mean = boxed[0:4]
    return mean, lax.rsqrt(boxed[4:8] - mean * mean + 1e-5)


PART = 8
PACKED = 136
PARTS = 4
FIRST = 3


def pick(idx, features, blocks):
    count = idx.shape[0]
    images, channels, rows, _ = features.shape

    def kernel(idx_ref, features_ref, out_ref, strips, in_sem, out_sem):
        def read(k):
            return pltpu.make_async_copy(
                features_ref.at[k, :, :, pl.ds(0, 128 * blocks)], strips.at[k], in_sem.at[k]
            )

        def write(s, j):
            return pltpu.make_async_copy(
                strips.at[idx_ref[s], :, :, pl.ds(128 * j, 128)], out_ref.at[s, j], out_sem.at[s, j]
            )

        for k in range(images):
            read(k).start()
        part = images // PARTS
        for q in range(PARTS):
            for k in range(q * part, (q + 1) * part):
                read(k).wait()
            for s in range(count):

                @pl.when(idx_ref[s] // part == q)
                def _():
                    for j in range(blocks):
                        write(s, j).start()

        for s in range(count):
            for j in range(blocks):
                write(s, j).wait()

    out = pl.pallas_call(
        kernel,
        grid_spec=pltpu.PrefetchScalarGridSpec(
            num_scalar_prefetch=1,
            grid=(1,),
            in_specs=[pl.BlockSpec(memory_space=pl.ANY)],
            out_specs=pl.BlockSpec(memory_space=pl.ANY),
            scratch_shapes=[
                pltpu.VMEM((images, channels, rows, 128 * blocks), BF),
                pltpu.SemaphoreType.DMA((images,)),
                pltpu.SemaphoreType.DMA((count, blocks)),
            ],
        ),
        out_shape=jax.ShapeDtypeStruct((count, blocks, channels, rows, 128), BF),
        compiler_params=PARAMS,
        cost_estimate=pl.CostEstimate(
            flops=0, bytes_accessed=count * blocks * 131072, transcendentals=0
        ),
        name="pick",
    )(idx, features)
    return out.reshape(count, blocks, channels * rows, 128)


def pack_constants():
    spread = np.zeros((128, 256), np.float32)
    for i in range(64):
        spread[i, i] = 1.0
        spread[64 + i, 128 + i] = 1.0
    column = np.zeros((8, 128), np.float32)
    column[0, 64] = 1.0
    into = np.zeros((256, 128), np.float32)
    into[:, 64] = 1.0
    return tuple(jnp.asarray(m, BF) for m in (spread, column, into, np.eye(256)))


def pack_kernel(idx_ref, *refs):
    whole, part = refs[:PART], refs[PART : 2 * PART]
    spread_ref, column_ref, out_ref = refs[2 * PART :]
    for g in range(PART):
        out_ref[g, 0:256, :] = whole[g][0, 0]
        block = part[g][0, 0]
        out_ref[g, 256:384, :] = (
            dot_nt(block[0:128], spread_ref[:, 0:128]) + dot_nt(block[128:256], spread_ref[:, 128:])
        ).astype(BF)
        line = dot_nt(column_ref[...], block)
        out_ref[g, 384:392, :] = jnp.concatenate(
            [line[0:1, 0:128], line[0:1, 128:256], jnp.zeros((6, 128), F32)], axis=0
        ).astype(BF)


def pack(idx, own):
    count = idx.shape[0]
    spread, column, _, _ = pack_constants()

    def chosen(g, j):
        return lambda k, s: (s[PART * k + g], j, 0, 0)

    return pl.pallas_call(
        pack_kernel,
        grid_spec=pltpu.PrefetchScalarGridSpec(
            num_scalar_prefetch=1,
            grid=(count // PART,),
            in_specs=[
                pl.BlockSpec((1, 1, 256, 128), chosen(g, j))
                for j in (FIRST, FIRST + 1)
                for g in range(PART)
            ]
            + [
                pl.BlockSpec((128, 256), lambda k, s: (0, 0)),
                pl.BlockSpec((8, 128), lambda k, s: (0, 0)),
            ],
            out_specs=pl.BlockSpec((PART, 256 + PACKED, 128), lambda k, s: (k, 0, 0)),
        ),
        out_shape=jax.ShapeDtypeStruct((count, 256 + PACKED, 128), BF),
        compiler_params=PARAMS,
        name="pack",
    )(idx, *[own] * (2 * PART), spread, column)


def block_edges(block, sel_ref):
    rows = dot(sel_ref[...], block).astype(BF)
    value = block.astype(F32).reshape(32, 8, 128)
    total = jnp.sum(value, 0)
    square = jnp.sum(value * value, 0)
    stats = jnp.concatenate([total[0:4] + total[4:8], square[0:4] + square[4:8]], axis=0)
    return rows[0:64], rows[64:128], stats


def edge_kernel(slot_ref, *refs):
    blocks, (sel_ref, head_ref, tail_ref, stats_ref, *kept) = refs[:PART], refs[PART:]
    for g in range(PART):
        if kept:
            kept[0][g, 0] = blocks[g][0, blocks[g].shape[1] - 1]
        for j in range(stats_ref.shape[1]):
            head, tail, stats = block_edges(blocks[g][0, j], sel_ref)
            head_ref[g, j] = head
            tail_ref[g, j] = tail
            stats_ref[g, j] = stats


def unpack_kernel(slot_ref, *refs):
    packed = refs[:PART]
    (
        spread_ref, into_ref, eye_ref, sel_ref, head_ref, tail_ref, stats_ref, block_ref,
    ) = refs[PART:]
    for g in range(PART):
        wide = dot(packed[g][0, 256:384, :], spread_ref[...])
        line = packed[g][0, 384:392, :]
        line = jnp.concatenate([line[0:1], line[1:2]], axis=1)
        column = dot(eye_ref[...] * line, into_ref[...])
        block = jnp.concatenate([wide[:, :128], wide[:, 128:]], axis=0) + column
        blocks = (packed[g][0, 0:256, :], block.astype(BF))
        for j in range(2):
            block_ref[g, j] = blocks[j]
            head, tail, stats = block_edges(blocks[j], sel_ref)
            head_ref[g, j] = head
            tail_ref[g, j] = tail
            stats_ref[g, j] = stats


def edge_outputs(images, blocks):
    specs = [
        pl.BlockSpec((PART, blocks, 64, 128), lambda k, s: (k, 0, 0, 0)),
        pl.BlockSpec((PART, blocks, 64, 128), lambda k, s: (k, 0, 0, 0)),
        pl.BlockSpec((PART, blocks, 8, 128), lambda k, s: (k, 0, 0, 0)),
    ]
    shapes = [
        jax.ShapeDtypeStruct((images, blocks, 64, 128), BF),
        jax.ShapeDtypeStruct((images, blocks, 64, 128), BF),
        jax.ShapeDtypeStruct((images, blocks, 8, 128), F32),
    ]
    return specs, shapes


def whole_spec(a):
    return pl.BlockSpec(a.shape, lambda k, s: (0,) * a.ndim)


def edges(slot, recv, keep_last):
    images, blocks = slot.shape[0], recv.shape[1]
    constants = edge_constants()
    specs, shapes = edge_outputs(images, blocks)
    if keep_last:
        specs = specs + [pl.BlockSpec((PART, 1, 256, 128), lambda k, s: (k, 0, 0, 0))]
        shapes = shapes + [jax.ShapeDtypeStruct((images, 1, 256, 128), BF)]

    def by_slot(g):
        return lambda k, s: (s[PART * k + g], 0, 0, 0)

    return pl.pallas_call(
        edge_kernel,
        grid_spec=pltpu.PrefetchScalarGridSpec(
            num_scalar_prefetch=1,
            grid=(images // PART,),
            in_specs=[pl.BlockSpec((1, blocks, 256, 128), by_slot(g)) for g in range(PART)]
            + [whole_spec(a) for a in constants],
            out_specs=specs,
        ),
        out_shape=shapes,
        cost_estimate=pl.CostEstimate(
            flops=images * blocks * 20_000_000, bytes_accessed=images * blocks * 100_000,
            transcendentals=0,
        ),
        compiler_params=PARAMS,
        name="edges",
    )(slot, *[recv] * PART, *constants)


def unpack(slot, packed):
    images = slot.shape[0]
    spread, _, into, eye = pack_constants()
    constants = (spread, into, eye) + edge_constants()
    specs, shapes = edge_outputs(images, 2)

    def by_slot(g):
        return lambda k, s: (s[PART * k + g], 0, 0)

    return pl.pallas_call(
        unpack_kernel,
        grid_spec=pltpu.PrefetchScalarGridSpec(
            num_scalar_prefetch=1,
            grid=(images // PART,),
            in_specs=[pl.BlockSpec((1, 256 + PACKED, 128), by_slot(g)) for g in range(PART)]
            + [whole_spec(a) for a in constants],
            out_specs=specs + [pl.BlockSpec((PART, 2, 256, 128), lambda k, s: (k, 0, 0, 0))],
        ),
        out_shape=shapes + [jax.ShapeDtypeStruct((images, 2, 256, 128), BF)],
        compiler_params=SMALL,
        name="unpack",
    )(slot, *[packed] * PART, *constants)


def prepare_kernel(
    own_ref, up_ref, up_last_ref, down_ref, down_last_ref, stat_ref, index_ref, rev_ref, flip_ref, own_out, edge_out, table_out
):
    mean_inv = 24.0 * LOG2E
    for n in range(STEPS):
        block = jnp.concatenate([own_ref[0, n], own_ref[0, n + 1]], axis=1)
        final = n + 1 == STEPS
        up = jnp.concatenate([up_ref[0, n], up_last_ref[0] if final else up_ref[0, n + 1]], axis=1)
        down = jnp.concatenate(
            [down_ref[0, n], down_last_ref[0] if final else down_ref[0, n + 1]], axis=1
        )
        own_out[0, n] = dot_nt(rev_ref[...], block).astype(BF)
        edge_out[0, n] = dot_nt(rev_ref[...], jnp.concatenate([up, down], axis=0)).astype(BF)
        stats = jnp.concatenate([stat_ref[0, n], stat_ref[0, n + 1]], axis=1)
        mean, inv = boxed_stats(stats, up, down)
        scaled = inv * mean_inv
        both = jnp.concatenate([scaled * (1.0 / 576.0), scaled * mean], axis=0)[:, :128]
        high = both.astype(BF).astype(F32)
        mid = (both - high).astype(BF).astype(F32)
        index = index_ref[0, :, 128 * n : 128 * n + 128].astype(F32)
        rows = jnp.concatenate(
            [high, mid, both - high - mid, index, jnp.zeros((4, 128), F32)], axis=0
        ).astype(BF)
        blank = jnp.zeros((64, 64), F32)
        left = dot_nt(flip_ref[0:64, :], rows)
        right = dot_nt(flip_ref[64:128, :], rows)
        table_out[0, n] = jnp.concatenate([left, right, blank], axis=1).astype(BF)


def prepare(own, up, up_last, down, down_last, stats, depth_index):
    images, blocks = own.shape[0], own.shape[1]
    return pl.pallas_call(
        prepare_kernel,
        grid=(images,),
        in_specs=[
            pl.BlockSpec((1, blocks, 256, 128), lambda k: (k, 0, 0, 0)),
            pl.BlockSpec((1, STEPS, 64, 128), lambda k: (k, 0, 0, 0)),
            pl.BlockSpec((1, 64, 128), lambda k: (k, 0, 0)),
            pl.BlockSpec((1, STEPS, 64, 128), lambda k: (k, 0, 0, 0)),
            pl.BlockSpec((1, 64, 128), lambda k: (k, 0, 0)),
            pl.BlockSpec((1, blocks, 8, 128), lambda k: (k, 0, 0, 0)),
            pl.BlockSpec((1, 4, 512), lambda k: (k, 0, 0)),
            pl.BlockSpec((WIN, 256), lambda k: (0, 0)),
            pl.BlockSpec((128, 128), lambda k: (0, 0)),
        ],
        out_specs=[
            pl.BlockSpec((1, STEPS, WIN, 256), lambda k: (k, 0, 0, 0)),
            pl.BlockSpec((1, STEPS, WIN, 128), lambda k: (k, 0, 0, 0)),
            pl.BlockSpec((1, STEPS, 64, 128), lambda k: (k, 0, 0, 0)),
        ],
        out_shape=[
            jax.ShapeDtypeStruct((images, STEPS, WIN, 256), BF),
            jax.ShapeDtypeStruct((images, STEPS, WIN, 128), BF),
            jax.ShapeDtypeStruct((images, STEPS, 64, 128), BF),
        ],
        cost_estimate=pl.CostEstimate(
            flops=images * STEPS * 40_000_000, bytes_accessed=images * 1_000_000, transcendentals=0
        ),
        compiler_params=PARAMS,
        name="prepare",
    )(own, up, up_last, down, down_last, stats, depth_index, reversal(), flips())


def skewed(left, right, column, lane, shift):
    return pltpu.roll(jnp.where(lane < column, right, left), shift, 1, stride=1, stride_axis=0)


def sweep_kernel(group, ys, halo, late, *refs):
    refs = list(refs[1:])

    def take(count):
        out = refs[:count]
        del refs[:count]
        return out

    count = len(ys)
    block_refs = take(3) if late else (take(group), take(group))
    own_ref, table_ref, pat_ref, mask_ref, w2_ref, flip_ref, elev_ref, cell_ref = take(8)

    def joined(three, g):
        if late:
            early, before, after = three
            near = jnp.where(pl.program_id(0) == 0, early[g, 0], before[g, 0])
        else:
            near, after = three[0][g, 0], three[1]
        return jnp.concatenate([near, after[g, 0]], axis=1)

    width = 3 if late else 2
    stat_refs = take(width)
    up_refs = take(width) if halo else None
    down_refs = take(width) if halo else None
    edge_ref = take(1)[0] if halo else None
    mean_ref, rows_ref, skew = refs

    column = 63 - lax.broadcasted_iota(jnp.int32, (64, 128), 0)
    lane = lax.broadcasted_iota(jnp.int32, (64, 128), 1)
    wrapped = lane < column
    first = lane < column + 64
    column8 = 7 - lax.broadcasted_iota(jnp.int32, (8, 128), 0)
    lane8 = lax.broadcasted_iota(jnp.int32, (8, 128), 1)
    hyp = (lane % 64).astype(F32)
    tables = dot(table_ref[:, 0].reshape(group * 64, 128), pat_ref[...])

    soft = []
    chosen = []
    for g in range(group):
        if late:
            rhs = joined(block_refs, g)
        else:
            rhs = jnp.concatenate([block_refs[0][g][0, 0], block_refs[1][g][0, 0]], axis=1)
        stats = joined(stat_refs, g)
        if halo:
            up = joined(up_refs, g)
            down = joined(down_refs, g)
            rhs = jnp.concatenate([rhs, up, down], axis=0)
            sides = edge_ref[g, 0]
        else:
            up = down = None
        mean_b, inv_b = boxed_stats(stats, up, down)
        own = own_ref[g, 0]
        masked = jnp.concatenate([own * mask_ref[y : y + 1, :] for y in ys], axis=0)
        if halo:
            sides = jnp.concatenate([sides * mask_ref[8 + y : 9 + y, 0:128] for y in ys], axis=0)
            masked = jnp.concatenate([masked, sides], axis=1)
        product = dot(masked, rhs)
        for i, y in enumerate(ys):
            p = product[WIN * i : WIN * i + WIN]
            z = jnp.where(
                wrapped, p[16:80, 128:], jnp.where(first, p[80:144, :128], p[16:80, :128])
            )
            z8 = jnp.where(
                lane8 < column8,
                p[72:80, 128:],
                jnp.where(lane8 < column8 + 64, p[8:16, 128:], p[72:80, :128]),
            )
            at = count * g + i
            skew[at, 0:8, :] = pltpu.roll(z8, 57, 1, stride=1, stride_axis=0)
            skew[at, 8:72, :] = pltpu.roll(z, 65, 1, stride=1, stride_axis=0)
            cross = skew[at, 8:72, :] + skew[at, 7:71, :] + skew[at, 6:70, :]
            mb = skewed(mean_b[y : y + 1, :128], mean_b[y : y + 1, 128:], column, lane, 65)
            rb = skewed(inv_b[y : y + 1, :128], inv_b[y : y + 1, 128:], column, lane, 65)
            a1, a2, index = (
                tables[64 * g : 64 * g + 64, (3 * i + q) * 128 : (3 * i + q + 1) * 128]
                for q in range(3)
            )
            weight = jnp.exp2((cross * a1 - a2 * mb) * rb)
            picked = jnp.where(index == hyp, weight, 0.0)
            soft.append(jnp.concatenate(split2(weight), axis=1))
            chosen.append(jnp.concatenate(split2(picked), axis=1))
    soft = jnp.concatenate(soft, axis=0)
    chosen = jnp.concatenate(chosen, axis=0)
    r = dot_nt(w2_ref[...], soft)
    rc = dot_nt(w2_ref[...], chosen)
    inv = 1.0 / r[0:2]
    both = jnp.concatenate([(r[2:4] + r[4:6] + r[6:8]) * inv, rc[0:2] * inv], axis=0)
    pieces = group * count // 2
    both = jnp.concatenate([both[:, 128 * v : 128 * v + 128] for v in range(pieces)], axis=0)
    high = both.astype(BF)
    rest = both - high.astype(F32)
    mid = rest.astype(BF)
    low = (rest - mid.astype(F32)).astype(BF)
    both = dot(jnp.concatenate([high, mid, low], axis=0), flip_ref[...])
    both = both[0 : 4 * pieces] + both[4 * pieces : 8 * pieces] + both[8 * pieces :]
    turned = pltpu.roll(both, 64, 1)
    left = lax.broadcasted_iota(jnp.int32, (1, 128), 1) < 64
    cell_iota = lax.broadcasted_iota(jnp.int32, (128, 128), 0)
    blank = jnp.zeros((4, 128), F32)
    for g in range(group):
        for i in range(0, count, 2):
            lines = []
            hots = []
            for j, y in enumerate(ys[i : i + 2]):
                at = (count * g + i) // 2 * 4
                lo, hi = (both, turned) if j == 0 else (turned, both)
                mean = jnp.where(left, lo[at : at + 1], hi[at + 1 : at + 2])
                mean_ref[g, i + j : i + j + 1, :] = mean
                c = jnp.where(left, lo[at + 2 : at + 3], hi[at + 3 : at + 4])
                values = jnp.concatenate([c * elev_ref[g, y : y + 1, :], c], axis=0)
                value_hi = values.astype(BF).astype(F32)
                line = jnp.concatenate([value_hi, values - value_hi], axis=0)
                lines.append(jnp.concatenate([line, blank] if j == 0 else [blank, line], axis=1))
                hot = jnp.where(cell_iota == cell_ref[g, y : y + 1, :], 1.0, 0.0)
                hots.append(hot.astype(BF))
            binned = dot_nt(
                jnp.concatenate(lines, axis=0).astype(BF), jnp.concatenate(hots, axis=1)
            )
            for j in range(2):
                got = binned[4 * j : 4 * j + 2] + binned[4 * j + 2 : 4 * j + 4]
                at = count * g + i + j
                rows_ref[0, at : at + 1, 0:128] = got[0:1]
                rows_ref[0, at : at + 1, 128:256] = got[1:2]


def sweep_steps(
    first, steps, ys, group, slot, blocks, stats, ups, downs, own, edge, table, w2, elev, cell, late
):
    images = own.shape[0]
    halo = ups is not None
    count = len(ys)

    def slot_block(g, j):
        return lambda n, k, s: (s[group * k + g], n + first + j, 0, 0)

    def near(n, k, s):
        return (k, n + first, 0, 0)

    def whole(n, k, s):
        return (0, 0)

    def pixels(n, k, s):
        return (k, 0, n + first)

    def pair_specs(rows, kept=FIRST - 1):
        if late:
            maps = (
                lambda n, k, s: (k, kept, 0, 0),
                lambda n, k, s: (k, 0, 0, 0),
                lambda n, k, s: (k, n, 0, 0),
            )
        else:
            maps = (near, lambda n, k, s: (k, n + first + 1, 0, 0))
        return [pl.BlockSpec((group, 1, rows, 128), m) for m in maps]

    def pair_args(arrays):
        return [arrays[0], arrays[1], arrays[1]] if late else [arrays[0], arrays[0]]

    if late:
        in_specs = pair_specs(256, 0)
        args = pair_args(blocks)
    else:
        in_specs = [
            pl.BlockSpec((1, 1, 256, 128), slot_block(g, j)) for j in range(2) for g in range(group)
        ]
        args = [blocks] * (2 * group)
    in_specs += [
        pl.BlockSpec((group, 1, WIN, 256), near),
        pl.BlockSpec((group, 1, 64, 128), near),
        pl.BlockSpec((128, 3 * 128 * count), whole),
        pl.BlockSpec((16, 256), whole),
        pl.BlockSpec((8, 256), whole),
        pl.BlockSpec((128, 128), whole),
        pl.BlockSpec((group, 4, 128), pixels),
        pl.BlockSpec((group, 4, 128), pixels),
    ] + pair_specs(8)
    args += [
        own, table, table_patterns(ys), row_masks(), w2, flips(), elev, cell,
    ] + pair_args(stats)
    if halo:
        in_specs += pair_specs(64) + pair_specs(64) + [pl.BlockSpec((group, 1, WIN, 128), near)]
        args += pair_args(ups) + pair_args(downs) + [edge]
    work = steps * images * count // 4
    return pl.pallas_call(
        functools.partial(sweep_kernel, group, ys, halo, late),
        grid_spec=pltpu.PrefetchScalarGridSpec(
            num_scalar_prefetch=1,
            grid=(steps, images // group),
            in_specs=in_specs,
            out_specs=[
                pl.BlockSpec((group, count, 128), lambda n, k, s: (k, 0, n)),
                pl.BlockSpec((1, count * group, 256), lambda n, k, s: (n, k, 0)),
            ],
            scratch_shapes=[pltpu.VMEM((count * group, 72, 128), F32)],
        ),
        out_shape=[
            jax.ShapeDtypeStruct((images, count, steps * 128), F32),
            jax.ShapeDtypeStruct((steps, images * count, 256), F32),
        ],
        compiler_params=LATE if late else PARAMS,
        cost_estimate=pl.CostEstimate(
            flops=work * 200_000_000, bytes_accessed=work * 400_000, transcendentals=0
        ),
        name="sweep",
    )(slot, *args)


def depth_weights(planes):
    high = lax.reduce_precision(planes, 8, 7)
    mid = lax.reduce_precision(planes - high, 8, 7)
    zero = jnp.zeros_like(planes)
    rows = []
    for v in (jnp.ones_like(planes), high, mid, planes - high - mid):
        rows.append(jnp.concatenate([v, zero]))
        rows.append(jnp.concatenate([zero, v]))
    w = jnp.stack(rows)
    return jnp.concatenate([w, w], axis=1).astype(BF)


def collect_kernel(list_ref, count_ref, a_ref, b_ref, c_ref, d_ref, out_ref, rows):
    at = 0
    for part in (a_ref, b_ref, c_ref, d_ref):
        for n in range(part.shape[0]):
            rows[at : at + part.shape[1], :] = part[n]
            at += part.shape[1]
    for o in range(out_ref.shape[0]):

        def move(step, carry):
            for i in range(8):
                e = step * 8 + i
                out_ref[o, pl.ds(e, 1), :] = rows[pl.ds(list_ref[o, e], 1), :]
            return carry

        lax.fori_loop(0, (count_ref[o] + 7) // 8, move, 0)


def collect(row_list, counts, parts):
    owners, cap = row_list.shape
    total = sum(p.shape[0] * p.shape[1] for p in parts)
    return pl.pallas_call(
        collect_kernel,
        grid_spec=pltpu.PrefetchScalarGridSpec(
            num_scalar_prefetch=2,
            grid=(1,),
            in_specs=[pl.BlockSpec(p.shape, lambda i, a, b: (0, 0, 0)) for p in parts],
            out_specs=pl.BlockSpec((owners, cap, 2 * CELLS), lambda i, a, b: (0, 0, 0)),
            scratch_shapes=[pltpu.VMEM((total, 2 * CELLS), F32)],
        ),
        out_shape=jax.ShapeDtypeStruct((owners, cap, 2 * CELLS), F32),
        compiler_params=SMALL,
        name="collect",
    )(row_list, counts, *parts)


def place_kernel(slot_ref, count_ref, got_ref, out_ref):
    out_ref[...] = jnp.zeros_like(out_ref)
    for t in range(got_ref.shape[0]):
        count = count_ref[t]

        def add(step, carry):
            for i in range(8):
                e = step * 8 + i
                at = pl.ds(slot_ref[t, e], 1)
                row = jnp.where(e < count, got_ref[t, pl.ds(e, 1), :], 0.0)
                out_ref[at, :] = out_ref[at, :] + row
            return carry

        lax.fori_loop(0, (count + 7) // 8, add, 0)


def place(slots, counts, got, total):
    return pl.pallas_call(
        place_kernel,
        grid_spec=pltpu.PrefetchScalarGridSpec(
            num_scalar_prefetch=2,
            grid=(1,),
            in_specs=[pl.BlockSpec(got.shape, lambda i, a, b: (0, 0, 0))],
            out_specs=pl.BlockSpec((total, 2 * CELLS), lambda i, a, b: (0, 0)),
        ),
        out_shape=jax.ShapeDtypeStruct((total, 2 * CELLS), F32),
        compiler_params=SMALL,
        name="place",
    )(slots, counts, got)


def neighbour_rows(head, tail):
    count = lax.axis_size("tile")
    above = lax.ppermute(tail, "tile", [(i, i + 1) for i in range(count - 1)])
    below = lax.ppermute(head, "tile", [(i + 1, i) for i in range(count - 1)])
    return above, below


def on_device(
    features, partner_ids, depth_planes, cam_height, ray_down, depth_index, cell_index,
    block_list, block_slot, block_count,
):
    group_count = lax.axis_size("img")
    owners = lax.axis_size("tile")
    my_group = lax.axis_index("img")
    my_tile = lax.axis_index("tile")
    images = features.shape[0]
    table = partner_ids.reshape(group_count, images)
    source_of = table // images
    chosen = jnp.sum(jnp.where(source_of == my_group, table % images, 0), axis=1)
    slot = lax.dynamic_index_in_dim(source_of, my_group, 0, False)

    def exchange(a):
        return lax.all_to_all(a, "img", split_axis=0, concat_axis=0, tiled=True)

    main = exchange(pick(chosen, features, FIRST))

    every = jnp.arange(images, dtype=jnp.int32)
    own = pick(every, features, STEPS + 1)
    own_head, own_tail, own_stats = edges(every, own, False)
    own_up, own_down = neighbour_rows(own_head[:, :STEPS], own_tail[:, :STEPS])
    ends = [jnp.transpose(v[:, STEPS, :, :2], (0, 2, 1)).reshape(images, -1) for v in (own_head, own_tail)]
    ends = [v.reshape(images, 2, -1) for v in neighbour_rows(*ends)]
    up_last, down_last = (
        jnp.pad(jnp.transpose(v, (0, 2, 1)), ((0, 0), (0, 0), (0, 126))) for v in ends
    )
    own_turned, edge_turned, own_table = prepare(
        own, own_up, up_last, own_down, down_last, own_stats, depth_index
    )
    packed = pack(chosen, own)

    hyp = jnp.arange(NDEPTH, dtype=jnp.int32)[:, None, None, None]
    plane_at = jnp.sum(
        jnp.where(hyp == depth_index[None], depth_planes[:, None, None, None], 0.0), 0
    )
    elevation = cam_height[:, None, None] - ray_down * plane_at

    meta = jnp.concatenate(
        [block_slot[0, 0], jnp.broadcast_to(block_count[0, 0][:, None], (owners, 128))], axis=1
    )
    metas = [lax.dynamic_slice_in_dim(meta, my_tile, 1, 0)]
    for s in range(1, owners):
        mine = lax.dynamic_slice_in_dim(meta, (my_tile + s) % owners, 1, 0)
        metas.append(lax.ppermute(mine, "tile", [(i, (i + s) % owners) for i in range(owners)]))
    metas = jnp.concatenate(metas, axis=0)
    metas = jnp.take(metas, (my_tile - jnp.arange(owners)) % owners, axis=0)

    w2 = depth_weights(depth_planes)

    packed, own_turned, edge_turned, own_table, elevation, metas, w2 = lax.optimization_barrier(
        (packed, own_turned, edge_turned, own_table, elevation, metas, w2)
    )
    last = exchange(packed)
    head, tail, stats, early = edges(slot, main, True)
    up, down = neighbour_rows(head, tail)
    shared = (own_turned, edge_turned, own_table, w2, elevation, cell_index)
    shared = (own_turned, edge_turned, own_table, w2, elevation, cell_index)
    inner, outer = (1, 2), (0, 3)
    one = (stats,)
    mean_i, rows_i = sweep_steps(0, 2, inner, 16, slot, main, one, None, None, *shared, False)
    up, down, mean_i = lax.optimization_barrier((up, down, mean_i))
    mean_o, rows_o = sweep_steps(0, 2, outer, 16, slot, main, one, (up,), (down,), *shared, False)
    last, mean_o = lax.optimization_barrier((last, mean_o))
    head_l, tail_l, stats_l, late = unpack(slot, last)
    up_l, down_l = neighbour_rows(head_l, tail_l)
    blocks, both = (early, late), (stats, stats_l)
    mean_il, rows_il = sweep_steps(2, 2, inner, 16, slot, blocks, both, None, None, *shared, True)
    mean_ol, rows_ol = sweep_steps(
        2, 2, outer, 16, slot, blocks, both, (up, up_l), (down, down_l), *shared, True
    )
    mean_i = jnp.concatenate([mean_i, mean_il], axis=2)
    mean_o = jnp.concatenate([mean_o, mean_ol], axis=2)
    mean_range = jnp.concatenate([mean_o[:, 0:1], mean_i, mean_o[:, 1:2]], axis=1)

    lists = block_list[0, 0]
    n, r, k = lists % STEPS, lists // STEPS % 4, lists // (4 * STEPS)
    inside = (r == 1) | (r == 2)
    row_list = 2 * images * n + 2 * k + jnp.where(inside, r - 1, 8 * images + r // 3)
    send = collect(row_list, block_count[0, 0], (rows_i, rows_il, rows_o, rows_ol))
    got = lax.all_to_all(send, "tile", split_axis=0, concat_axis=0, tiled=True)
    dense = place(metas[:, :128], metas[:, 128], got, group_count * PATCH_DEV)
    parts = exchange(dense.reshape(group_count, PATCH_DEV, 2 * CELLS))
    total = jnp.sum(parts, axis=0)
    return mean_range, total[:, :CELLS] / (total[:, CELLS:] + 1.0)


def solution(mesh):
    return jax.shard_map(
        on_device,
        mesh=mesh,
        in_specs=(
            P("img", None, "tile", None),
            P(),
            P(),
            P("img"),
            P("img", "tile", None),
            P("img", "tile", None),
            P("img", "tile", None),
            P("img", "tile", None, None),
            P("img", "tile", None, None),
            P("img", "tile", None),
        ),
        out_specs=(P("img", "tile", None), P(("img", "tile"), None)),
        check_vma=False,
    )
```

```python
import functools
import math

import numpy as np
import jax
import jax.numpy as jnp
from jax import lax
from jax.experimental import pallas as pl
from jax.experimental.pallas import tpu as pltpu
from jax.sharding import PartitionSpec as P

NDEPTH = 64
CELLS = 128
PATCH_DEV = 16
STEPS = 4
WIN = 144
LOG2E = math.log2(math.e)
BF = jnp.bfloat16
F32 = jnp.float32
NT = (((1,), (1,)), ((), ()))
PARAMS = pltpu.CompilerParams(vmem_limit_bytes=60 * 1024 * 1024)
LATE = pltpu.CompilerParams(vmem_limit_bytes=40 * 1024 * 1024)
SMALL = pltpu.CompilerParams(vmem_limit_bytes=24 * 1024 * 1024)


def dot(a, b):
    return jnp.dot(a, b, preferred_element_type=F32)


def dot_nt(a, b):
    return lax.dot_general(a, b, NT, preferred_element_type=F32)


def table_patterns(ys):
    pat = np.zeros((128, 3 * len(ys), 128), np.float32)
    for half in range(2):
        lanes = slice(64 * half, 64 * half + 64)
        for i, y in enumerate(ys):
            for q in range(2):
                for s in range(3):
                    pat[half * 32 + s * 8 + q * 4 + y, i * 3 + q, lanes] = 1.0
            pat[half * 32 + 24 + y, i * 3 + 2, lanes] = 1.0
    return jnp.asarray(pat.reshape(128, -1), BF)


def row_masks():
    masks = np.zeros((16, 256), np.float32)
    for y in range(4):
        masks[y] = np.abs(np.arange(256) % 4 - y) <= 1
    masks[8, 0:64] = 1.0
    masks[11, 64:128] = 1.0
    return jnp.asarray(masks, BF)


def flips():
    m = np.zeros((128, 128), np.float32)
    for i in range(128):
        m[i, i // 64 * 64 + 63 - i % 64] = 1.0
    return jnp.asarray(m, BF)


def reversal():
    m = np.zeros((WIN, 256), np.float32)
    for i in range(WIN):
        m[i, WIN - 1 - i] = 1.0
    return jnp.asarray(m, BF)


def edge_constants():
    sel = np.zeros((128, 256), np.float32)
    for c in range(64):
        sel[c, 4 * c] = 1.0
        sel[64 + c, 4 * c + 3] = 1.0
    return (jnp.asarray(sel, BF),)


def split2(a):
    high = a.astype(BF)
    return high, (a - high.astype(F32)).astype(BF)


def boxed_stats(stats, up, down):
    blank = jnp.zeros((1, 256), F32)
    sums = [blank] + [stats[y : y + 1] for y in range(4)] + [blank]
    sqs = [blank] + [stats[4 + y : 5 + y] for y in range(4)] + [blank]
    if up is not None:
        for at, halo in ((0, up.astype(F32)), (5, down.astype(F32))):
            sums[at] = jnp.sum(halo, 0, keepdims=True)
            sqs[at] = jnp.sum(halo * halo, 0, keepdims=True)
    tall = jnp.concatenate(
        [v[y] + v[y + 1] + v[y + 2] for v in (sums, sqs) for y in range(4)], axis=0
    )
    boxed = (tall + pltpu.roll(tall, 255, 1) + pltpu.roll(tall, 254, 1)) * (1.0 / 576.0)
    mean = boxed[0:4]
    return mean, lax.rsqrt(boxed[4:8] - mean * mean + 1e-5)


PART = 8
PACKED = 136
PARTS = 4
FIRST = 3


def pick(idx, features, blocks):
    count = idx.shape[0]
    images, channels, rows, _ = features.shape

    def kernel(idx_ref, features_ref, out_ref, strips, in_sem, out_sem):
        def read(k):
            return pltpu.make_async_copy(
                features_ref.at[k, :, :, pl.ds(0, 128 * blocks)], strips.at[k], in_sem.at[k]
            )

        def write(s, j):
            return pltpu.make_async_copy(
                strips.at[idx_ref[s], :, :, pl.ds(128 * j, 128)], out_ref.at[s, j], out_sem.at[s, j]
            )

        for k in range(images):
            read(k).start()
        part = images // PARTS
        for q in range(PARTS):
            for k in range(q * part, (q + 1) * part):
                read(k).wait()
            for s in range(count):

                @pl.when(idx_ref[s] // part == q)
                def _():
                    for j in range(blocks):
                        write(s, j).start()

        for s in range(count):
            for j in range(blocks):
                write(s, j).wait()

    out = pl.pallas_call(
        kernel,
        grid_spec=pltpu.PrefetchScalarGridSpec(
            num_scalar_prefetch=1,
            grid=(1,),
            in_specs=[pl.BlockSpec(memory_space=pl.ANY)],
            out_specs=pl.BlockSpec(memory_space=pl.ANY),
            scratch_shapes=[
                pltpu.VMEM((images, channels, rows, 128 * blocks), BF),
                pltpu.SemaphoreType.DMA((images,)),
                pltpu.SemaphoreType.DMA((count, blocks)),
            ],
        ),
        out_shape=jax.ShapeDtypeStruct((count, blocks, channels, rows, 128), BF),
        compiler_params=PARAMS,
        cost_estimate=pl.CostEstimate(
            flops=0, bytes_accessed=count * blocks * 131072, transcendentals=0
        ),
        name="pick",
    )(idx, features)
    return out.reshape(count, blocks, channels * rows, 128)


def pack_constants():
    spread = np.zeros((128, 256), np.float32)
    for i in range(64):
        spread[i, i] = 1.0
        spread[64 + i, 128 + i] = 1.0
    column = np.zeros((8, 128), np.float32)
    column[0, 64] = 1.0
    into = np.zeros((256, 128), np.float32)
    into[:, 64] = 1.0
    return tuple(jnp.asarray(m, BF) for m in (spread, column, into, np.eye(256)))


def pack_kernel(idx_ref, *refs):
    whole, part = refs[:PART], refs[PART : 2 * PART]
    spread_ref, column_ref, out_ref = refs[2 * PART :]
    for g in range(PART):
        out_ref[g, 0:256, :] = whole[g][0, 0]
        block = part[g][0, 0]
        out_ref[g, 256:384, :] = (
            dot_nt(block[0:128], spread_ref[:, 0:128]) + dot_nt(block[128:256], spread_ref[:, 128:])
        ).astype(BF)
        line = dot_nt(column_ref[...], block)
        out_ref[g, 384:392, :] = jnp.concatenate(
            [line[0:1, 0:128], line[0:1, 128:256], jnp.zeros((6, 128), F32)], axis=0
        ).astype(BF)


def pack(idx, own):
    count = idx.shape[0]
    spread, column, _, _ = pack_constants()

    def chosen(g, j):
        return lambda k, s: (s[PART * k + g], j, 0, 0)

    return pl.pallas_call(
        pack_kernel,
        grid_spec=pltpu.PrefetchScalarGridSpec(
            num_scalar_prefetch=1,
            grid=(count // PART,),
            in_specs=[
                pl.BlockSpec((1, 1, 256, 128), chosen(g, j))
                for j in (FIRST, FIRST + 1)
                for g in range(PART)
            ]
            + [
                pl.BlockSpec((128, 256), lambda k, s: (0, 0)),
                pl.BlockSpec((8, 128), lambda k, s: (0, 0)),
            ],
            out_specs=pl.BlockSpec((PART, 256 + PACKED, 128), lambda k, s: (k, 0, 0)),
        ),
        out_shape=jax.ShapeDtypeStruct((count, 256 + PACKED, 128), BF),
        compiler_params=PARAMS,
        name="pack",
    )(idx, *[own] * (2 * PART), spread, column)


def block_edges(block, sel_ref):
    rows = dot(sel_ref[...], block).astype(BF)
    value = block.astype(F32).reshape(32, 8, 128)
    total = jnp.sum(value, 0)
    square = jnp.sum(value * value, 0)
    stats = jnp.concatenate([total[0:4] + total[4:8], square[0:4] + square[4:8]], axis=0)
    return rows[0:64], rows[64:128], stats


def edge_kernel(slot_ref, *refs):
    blocks, (sel_ref, head_ref, tail_ref, stats_ref, *kept) = refs[:PART], refs[PART:]
    for g in range(PART):
        if kept:
            kept[0][g, 0] = blocks[g][0, blocks[g].shape[1] - 1]
        for j in range(stats_ref.shape[1]):
            head, tail, stats = block_edges(blocks[g][0, j], sel_ref)
            head_ref[g, j] = head
            tail_ref[g, j] = tail
            stats_ref[g, j] = stats


def unpack_kernel(slot_ref, *refs):
    packed = refs[:PART]
    (
        spread_ref, into_ref, eye_ref, sel_ref, head_ref, tail_ref, stats_ref, block_ref,
    ) = refs[PART:]
    for g in range(PART):
        wide = dot(packed[g][0, 256:384, :], spread_ref[...])
        line = packed[g][0, 384:392, :]
        line = jnp.concatenate([line[0:1], line[1:2]], axis=1)
        column = dot(eye_ref[...] * line, into_ref[...])
        block = jnp.concatenate([wide[:, :128], wide[:, 128:]], axis=0) + column
        blocks = (packed[g][0, 0:256, :], block.astype(BF))
        for j in range(2):
            block_ref[g, j] = blocks[j]
            head, tail, stats = block_edges(blocks[j], sel_ref)
            head_ref[g, j] = head
            tail_ref[g, j] = tail
            stats_ref[g, j] = stats


def edge_outputs(images, blocks):
    specs = [
        pl.BlockSpec((PART, blocks, 64, 128), lambda k, s: (k, 0, 0, 0)),
        pl.BlockSpec((PART, blocks, 64, 128), lambda k, s: (k, 0, 0, 0)),
        pl.BlockSpec((PART, blocks, 8, 128), lambda k, s: (k, 0, 0, 0)),
    ]
    shapes = [
        jax.ShapeDtypeStruct((images, blocks, 64, 128), BF),
        jax.ShapeDtypeStruct((images, blocks, 64, 128), BF),
        jax.ShapeDtypeStruct((images, blocks, 8, 128), F32),
    ]
    return specs, shapes


def whole_spec(a):
    return pl.BlockSpec(a.shape, lambda k, s: (0,) * a.ndim)


def edges(slot, recv, keep_last):
    images, blocks = slot.shape[0], recv.shape[1]
    constants = edge_constants()
    specs, shapes = edge_outputs(images, blocks)
    if keep_last:
        specs = specs + [pl.BlockSpec((PART, 1, 256, 128), lambda k, s: (k, 0, 0, 0))]
        shapes = shapes + [jax.ShapeDtypeStruct((images, 1, 256, 128), BF)]

    def by_slot(g):
        return lambda k, s: (s[PART * k + g], 0, 0, 0)

    return pl.pallas_call(
        edge_kernel,
        grid_spec=pltpu.PrefetchScalarGridSpec(
            num_scalar_prefetch=1,
            grid=(images // PART,),
            in_specs=[pl.BlockSpec((1, blocks, 256, 128), by_slot(g)) for g in range(PART)]
            + [whole_spec(a) for a in constants],
            out_specs=specs,
        ),
        out_shape=shapes,
        cost_estimate=pl.CostEstimate(
            flops=images * blocks * 20_000_000, bytes_accessed=images * blocks * 100_000,
            transcendentals=0,
        ),
        compiler_params=PARAMS,
        name="edges",
    )(slot, *[recv] * PART, *constants)


def unpack(slot, packed):
    images = slot.shape[0]
    spread, _, into, eye = pack_constants()
    constants = (spread, into, eye) + edge_constants()
    specs, shapes = edge_outputs(images, 2)

    def by_slot(g):
        return lambda k, s: (s[PART * k + g], 0, 0)

    return pl.pallas_call(
        unpack_kernel,
        grid_spec=pltpu.PrefetchScalarGridSpec(
            num_scalar_prefetch=1,
            grid=(images // PART,),
            in_specs=[pl.BlockSpec((1, 256 + PACKED, 128), by_slot(g)) for g in range(PART)]
            + [whole_spec(a) for a in constants],
            out_specs=specs + [pl.BlockSpec((PART, 2, 256, 128), lambda k, s: (k, 0, 0, 0))],
        ),
        out_shape=shapes + [jax.ShapeDtypeStruct((images, 2, 256, 128), BF)],
        compiler_params=SMALL,
        name="unpack",
    )(slot, *[packed] * PART, *constants)


def prepare_kernel(
    own_ref, up_ref, up_last_ref, down_ref, down_last_ref, stat_ref, index_ref, rev_ref, flip_ref, own_out, edge_out, table_out
):
    mean_inv = 24.0 * LOG2E
    for n in range(STEPS):
        block = jnp.concatenate([own_ref[0, n], own_ref[0, n + 1]], axis=1)
        final = n + 1 == STEPS
        up = jnp.concatenate([up_ref[0, n], up_last_ref[0] if final else up_ref[0, n + 1]], axis=1)
        down = jnp.concatenate(
            [down_ref[0, n], down_last_ref[0] if final else down_ref[0, n + 1]], axis=1
        )
        own_out[0, n] = dot_nt(rev_ref[...], block).astype(BF)
        edge_out[0, n] = dot_nt(rev_ref[...], jnp.concatenate([up, down], axis=0)).astype(BF)
        stats = jnp.concatenate([stat_ref[0, n], stat_ref[0, n + 1]], axis=1)
        mean, inv = boxed_stats(stats, up, down)
        scaled = inv * mean_inv
        both = jnp.concatenate([scaled * (1.0 / 576.0), scaled * mean], axis=0)[:, :128]
        high = both.astype(BF).astype(F32)
        mid = (both - high).astype(BF).astype(F32)
        index = index_ref[0, :, 128 * n : 128 * n + 128].astype(F32)
        rows = jnp.concatenate(
            [high, mid, both - high - mid, index, jnp.zeros((4, 128), F32)], axis=0
        ).astype(BF)
        blank = jnp.zeros((64, 64), F32)
        left = dot_nt(flip_ref[0:64, :], rows)
        right = dot_nt(flip_ref[64:128, :], rows)
        table_out[0, n] = jnp.concatenate([left, right, blank], axis=1).astype(BF)


def prepare(own, up, up_last, down, down_last, stats, depth_index):
    images, blocks = own.shape[0], own.shape[1]
    return pl.pallas_call(
        prepare_kernel,
        grid=(images,),
        in_specs=[
            pl.BlockSpec((1, blocks, 256, 128), lambda k: (k, 0, 0, 0)),
            pl.BlockSpec((1, STEPS, 64, 128), lambda k: (k, 0, 0, 0)),
            pl.BlockSpec((1, 64, 128), lambda k: (k, 0, 0)),
            pl.BlockSpec((1, STEPS, 64, 128), lambda k: (k, 0, 0, 0)),
            pl.BlockSpec((1, 64, 128), lambda k: (k, 0, 0)),
            pl.BlockSpec((1, blocks, 8, 128), lambda k: (k, 0, 0, 0)),
            pl.BlockSpec((1, 4, 512), lambda k: (k, 0, 0)),
            pl.BlockSpec((WIN, 256), lambda k: (0, 0)),
            pl.BlockSpec((128, 128), lambda k: (0, 0)),
        ],
        out_specs=[
            pl.BlockSpec((1, STEPS, WIN, 256), lambda k: (k, 0, 0, 0)),
            pl.BlockSpec((1, STEPS, WIN, 128), lambda k: (k, 0, 0, 0)),
            pl.BlockSpec((1, STEPS, 64, 128), lambda k: (k, 0, 0, 0)),
        ],
        out_shape=[
            jax.ShapeDtypeStruct((images, STEPS, WIN, 256), BF),
            jax.ShapeDtypeStruct((images, STEPS, WIN, 128), BF),
            jax.ShapeDtypeStruct((images, STEPS, 64, 128), BF),
        ],
        cost_estimate=pl.CostEstimate(
            flops=images * STEPS * 40_000_000, bytes_accessed=images * 1_000_000, transcendentals=0
        ),
        compiler_params=PARAMS,
        name="prepare",
    )(own, up, up_last, down, down_last, stats, depth_index, reversal(), flips())


def skewed(left, right, column, lane, shift):
    return pltpu.roll(jnp.where(lane < column, right, left), shift, 1, stride=1, stride_axis=0)


def sweep_kernel(group, ys, halo, late, *refs):
    refs = list(refs[1:])

    def take(count):
        out = refs[:count]
        del refs[:count]
        return out

    count = len(ys)
    block_refs = take(3) if late else (take(group), take(group))
    own_ref, table_ref, pat_ref, mask_ref, w2_ref, flip_ref, elev_ref, cell_ref = take(8)

    def joined(three, g):
        if late:
            early, before, after = three
            near = jnp.where(pl.program_id(0) == 0, early[g, 0], before[g, 0])
        else:
            near, after = three[0][g, 0], three[1]
        return jnp.concatenate([near, after[g, 0]], axis=1)

    width = 3 if late else 2
    stat_refs = take(width)
    up_refs = take(width) if halo else None
    down_refs = take(width) if halo else None
    edge_ref = take(1)[0] if halo else None
    mean_ref, rows_ref, skew = refs

    column = 63 - lax.broadcasted_iota(jnp.int32, (64, 128), 0)
    lane = lax.broadcasted_iota(jnp.int32, (64, 128), 1)
    wrapped = lane < column
    first = lane < column + 64
    column8 = 7 - lax.broadcasted_iota(jnp.int32, (8, 128), 0)
    lane8 = lax.broadcasted_iota(jnp.int32, (8, 128), 1)
    hyp = (lane % 64).astype(F32)
    tables = dot(table_ref[:, 0].reshape(group * 64, 128), pat_ref[...])

    soft = []
    chosen = []
    for g in range(group):
        if late:
            rhs = joined(block_refs, g)
        else:
            rhs = jnp.concatenate([block_refs[0][g][0, 0], block_refs[1][g][0, 0]], axis=1)
        stats = joined(stat_refs, g)
        if halo:
            up = joined(up_refs, g)
            down = joined(down_refs, g)
            rhs = jnp.concatenate([rhs, up, down], axis=0)
            sides = edge_ref[g, 0]
        else:
            up = down = None
        mean_b, inv_b = boxed_stats(stats, up, down)
        own = own_ref[g, 0]
        masked = jnp.concatenate([own * mask_ref[y : y + 1, :] for y in ys], axis=0)
        if halo:
            sides = jnp.concatenate([sides * mask_ref[8 + y : 9 + y, 0:128] for y in ys], axis=0)
            masked = jnp.concatenate([masked, sides], axis=1)
        product = dot(masked, rhs)
        for i, y in enumerate(ys):
            p = product[WIN * i : WIN * i + WIN]
            z = jnp.where(
                wrapped, p[16:80, 128:], jnp.where(first, p[80:144, :128], p[16:80, :128])
            )
            z8 = jnp.where(
                lane8 < column8,
                p[72:80, 128:],
                jnp.where(lane8 < column8 + 64, p[8:16, 128:], p[72:80, :128]),
            )
            at = count * g + i
            skew[at, 0:8, :] = pltpu.roll(z8, 57, 1, stride=1, stride_axis=0)
            skew[at, 8:72, :] = pltpu.roll(z, 65, 1, stride=1, stride_axis=0)
            cross = skew[at, 8:72, :] + skew[at, 7:71, :] + skew[at, 6:70, :]
            mb = skewed(mean_b[y : y + 1, :128], mean_b[y : y + 1, 128:], column, lane, 65)
            rb = skewed(inv_b[y : y + 1, :128], inv_b[y : y + 1, 128:], column, lane, 65)
            a1, a2, index = (
                tables[64 * g : 64 * g + 64, (3 * i + q) * 128 : (3 * i + q + 1) * 128]
                for q in range(3)
            )
            weight = jnp.exp2((cross * a1 - a2 * mb) * rb)
            picked = jnp.where(index == hyp, weight, 0.0)
            soft.append(jnp.concatenate(split2(weight), axis=1))
            chosen.append(jnp.concatenate(split2(picked), axis=1))
    soft = jnp.concatenate(soft, axis=0)
    chosen = jnp.concatenate(chosen, axis=0)
    r = dot_nt(w2_ref[...], soft)
    rc = dot_nt(w2_ref[...], chosen)
    inv = 1.0 / r[0:2]
    both = jnp.concatenate([(r[2:4] + r[4:6] + r[6:8]) * inv, rc[0:2] * inv], axis=0)
    pieces = group * count // 2
    both = jnp.concatenate([both[:, 128 * v : 128 * v + 128] for v in range(pieces)], axis=0)
    high = both.astype(BF)
    rest = both - high.astype(F32)
    mid = rest.astype(BF)
    low = (rest - mid.astype(F32)).astype(BF)
    both = dot(jnp.concatenate([high, mid, low], axis=0), flip_ref[...])
    both = both[0 : 4 * pieces] + both[4 * pieces : 8 * pieces] + both[8 * pieces :]
    turned = pltpu.roll(both, 64, 1)
    left = lax.broadcasted_iota(jnp.int32, (1, 128), 1) < 64
    cell_iota = lax.broadcasted_iota(jnp.int32, (128, 128), 0)
    blank = jnp.zeros((4, 128), F32)
    for g in range(group):
        for i in range(0, count, 2):
            lines = []
            hots = []
            for j, y in enumerate(ys[i : i + 2]):
                at = (count * g + i) // 2 * 4
                lo, hi = (both, turned) if j == 0 else (turned, both)
                mean = jnp.where(left, lo[at : at + 1], hi[at + 1 : at + 2])
                mean_ref[g, i + j : i + j + 1, :] = mean
                c = jnp.where(left, lo[at + 2 : at + 3], hi[at + 3 : at + 4])
                values = jnp.concatenate([c * elev_ref[g, y : y + 1, :], c], axis=0)
                value_hi = values.astype(BF).astype(F32)
                line = jnp.concatenate([value_hi, values - value_hi], axis=0)
                lines.append(jnp.concatenate([line, blank] if j == 0 else [blank, line], axis=1))
                hot = jnp.where(cell_iota == cell_ref[g, y : y + 1, :], 1.0, 0.0)
                hots.append(hot.astype(BF))
            binned = dot_nt(
                jnp.concatenate(lines, axis=0).astype(BF), jnp.concatenate(hots, axis=1)
            )
            for j in range(2):
                got = binned[4 * j : 4 * j + 2] + binned[4 * j + 2 : 4 * j + 4]
                at = count * g + i + j
                rows_ref[0, at : at + 1, 0:128] = got[0:1]
                rows_ref[0, at : at + 1, 128:256] = got[1:2]


def sweep_steps(
    first, steps, ys, group, slot, blocks, stats, ups, downs, own, edge, table, w2, elev, cell, late
):
    images = own.shape[0]
    halo = ups is not None
    count = len(ys)

    def slot_block(g, j):
        return lambda n, k, s: (s[group * k + g], n + first + j, 0, 0)

    def near(n, k, s):
        return (k, n + first, 0, 0)

    def whole(n, k, s):
        return (0, 0)

    def pixels(n, k, s):
        return (k, 0, n + first)

    def pair_specs(rows, kept=FIRST - 1):
        if late:
            maps = (
                lambda n, k, s: (k, kept, 0, 0),
                lambda n, k, s: (k, 0, 0, 0),
                lambda n, k, s: (k, n, 0, 0),
            )
        else:
            maps = (near, lambda n, k, s: (k, n + first + 1, 0, 0))
        return [pl.BlockSpec((group, 1, rows, 128), m) for m in maps]

    def pair_args(arrays):
        return [arrays[0], arrays[1], arrays[1]] if late else [arrays[0], arrays[0]]

    if late:
        in_specs = pair_specs(256, 0)
        args = pair_args(blocks)
    else:
        in_specs = [
            pl.BlockSpec((1, 1, 256, 128), slot_block(g, j)) for j in range(2) for g in range(group)
        ]
        args = [blocks] * (2 * group)
    in_specs += [
        pl.BlockSpec((group, 1, WIN, 256), near),
        pl.BlockSpec((group, 1, 64, 128), near),
        pl.BlockSpec((128, 3 * 128 * count), whole),
        pl.BlockSpec((16, 256), whole),
        pl.BlockSpec((8, 256), whole),
        pl.BlockSpec((128, 128), whole),
        pl.BlockSpec((group, 4, 128), pixels),
        pl.BlockSpec((group, 4, 128), pixels),
    ] + pair_specs(8)
    args += [
        own, table, table_patterns(ys), row_masks(), w2, flips(), elev, cell,
    ] + pair_args(stats)
    if halo:
        in_specs += pair_specs(64) + pair_specs(64) + [pl.BlockSpec((group, 1, WIN, 128), near)]
        args += pair_args(ups) + pair_args(downs) + [edge]
    work = steps * images * count // 4
    return pl.pallas_call(
        functools.partial(sweep_kernel, group, ys, halo, late),
        grid_spec=pltpu.PrefetchScalarGridSpec(
            num_scalar_prefetch=1,
            grid=(steps, images // group),
            in_specs=in_specs,
            out_specs=[
                pl.BlockSpec((group, count, 128), lambda n, k, s: (k, 0, n)),
                pl.BlockSpec((1, count * group, 256), lambda n, k, s: (n, k, 0)),
            ],
            scratch_shapes=[pltpu.VMEM((count * group, 72, 128), F32)],
        ),
        out_shape=[
            jax.ShapeDtypeStruct((images, count, steps * 128), F32),
            jax.ShapeDtypeStruct((steps, images * count, 256), F32),
        ],
        compiler_params=LATE,
        cost_estimate=pl.CostEstimate(
            flops=work * 200_000_000, bytes_accessed=work * 400_000, transcendentals=0
        ),
        name="sweep",
    )(slot, *args)


def depth_weights(planes):
    high = lax.reduce_precision(planes, 8, 7)
    mid = lax.reduce_precision(planes - high, 8, 7)
    zero = jnp.zeros_like(planes)
    rows = []
    for v in (jnp.ones_like(planes), high, mid, planes - high - mid):
        rows.append(jnp.concatenate([v, zero]))
        rows.append(jnp.concatenate([zero, v]))
    w = jnp.stack(rows)
    return jnp.concatenate([w, w], axis=1).astype(BF)


def collect_kernel(list_ref, count_ref, a_ref, b_ref, c_ref, d_ref, out_ref, rows):
    at = 0
    for part in (a_ref, b_ref, c_ref, d_ref):
        for n in range(part.shape[0]):
            rows[at : at + part.shape[1], :] = part[n]
            at += part.shape[1]
    for o in range(out_ref.shape[0]):

        def move(step, carry):
            for i in range(8):
                e = step * 8 + i
                out_ref[o, pl.ds(e, 1), :] = rows[pl.ds(list_ref[o, e], 1), :]
            return carry

        lax.fori_loop(0, (count_ref[o] + 7) // 8, move, 0)


def collect(row_list, counts, parts):
    owners, cap = row_list.shape
    total = sum(p.shape[0] * p.shape[1] for p in parts)
    return pl.pallas_call(
        collect_kernel,
        grid_spec=pltpu.PrefetchScalarGridSpec(
            num_scalar_prefetch=2,
            grid=(1,),
            in_specs=[pl.BlockSpec(p.shape, lambda i, a, b: (0, 0, 0)) for p in parts],
            out_specs=pl.BlockSpec((owners, cap, 2 * CELLS), lambda i, a, b: (0, 0, 0)),
            scratch_shapes=[pltpu.VMEM((total, 2 * CELLS), F32)],
        ),
        out_shape=jax.ShapeDtypeStruct((owners, cap, 2 * CELLS), F32),
        compiler_params=SMALL,
        name="collect",
    )(row_list, counts, *parts)


def place_kernel(slot_ref, count_ref, got_ref, out_ref):
    out_ref[...] = jnp.zeros_like(out_ref)
    for t in range(got_ref.shape[0]):
        count = count_ref[t]

        def add(step, carry):
            for i in range(8):
                e = step * 8 + i
                at = pl.ds(slot_ref[t, e], 1)
                row = jnp.where(e < count, got_ref[t, pl.ds(e, 1), :], 0.0)
                out_ref[at, :] = out_ref[at, :] + row
            return carry

        lax.fori_loop(0, (count + 7) // 8, add, 0)


def place(slots, counts, got, total):
    return pl.pallas_call(
        place_kernel,
        grid_spec=pltpu.PrefetchScalarGridSpec(
            num_scalar_prefetch=2,
            grid=(1,),
            in_specs=[pl.BlockSpec(got.shape, lambda i, a, b: (0, 0, 0))],
            out_specs=pl.BlockSpec((total, 2 * CELLS), lambda i, a, b: (0, 0)),
        ),
        out_shape=jax.ShapeDtypeStruct((total, 2 * CELLS), F32),
        compiler_params=SMALL,
        name="place",
    )(slots, counts, got)


def neighbour_rows(head, tail):
    count = lax.axis_size("tile")
    above = lax.ppermute(tail, "tile", [(i, i + 1) for i in range(count - 1)])
    below = lax.ppermute(head, "tile", [(i + 1, i) for i in range(count - 1)])
    return above, below


def on_device(
    features, partner_ids, depth_planes, cam_height, ray_down, depth_index, cell_index,
    block_list, block_slot, block_count,
):
    group_count = lax.axis_size("img")
    owners = lax.axis_size("tile")
    my_group = lax.axis_index("img")
    my_tile = lax.axis_index("tile")
    images = features.shape[0]
    table = partner_ids.reshape(group_count, images)
    source_of = table // images
    chosen = jnp.sum(jnp.where(source_of == my_group, table % images, 0), axis=1)
    slot = lax.dynamic_index_in_dim(source_of, my_group, 0, False)

    def exchange(a):
        return lax.all_to_all(a, "img", split_axis=0, concat_axis=0, tiled=True)

    main = exchange(pick(chosen, features, FIRST))

    every = jnp.arange(images, dtype=jnp.int32)
    own = pick(every, features, STEPS + 1)
    own_head, own_tail, own_stats = edges(every, own, False)
    own_up, own_down = neighbour_rows(own_head[:, :STEPS], own_tail[:, :STEPS])
    ends = [jnp.transpose(v[:, STEPS, :, :2], (0, 2, 1)).reshape(images, -1) for v in (own_head, own_tail)]
    ends = [v.reshape(images, 2, -1) for v in neighbour_rows(*ends)]
    up_last, down_last = (
        jnp.pad(jnp.transpose(v, (0, 2, 1)), ((0, 0), (0, 0), (0, 126))) for v in ends
    )
    own_turned, edge_turned, own_table = prepare(
        own, own_up, up_last, own_down, down_last, own_stats, depth_index
    )
    packed = pack(chosen, own)

    hyp = jnp.arange(NDEPTH, dtype=jnp.int32)[:, None, None, None]
    plane_at = jnp.sum(
        jnp.where(hyp == depth_index[None], depth_planes[:, None, None, None], 0.0), 0
    )
    elevation = cam_height[:, None, None] - ray_down * plane_at

    meta = jnp.concatenate(
        [block_slot[0, 0], jnp.broadcast_to(block_count[0, 0][:, None], (owners, 128))], axis=1
    )
    metas = [lax.dynamic_slice_in_dim(meta, my_tile, 1, 0)]
    for s in range(1, owners):
        mine = lax.dynamic_slice_in_dim(meta, (my_tile + s) % owners, 1, 0)
        metas.append(lax.ppermute(mine, "tile", [(i, (i + s) % owners) for i in range(owners)]))
    metas = jnp.concatenate(metas, axis=0)
    metas = jnp.take(metas, (my_tile - jnp.arange(owners)) % owners, axis=0)

    w2 = depth_weights(depth_planes)

    packed, own_turned, edge_turned, own_table, elevation, metas, w2 = lax.optimization_barrier(
        (packed, own_turned, edge_turned, own_table, elevation, metas, w2)
    )
    last = exchange(packed)
    head, tail, stats, early = edges(slot, main, True)
    up, down = neighbour_rows(head, tail)
    shared = (own_turned, edge_turned, own_table, w2, elevation, cell_index)
    shared = (own_turned, edge_turned, own_table, w2, elevation, cell_index)
    inner, outer = (1, 2), (0, 3)
    one = (stats,)
    mean_i, rows_i = sweep_steps(0, 2, inner, 16, slot, main, one, None, None, *shared, False)
    up, down, mean_i = lax.optimization_barrier((up, down, mean_i))
    mean_o, rows_o = sweep_steps(0, 2, outer, 16, slot, main, one, (up,), (down,), *shared, False)
    last, mean_o = lax.optimization_barrier((last, mean_o))
    head_l, tail_l, stats_l, late = unpack(slot, last)
    up_l, down_l = neighbour_rows(head_l, tail_l)
    blocks, both = (early, late), (stats, stats_l)
    mean_il, rows_il = sweep_steps(2, 2, inner, 16, slot, blocks, both, None, None, *shared, True)
    mean_ol, rows_ol = sweep_steps(
        2, 2, outer, 16, slot, blocks, both, (up, up_l), (down, down_l), *shared, True
    )
    mean_i = jnp.concatenate([mean_i, mean_il], axis=2)
    mean_o = jnp.concatenate([mean_o, mean_ol], axis=2)
    mean_range = jnp.concatenate([mean_o[:, 0:1], mean_i, mean_o[:, 1:2]], axis=1)

    lists = block_list[0, 0]
    n, r, k = lists % STEPS, lists // STEPS % 4, lists // (4 * STEPS)
    inside = (r == 1) | (r == 2)
    row_list = 2 * images * n + 2 * k + jnp.where(inside, r - 1, 8 * images + r // 3)
    send = collect(row_list, block_count[0, 0], (rows_i, rows_il, rows_o, rows_ol))
    got = lax.all_to_all(send, "tile", split_axis=0, concat_axis=0, tiled=True)
    dense = place(metas[:, :128], metas[:, 128], got, group_count * PATCH_DEV)
    parts = exchange(dense.reshape(group_count, PATCH_DEV, 2 * CELLS))
    total = jnp.sum(parts, axis=0)
    return mean_range, total[:, :CELLS] / (total[:, CELLS:] + 1.0)


def solution(mesh):
    return jax.shard_map(
        on_device,
        mesh=mesh,
        in_specs=(
            P("img", None, "tile", None),
            P(),
            P(),
            P("img"),
            P("img", "tile", None),
            P("img", "tile", None),
            P("img", "tile", None),
            P("img", "tile", None, None),
            P("img", "tile", None, None),
            P("img", "tile", None),
        ),
        out_specs=(P("img", "tile", None), P(("img", "tile"), None)),
        check_vma=False,
    )
```

```python
import functools
import math

import numpy as np
import jax
import jax.numpy as jnp
from jax import lax
from jax.experimental import pallas as pl
from jax.experimental.pallas import tpu as pltpu
from jax.sharding import PartitionSpec as P

NDEPTH = 64
CELLS = 128
PATCH_DEV = 16
STEPS = 4
WIN = 144
LOG2E = math.log2(math.e)
BF = jnp.bfloat16
F32 = jnp.float32
NT = (((1,), (1,)), ((), ()))
PARAMS = pltpu.CompilerParams(vmem_limit_bytes=60 * 1024 * 1024)
LATE = pltpu.CompilerParams(vmem_limit_bytes=40 * 1024 * 1024)
SMALL = pltpu.CompilerParams(vmem_limit_bytes=24 * 1024 * 1024)


def dot(a, b):
    return jnp.dot(a, b, preferred_element_type=F32)


def dot_nt(a, b):
    return lax.dot_general(a, b, NT, preferred_element_type=F32)


def table_patterns(ys):
    pat = np.zeros((128, 3 * len(ys), 128), np.float32)
    for half in range(2):
        lanes = slice(64 * half, 64 * half + 64)
        for i, y in enumerate(ys):
            for q in range(2):
                for s in range(3):
                    pat[half * 32 + s * 8 + q * 4 + y, i * 3 + q, lanes] = 1.0
            pat[half * 32 + 24 + y, i * 3 + 2, lanes] = 1.0
    return jnp.asarray(pat.reshape(128, -1), BF)


def row_masks():
    masks = np.zeros((16, 256), np.float32)
    for y in range(4):
        masks[y] = np.abs(np.arange(256) % 4 - y) <= 1
    masks[8, 0:64] = 1.0
    masks[11, 64:128] = 1.0
    return jnp.asarray(masks, BF)


def flips():
    m = np.zeros((128, 128), np.float32)
    for i in range(128):
        m[i, i // 64 * 64 + 63 - i % 64] = 1.0
    return jnp.asarray(m, BF)


def reversal():
    m = np.zeros((WIN, 256), np.float32)
    for i in range(WIN):
        m[i, WIN - 1 - i] = 1.0
    return jnp.asarray(m, BF)


def edge_constants():
    sel = np.zeros((128, 256), np.float32)
    for c in range(64):
        sel[c, 4 * c] = 1.0
        sel[64 + c, 4 * c + 3] = 1.0
    return (jnp.asarray(sel, BF),)


def split2(a):
    high = a.astype(BF)
    return high, (a - high.astype(F32)).astype(BF)


def boxed_stats(stats, up, down):
    blank = jnp.zeros((1, 256), F32)
    sums = [blank] + [stats[y : y + 1] for y in range(4)] + [blank]
    sqs = [blank] + [stats[4 + y : 5 + y] for y in range(4)] + [blank]
    if up is not None:
        for at, halo in ((0, up.astype(F32)), (5, down.astype(F32))):
            sums[at] = jnp.sum(halo, 0, keepdims=True)
            sqs[at] = jnp.sum(halo * halo, 0, keepdims=True)
    tall = jnp.concatenate(
        [v[y] + v[y + 1] + v[y + 2] for v in (sums, sqs) for y in range(4)], axis=0
    )
    boxed = (tall + pltpu.roll(tall, 255, 1) + pltpu.roll(tall, 254, 1)) * (1.0 / 576.0)
    mean = boxed[0:4]
    return mean, lax.rsqrt(boxed[4:8] - mean * mean + 1e-5)


PART = 8
PACKED = 136
PARTS = 4
FIRST = 3


def pick(idx, features, blocks):
    count = idx.shape[0]
    images, channels, rows, _ = features.shape

    def kernel(idx_ref, features_ref, out_ref, strips, in_sem, out_sem):
        def read(k):
            return pltpu.make_async_copy(
                features_ref.at[k, :, :, pl.ds(0, 128 * blocks)], strips.at[k], in_sem.at[k]
            )

        def write(s, j):
            return pltpu.make_async_copy(
                strips.at[idx_ref[s], :, :, pl.ds(128 * j, 128)], out_ref.at[s, j], out_sem.at[s, j]
            )

        for k in range(images):
            read(k).start()
        part = images // PARTS
        for q in range(PARTS):
            for k in range(q * part, (q + 1) * part):
                read(k).wait()
            for s in range(count):

                @pl.when(idx_ref[s] // part == q)
                def _():
                    for j in range(blocks):
                        write(s, j).start()

        for s in range(count):
            for j in range(blocks):
                write(s, j).wait()

    out = pl.pallas_call(
        kernel,
        grid_spec=pltpu.PrefetchScalarGridSpec(
            num_scalar_prefetch=1,
            grid=(1,),
            in_specs=[pl.BlockSpec(memory_space=pl.ANY)],
            out_specs=pl.BlockSpec(memory_space=pl.ANY),
            scratch_shapes=[
                pltpu.VMEM((images, channels, rows, 128 * blocks), BF),
                pltpu.SemaphoreType.DMA((images,)),
                pltpu.SemaphoreType.DMA((count, blocks)),
            ],
        ),
        out_shape=jax.ShapeDtypeStruct((count, blocks, channels, rows, 128), BF),
        compiler_params=PARAMS,
        cost_estimate=pl.CostEstimate(
            flops=0, bytes_accessed=count * blocks * 131072, transcendentals=0
        ),
        name="pick",
    )(idx, features)
    return out.reshape(count, blocks, channels * rows, 128)


def pack_constants():
    spread = np.zeros((128, 256), np.float32)
    for i in range(64):
        spread[i, i] = 1.0
        spread[64 + i, 128 + i] = 1.0
    column = np.zeros((8, 128), np.float32)
    column[0, 64] = 1.0
    into = np.zeros((256, 128), np.float32)
    into[:, 64] = 1.0
    return tuple(jnp.asarray(m, BF) for m in (spread, column, into, np.eye(256)))


def pack_kernel(idx_ref, *refs):
    whole, part = refs[:PART], refs[PART : 2 * PART]
    spread_ref, column_ref, out_ref = refs[2 * PART :]
    for g in range(PART):
        out_ref[g, 0:256, :] = whole[g][0, 0]
        block = part[g][0, 0]
        out_ref[g, 256:384, :] = (
            dot_nt(block[0:128], spread_ref[:, 0:128]) + dot_nt(block[128:256], spread_ref[:, 128:])
        ).astype(BF)
        line = dot_nt(column_ref[...], block)
        out_ref[g, 384:392, :] = jnp.concatenate(
            [line[0:1, 0:128], line[0:1, 128:256], jnp.zeros((6, 128), F32)], axis=0
        ).astype(BF)


def pack(idx, own):
    count = idx.shape[0]
    spread, column, _, _ = pack_constants()

    def chosen(g, j):
        return lambda k, s: (s[PART * k + g], j, 0, 0)

    return pl.pallas_call(
        pack_kernel,
        grid_spec=pltpu.PrefetchScalarGridSpec(
            num_scalar_prefetch=1,
            grid=(count // PART,),
            in_specs=[
                pl.BlockSpec((1, 1, 256, 128), chosen(g, j))
                for j in (FIRST, FIRST + 1)
                for g in range(PART)
            ]
            + [
                pl.BlockSpec((128, 256), lambda k, s: (0, 0)),
                pl.BlockSpec((8, 128), lambda k, s: (0, 0)),
            ],
            out_specs=pl.BlockSpec((PART, 256 + PACKED, 128), lambda k, s: (k, 0, 0)),
        ),
        out_shape=jax.ShapeDtypeStruct((count, 256 + PACKED, 128), BF),
        compiler_params=PARAMS,
        name="pack",
    )(idx, *[own] * (2 * PART), spread, column)


def block_edges(block, sel_ref):
    rows = dot(sel_ref[...], block).astype(BF)
    value = block.astype(F32).reshape(32, 8, 128)
    total = jnp.sum(value, 0)
    square = jnp.sum(value * value, 0)
    stats = jnp.concatenate([total[0:4] + total[4:8], square[0:4] + square[4:8]], axis=0)
    return rows[0:64], rows[64:128], stats


def edge_kernel(slot_ref, *refs):
    blocks, (sel_ref, head_ref, tail_ref, stats_ref, *kept) = refs[:PART], refs[PART:]
    for g in range(PART):
        if kept:
            kept[0][g, 0] = blocks[g][0, blocks[g].shape[1] - 1]
        for j in range(stats_ref.shape[1]):
            head, tail, stats = block_edges(blocks[g][0, j], sel_ref)
            head_ref[g, j] = head
            tail_ref[g, j] = tail
            stats_ref[g, j] = stats


def unpack_kernel(slot_ref, *refs):
    packed = refs[:PART]
    (
        spread_ref, into_ref, eye_ref, sel_ref, head_ref, tail_ref, stats_ref, block_ref,
    ) = refs[PART:]
    for g in range(PART):
        wide = dot(packed[g][0, 256:384, :], spread_ref[...])
        line = packed[g][0, 384:392, :]
        line = jnp.concatenate([line[0:1], line[1:2]], axis=1)
        column = dot(eye_ref[...] * line, into_ref[...])
        block = jnp.concatenate([wide[:, :128], wide[:, 128:]], axis=0) + column
        blocks = (packed[g][0, 0:256, :], block.astype(BF))
        for j in range(2):
            block_ref[g, j] = blocks[j]
            head, tail, stats = block_edges(blocks[j], sel_ref)
            head_ref[g, j] = head
            tail_ref[g, j] = tail
            stats_ref[g, j] = stats


def edge_outputs(images, blocks):
    specs = [
        pl.BlockSpec((PART, blocks, 64, 128), lambda k, s: (k, 0, 0, 0)),
        pl.BlockSpec((PART, blocks, 64, 128), lambda k, s: (k, 0, 0, 0)),
        pl.BlockSpec((PART, blocks, 8, 128), lambda k, s: (k, 0, 0, 0)),
    ]
    shapes = [
        jax.ShapeDtypeStruct((images, blocks, 64, 128), BF),
        jax.ShapeDtypeStruct((images, blocks, 64, 128), BF),
        jax.ShapeDtypeStruct((images, blocks, 8, 128), F32),
    ]
    return specs, shapes


def whole_spec(a):
    return pl.BlockSpec(a.shape, lambda k, s: (0,) * a.ndim)


def edges(slot, recv, keep_last):
    images, blocks = slot.shape[0], recv.shape[1]
    constants = edge_constants()
    specs, shapes = edge_outputs(images, blocks)
    if keep_last:
        specs = specs + [pl.BlockSpec((PART, 1, 256, 128), lambda k, s: (k, 0, 0, 0))]
        shapes = shapes + [jax.ShapeDtypeStruct((images, 1, 256, 128), BF)]

    def by_slot(g):
        return lambda k, s: (s[PART * k + g], 0, 0, 0)

    return pl.pallas_call(
        edge_kernel,
        grid_spec=pltpu.PrefetchScalarGridSpec(
            num_scalar_prefetch=1,
            grid=(images // PART,),
            in_specs=[pl.BlockSpec((1, blocks, 256, 128), by_slot(g)) for g in range(PART)]
            + [whole_spec(a) for a in constants],
            out_specs=specs,
        ),
        out_shape=shapes,
        cost_estimate=pl.CostEstimate(
            flops=images * blocks * 20_000_000, bytes_accessed=images * blocks * 100_000,
            transcendentals=0,
        ),
        compiler_params=PARAMS,
        name="edges",
    )(slot, *[recv] * PART, *constants)


def unpack(slot, packed):
    images = slot.shape[0]
    spread, _, into, eye = pack_constants()
    constants = (spread, into, eye) + edge_constants()
    specs, shapes = edge_outputs(images, 2)

    def by_slot(g):
        return lambda k, s: (s[PART * k + g], 0, 0)

    return pl.pallas_call(
        unpack_kernel,
        grid_spec=pltpu.PrefetchScalarGridSpec(
            num_scalar_prefetch=1,
            grid=(images // PART,),
            in_specs=[pl.BlockSpec((1, 256 + PACKED, 128), by_slot(g)) for g in range(PART)]
            + [whole_spec(a) for a in constants],
            out_specs=specs + [pl.BlockSpec((PART, 2, 256, 128), lambda k, s: (k, 0, 0, 0))],
        ),
        out_shape=shapes + [jax.ShapeDtypeStruct((images, 2, 256, 128), BF)],
        compiler_params=SMALL,
        name="unpack",
    )(slot, *[packed] * PART, *constants)


def prepare_kernel(
    own_ref, up_ref, up_last_ref, down_ref, down_last_ref, stat_ref, index_ref, rev_ref, flip_ref, own_out, edge_out, table_out
):
    mean_inv = 24.0 * LOG2E
    for n in range(STEPS):
        block = jnp.concatenate([own_ref[0, n], own_ref[0, n + 1]], axis=1)
        final = n + 1 == STEPS
        up = jnp.concatenate([up_ref[0, n], up_last_ref[0] if final else up_ref[0, n + 1]], axis=1)
        down = jnp.concatenate(
            [down_ref[0, n], down_last_ref[0] if final else down_ref[0, n + 1]], axis=1
        )
        own_out[0, n] = dot_nt(rev_ref[...], block).astype(BF)
        edge_out[0, n] = dot_nt(rev_ref[...], jnp.concatenate([up, down], axis=0)).astype(BF)
        stats = jnp.concatenate([stat_ref[0, n], stat_ref[0, n + 1]], axis=1)
        mean, inv = boxed_stats(stats, up, down)
        scaled = inv * mean_inv
        both = jnp.concatenate([scaled * (1.0 / 576.0), scaled * mean], axis=0)[:, :128]
        high = both.astype(BF).astype(F32)
        mid = (both - high).astype(BF).astype(F32)
        index = index_ref[0, :, 128 * n : 128 * n + 128].astype(F32)
        rows = jnp.concatenate(
            [high, mid, both - high - mid, index, jnp.zeros((4, 128), F32)], axis=0
        ).astype(BF)
        blank = jnp.zeros((64, 64), F32)
        left = dot_nt(flip_ref[0:64, :], rows)
        right = dot_nt(flip_ref[64:128, :], rows)
        table_out[0, n] = jnp.concatenate([left, right, blank], axis=1).astype(BF)


def prepare(own, up, up_last, down, down_last, stats, depth_index):
    images, blocks = own.shape[0], own.shape[1]
    return pl.pallas_call(
        prepare_kernel,
        grid=(images,),
        in_specs=[
            pl.BlockSpec((1, blocks, 256, 128), lambda k: (k, 0, 0, 0)),
            pl.BlockSpec((1, STEPS, 64, 128), lambda k: (k, 0, 0, 0)),
            pl.BlockSpec((1, 64, 128), lambda k: (k, 0, 0)),
            pl.BlockSpec((1, STEPS, 64, 128), lambda k: (k, 0, 0, 0)),
            pl.BlockSpec((1, 64, 128), lambda k: (k, 0, 0)),
            pl.BlockSpec((1, blocks, 8, 128), lambda k: (k, 0, 0, 0)),
            pl.BlockSpec((1, 4, 512), lambda k: (k, 0, 0)),
            pl.BlockSpec((WIN, 256), lambda k: (0, 0)),
            pl.BlockSpec((128, 128), lambda k: (0, 0)),
        ],
        out_specs=[
            pl.BlockSpec((1, STEPS, WIN, 256), lambda k: (k, 0, 0, 0)),
            pl.BlockSpec((1, STEPS, WIN, 128), lambda k: (k, 0, 0, 0)),
            pl.BlockSpec((1, STEPS, 64, 128), lambda k: (k, 0, 0, 0)),
        ],
        out_shape=[
            jax.ShapeDtypeStruct((images, STEPS, WIN, 256), BF),
            jax.ShapeDtypeStruct((images, STEPS, WIN, 128), BF),
            jax.ShapeDtypeStruct((images, STEPS, 64, 128), BF),
        ],
        cost_estimate=pl.CostEstimate(
            flops=images * STEPS * 40_000_000, bytes_accessed=images * 1_000_000, transcendentals=0
        ),
        compiler_params=PARAMS,
        name="prepare",
    )(own, up, up_last, down, down_last, stats, depth_index, reversal(), flips())


def skewed(left, right, column, lane, shift):
    return pltpu.roll(jnp.where(lane < column, right, left), shift, 1, stride=1, stride_axis=0)


def sweep_kernel(group, ys, halo, late, *refs):
    refs = list(refs[1:])

    def take(count):
        out = refs[:count]
        del refs[:count]
        return out

    count = len(ys)
    block_refs = take(3) if late else (take(group), take(group))
    own_ref, table_ref, pat_ref, mask_ref, w2_ref, flip_ref, elev_ref, cell_ref = take(8)

    def joined(three, g):
        if late:
            early, before, after = three
            near = jnp.where(pl.program_id(0) == 0, early[g, 0], before[g, 0])
        else:
            near, after = three[0][g, 0], three[1]
        return jnp.concatenate([near, after[g, 0]], axis=1)

    width = 3 if late else 2
    stat_refs = take(width)
    up_refs = take(width) if halo else None
    down_refs = take(width) if halo else None
    edge_ref = take(1)[0] if halo else None
    mean_ref, rows_ref, skew = refs

    column = 63 - lax.broadcasted_iota(jnp.int32, (64, 128), 0)
    lane = lax.broadcasted_iota(jnp.int32, (64, 128), 1)
    wrapped = lane < column
    first = lane < column + 64
    column8 = 7 - lax.broadcasted_iota(jnp.int32, (8, 128), 0)
    lane8 = lax.broadcasted_iota(jnp.int32, (8, 128), 1)
    hyp = (lane % 64).astype(F32)
    tables = dot(table_ref[:, 0].reshape(group * 64, 128), pat_ref[...])

    soft = []
    chosen = []
    for g in range(group):
        if late:
            rhs = joined(block_refs, g)
        else:
            rhs = jnp.concatenate([block_refs[0][g][0, 0], block_refs[1][g][0, 0]], axis=1)
        stats = joined(stat_refs, g)
        if halo:
            up = joined(up_refs, g)
            down = joined(down_refs, g)
            rhs = jnp.concatenate([rhs, up, down], axis=0)
            sides = edge_ref[g, 0]
        else:
            up = down = None
        mean_b, inv_b = boxed_stats(stats, up, down)
        own = own_ref[g, 0]
        masked = jnp.concatenate([own * mask_ref[y : y + 1, :] for y in ys], axis=0)
        if halo:
            sides = jnp.concatenate([sides * mask_ref[8 + y : 9 + y, 0:128] for y in ys], axis=0)
            masked = jnp.concatenate([masked, sides], axis=1)
        product = dot(masked, rhs)
        for i, y in enumerate(ys):
            p = product[WIN * i : WIN * i + WIN]
            z = jnp.where(
                wrapped, p[16:80, 128:], jnp.where(first, p[80:144, :128], p[16:80, :128])
            )
            z8 = jnp.where(
                lane8 < column8,
                p[72:80, 128:],
                jnp.where(lane8 < column8 + 64, p[8:16, 128:], p[72:80, :128]),
            )
            at = count * g + i
            skew[at, 0:8, :] = pltpu.roll(z8, 57, 1, stride=1, stride_axis=0)
            skew[at, 8:72, :] = pltpu.roll(z, 65, 1, stride=1, stride_axis=0)
            cross = skew[at, 8:72, :] + skew[at, 7:71, :] + skew[at, 6:70, :]
            mb = skewed(mean_b[y : y + 1, :128], mean_b[y : y + 1, 128:], column, lane, 65)
            rb = skewed(inv_b[y : y + 1, :128], inv_b[y : y + 1, 128:], column, lane, 65)
            a1, a2, index = (
                tables[64 * g : 64 * g + 64, (3 * i + q) * 128 : (3 * i + q + 1) * 128]
                for q in range(3)
            )
            weight = jnp.exp2((cross * a1 - a2 * mb) * rb)
            picked = jnp.where(index == hyp, weight, 0.0)
            soft.append(jnp.concatenate(split2(weight), axis=1))
            chosen.append(jnp.concatenate(split2(picked), axis=1))
    soft = jnp.concatenate(soft, axis=0)
    chosen = jnp.concatenate(chosen, axis=0)
    r = dot_nt(w2_ref[...], soft)
    rc = dot_nt(w2_ref[...], chosen)
    inv = 1.0 / r[0:2]
    both = jnp.concatenate([(r[2:4] + r[4:6] + r[6:8]) * inv, rc[0:2] * inv], axis=0)
    pieces = group * count // 2
    both = jnp.concatenate([both[:, 128 * v : 128 * v + 128] for v in range(pieces)], axis=0)
    high = both.astype(BF)
    rest = both - high.astype(F32)
    mid = rest.astype(BF)
    low = (rest - mid.astype(F32)).astype(BF)
    both = dot(jnp.concatenate([high, mid, low], axis=0), flip_ref[...])
    both = both[0 : 4 * pieces] + both[4 * pieces : 8 * pieces] + both[8 * pieces :]
    turned = pltpu.roll(both, 64, 1)
    left = lax.broadcasted_iota(jnp.int32, (1, 128), 1) < 64
    cell_iota = lax.broadcasted_iota(jnp.int32, (128, 128), 0)
    blank = jnp.zeros((4, 128), F32)
    for g in range(group):
        for i in range(0, count, 2):
            lines = []
            hots = []
            for j, y in enumerate(ys[i : i + 2]):
                at = (count * g + i) // 2 * 4
                lo, hi = (both, turned) if j == 0 else (turned, both)
                mean = jnp.where(left, lo[at : at + 1], hi[at + 1 : at + 2])
                mean_ref[g, i + j : i + j + 1, :] = mean
                c = jnp.where(left, lo[at + 2 : at + 3], hi[at + 3 : at + 4])
                values = jnp.concatenate([c * elev_ref[g, y : y + 1, :], c], axis=0)
                value_hi = values.astype(BF).astype(F32)
                line = jnp.concatenate([value_hi, values - value_hi], axis=0)
                lines.append(jnp.concatenate([line, blank] if j == 0 else [blank, line], axis=1))
                hot = jnp.where(cell_iota == cell_ref[g, y : y + 1, :], 1.0, 0.0)
                hots.append(hot.astype(BF))
            binned = dot_nt(
                jnp.concatenate(lines, axis=0).astype(BF), jnp.concatenate(hots, axis=1)
            )
            for j in range(2):
                got = binned[4 * j : 4 * j + 2] + binned[4 * j + 2 : 4 * j + 4]
                at = count * g + i + j
                rows_ref[0, at : at + 1, 0:128] = got[0:1]
                rows_ref[0, at : at + 1, 128:256] = got[1:2]


def sweep_steps(
    first, steps, ys, group, slot, blocks, stats, ups, downs, own, edge, table, w2, elev, cell, late
):
    images = own.shape[0]
    halo = ups is not None
    count = len(ys)

    def slot_block(g, j):
        return lambda n, k, s: (s[group * k + g], n + first + j, 0, 0)

    def near(n, k, s):
        return (k, n + first, 0, 0)

    def whole(n, k, s):
        return (0, 0)

    def pixels(n, k, s):
        return (k, 0, n + first)

    def pair_specs(rows, kept=FIRST - 1):
        if late:
            maps = (
                lambda n, k, s: (k, kept, 0, 0),
                lambda n, k, s: (k, 0, 0, 0),
                lambda n, k, s: (k, n, 0, 0),
            )
        else:
            maps = (near, lambda n, k, s: (k, n + first + 1, 0, 0))
        return [pl.BlockSpec((group, 1, rows, 128), m) for m in maps]

    def pair_args(arrays):
        return [arrays[0], arrays[1], arrays[1]] if late else [arrays[0], arrays[0]]

    if late:
        in_specs = pair_specs(256, 0)
        args = pair_args(blocks)
    else:
        in_specs = [
            pl.BlockSpec((1, 1, 256, 128), slot_block(g, j)) for j in range(2) for g in range(group)
        ]
        args = [blocks] * (2 * group)
    in_specs += [
        pl.BlockSpec((group, 1, WIN, 256), near),
        pl.BlockSpec((group, 1, 64, 128), near),
        pl.BlockSpec((128, 3 * 128 * count), whole),
        pl.BlockSpec((16, 256), whole),
        pl.BlockSpec((8, 256), whole),
        pl.BlockSpec((128, 128), whole),
        pl.BlockSpec((group, 4, 128), pixels),
        pl.BlockSpec((group, 4, 128), pixels),
    ] + pair_specs(8)
    args += [
        own, table, table_patterns(ys), row_masks(), w2, flips(), elev, cell,
    ] + pair_args(stats)
    if halo:
        in_specs += pair_specs(64) + pair_specs(64) + [pl.BlockSpec((group, 1, WIN, 128), near)]
        args += pair_args(ups) + pair_args(downs) + [edge]
    work = steps * images * count // 4
    return pl.pallas_call(
        functools.partial(sweep_kernel, group, ys, halo, late),
        grid_spec=pltpu.PrefetchScalarGridSpec(
            num_scalar_prefetch=1,
            grid=(steps, images // group),
            in_specs=in_specs,
            out_specs=[
                pl.BlockSpec((group, count, 128), lambda n, k, s: (k, 0, n)),
                pl.BlockSpec((1, count * group, 256), lambda n, k, s: (n, k, 0)),
            ],
            scratch_shapes=[pltpu.VMEM((count * group, 72, 128), F32)],
        ),
        out_shape=[
            jax.ShapeDtypeStruct((images, count, steps * 128), F32),
            jax.ShapeDtypeStruct((steps, images * count, 256), F32),
        ],
        compiler_params=LATE if late or halo else PARAMS,
        cost_estimate=pl.CostEstimate(
            flops=work * 200_000_000, bytes_accessed=work * 400_000, transcendentals=0
        ),
        name="sweep",
    )(slot, *args)


def depth_weights(planes):
    high = lax.reduce_precision(planes, 8, 7)
    mid = lax.reduce_precision(planes - high, 8, 7)
    zero = jnp.zeros_like(planes)
    rows = []
    for v in (jnp.ones_like(planes), high, mid, planes - high - mid):
        rows.append(jnp.concatenate([v, zero]))
        rows.append(jnp.concatenate([zero, v]))
    w = jnp.stack(rows)
    return jnp.concatenate([w, w], axis=1).astype(BF)


def collect_kernel(list_ref, count_ref, a_ref, b_ref, c_ref, d_ref, out_ref, rows):
    at = 0
    for part in (a_ref, b_ref, c_ref, d_ref):
        for n in range(part.shape[0]):
            rows[at : at + part.shape[1], :] = part[n]
            at += part.shape[1]
    for o in range(out_ref.shape[0]):

        def move(step, carry):
            for i in range(8):
                e = step * 8 + i
                out_ref[o, pl.ds(e, 1), :] = rows[pl.ds(list_ref[o, e], 1), :]
            return carry

        lax.fori_loop(0, (count_ref[o] + 7) // 8, move, 0)


def collect(row_list, counts, parts):
    owners, cap = row_list.shape
    total = sum(p.shape[0] * p.shape[1] for p in parts)
    return pl.pallas_call(
        collect_kernel,
        grid_spec=pltpu.PrefetchScalarGridSpec(
            num_scalar_prefetch=2,
            grid=(1,),
            in_specs=[pl.BlockSpec(p.shape, lambda i, a, b: (0, 0, 0)) for p in parts],
            out_specs=pl.BlockSpec((owners, cap, 2 * CELLS), lambda i, a, b: (0, 0, 0)),
            scratch_shapes=[pltpu.VMEM((total, 2 * CELLS), F32)],
        ),
        out_shape=jax.ShapeDtypeStruct((owners, cap, 2 * CELLS), F32),
        compiler_params=SMALL,
        name="collect",
    )(row_list, counts, *parts)


def place_kernel(slot_ref, count_ref, got_ref, out_ref):
    out_ref[...] = jnp.zeros_like(out_ref)
    for t in range(got_ref.shape[0]):
        count = count_ref[t]

        def add(step, carry):
            for i in range(8):
                e = step * 8 + i
                at = pl.ds(slot_ref[t, e], 1)
                row = jnp.where(e < count, got_ref[t, pl.ds(e, 1), :], 0.0)
                out_ref[at, :] = out_ref[at, :] + row
            return carry

        lax.fori_loop(0, (count + 7) // 8, add, 0)


def place(slots, counts, got, total):
    return pl.pallas_call(
        place_kernel,
        grid_spec=pltpu.PrefetchScalarGridSpec(
            num_scalar_prefetch=2,
            grid=(1,),
            in_specs=[pl.BlockSpec(got.shape, lambda i, a, b: (0, 0, 0))],
            out_specs=pl.BlockSpec((total, 2 * CELLS), lambda i, a, b: (0, 0)),
        ),
        out_shape=jax.ShapeDtypeStruct((total, 2 * CELLS), F32),
        compiler_params=SMALL,
        name="place",
    )(slots, counts, got)


def neighbour_rows(head, tail):
    count = lax.axis_size("tile")
    above = lax.ppermute(tail, "tile", [(i, i + 1) for i in range(count - 1)])
    below = lax.ppermute(head, "tile", [(i + 1, i) for i in range(count - 1)])
    return above, below


def on_device(
    features, partner_ids, depth_planes, cam_height, ray_down, depth_index, cell_index,
    block_list, block_slot, block_count,
):
    group_count = lax.axis_size("img")
    owners = lax.axis_size("tile")
    my_group = lax.axis_index("img")
    my_tile = lax.axis_index("tile")
    images = features.shape[0]
    table = partner_ids.reshape(group_count, images)
    source_of = table // images
    chosen = jnp.sum(jnp.where(source_of == my_group, table % images, 0), axis=1)
    slot = lax.dynamic_index_in_dim(source_of, my_group, 0, False)

    def exchange(a):
        return lax.all_to_all(a, "img", split_axis=0, concat_axis=0, tiled=True)

    main = exchange(pick(chosen, features, FIRST))

    every = jnp.arange(images, dtype=jnp.int32)
    own = pick(every, features, STEPS + 1)
    own_head, own_tail, own_stats = edges(every, own, False)
    own_up, own_down = neighbour_rows(own_head[:, :STEPS], own_tail[:, :STEPS])
    ends = [jnp.transpose(v[:, STEPS, :, :2], (0, 2, 1)).reshape(images, -1) for v in (own_head, own_tail)]
    ends = [v.reshape(images, 2, -1) for v in neighbour_rows(*ends)]
    up_last, down_last = (
        jnp.pad(jnp.transpose(v, (0, 2, 1)), ((0, 0), (0, 0), (0, 126))) for v in ends
    )
    own_turned, edge_turned, own_table = prepare(
        own, own_up, up_last, own_down, down_last, own_stats, depth_index
    )
    packed = pack(chosen, own)

    hyp = jnp.arange(NDEPTH, dtype=jnp.int32)[:, None, None, None]
    plane_at = jnp.sum(
        jnp.where(hyp == depth_index[None], depth_planes[:, None, None, None], 0.0), 0
    )
    elevation = cam_height[:, None, None] - ray_down * plane_at

    meta = jnp.concatenate(
        [block_slot[0, 0], jnp.broadcast_to(block_count[0, 0][:, None], (owners, 128))], axis=1
    )
    metas = [lax.dynamic_slice_in_dim(meta, my_tile, 1, 0)]
    for s in range(1, owners):
        mine = lax.dynamic_slice_in_dim(meta, (my_tile + s) % owners, 1, 0)
        metas.append(lax.ppermute(mine, "tile", [(i, (i + s) % owners) for i in range(owners)]))
    metas = jnp.concatenate(metas, axis=0)
    metas = jnp.take(metas, (my_tile - jnp.arange(owners)) % owners, axis=0)

    w2 = depth_weights(depth_planes)

    packed, own_turned, edge_turned, own_table, elevation, metas, w2 = lax.optimization_barrier(
        (packed, own_turned, edge_turned, own_table, elevation, metas, w2)
    )
    last = exchange(packed)
    head, tail, stats, early = edges(slot, main, True)
    up, down = neighbour_rows(head, tail)
    shared = (own_turned, edge_turned, own_table, w2, elevation, cell_index)
    shared = (own_turned, edge_turned, own_table, w2, elevation, cell_index)
    inner, outer = (1, 2), (0, 3)
    one = (stats,)
    mean_i, rows_i = sweep_steps(0, 2, inner, 16, slot, main, one, None, None, *shared, False)
    up, down, mean_i = lax.optimization_barrier((up, down, mean_i))
    mean_o, rows_o = sweep_steps(0, 2, outer, 16, slot, main, one, (up,), (down,), *shared, False)
    last, mean_o = lax.optimization_barrier((last, mean_o))
    head_l, tail_l, stats_l, late = unpack(slot, last)
    up_l, down_l = neighbour_rows(head_l, tail_l)
    blocks, both = (early, late), (stats, stats_l)
    mean_il, rows_il = sweep_steps(2, 2, inner, 16, slot, blocks, both, None, None, *shared, True)
    mean_ol, rows_ol = sweep_steps(
        2, 2, outer, 16, slot, blocks, both, (up, up_l), (down, down_l), *shared, True
    )
    mean_i = jnp.concatenate([mean_i, mean_il], axis=2)
    mean_o = jnp.concatenate([mean_o, mean_ol], axis=2)
    mean_range = jnp.concatenate([mean_o[:, 0:1], mean_i, mean_o[:, 1:2]], axis=1)

    lists = block_list[0, 0]
    n, r, k = lists % STEPS, lists // STEPS % 4, lists // (4 * STEPS)
    inside = (r == 1) | (r == 2)
    row_list = 2 * images * n + 2 * k + jnp.where(inside, r - 1, 8 * images + r // 3)
    send = collect(row_list, block_count[0, 0], (rows_i, rows_il, rows_o, rows_ol))
    got = lax.all_to_all(send, "tile", split_axis=0, concat_axis=0, tiled=True)
    dense = place(metas[:, :128], metas[:, 128], got, group_count * PATCH_DEV)
    parts = exchange(dense.reshape(group_count, PATCH_DEV, 2 * CELLS))
    total = jnp.sum(parts, axis=0)
    return mean_range, total[:, :CELLS] / (total[:, CELLS:] + 1.0)


def solution(mesh):
    return jax.shard_map(
        on_device,
        mesh=mesh,
        in_specs=(
            P("img", None, "tile", None),
            P(),
            P(),
            P("img"),
            P("img", "tile", None),
            P("img", "tile", None),
            P("img", "tile", None),
            P("img", "tile", None, None),
            P("img", "tile", None, None),
            P("img", "tile", None),
        ),
        out_specs=(P("img", "tile", None), P(("img", "tile"), None)),
        check_vma=False,
    )
```
